32 devices in a mesh: dp: 2 (over core), row: 4 (over y, x), col: 4 (over z).
Axes of the slice: x: 2, y: 2, z: 4, core: 2. Of those that a mesh axis runs over, the one named last changes fastest.
Arguments:
- states: float32 [5120, 1024], P(('dp', 'row'), 'col'), may hold values from -6 to 6
- teacher: bfloat16 [5120, 1024], P(('dp', 'row'), 'col'), may hold values from -6 to 6
- cotangent: float32 [5120, 1024], P(('dp', 'row'), 'col'), may hold values from -6 to 6
- lengths: int32 [16], P(('dp', 'row')), may hold values from 256 to 320
- norm_gain: float32 [2, 2, 1024], P(None, None, 'col'), may hold values from 0.5 to 1.5
- norm_bias: float32 [2, 2, 1024], P(None, None, 'col'), may hold values from -2 to 2
- in_weight: bfloat16 [2, 1024, 3, 1024], P(None, 'row', None, 'col'), may hold values from -0.1875 to 0.1875
- in_bias: float32 [2, 2, 1024], P(None, None, 'col'), may hold values from -2 to 2
- proj_weight: bfloat16 [2, 1024, 1024], P(None, 'col', 'row'), may hold values from -0.75 to 0.75
- proj_bias: float32 [2, 1024], P(None, 'col'), may hold values from -2 to 2
- up_weight: bfloat16 [2, 1024, 4096], P(None, 'row', 'col'), may hold values from -0.1875 to 0.1875
- up_bias: float32 [2, 4096], P(None, 'col'), may hold values from -2 to 2
- down_weight: bfloat16 [2, 4096, 1024], P(None, 'col', 'row'), may hold values from -0.125 to 0.125
- down_bias: float32 [2, 1024], P(None, 'col'), may hold values from -2 to 2
Outputs:
- loss_value: float32 [], replicated
- output: float32 [5120, 1024], P(('dp', 'row'), 'col')
- input_grad: float32 [5120, 1024], P(('dp', 'row'), 'col')
- norm_gain_grad: float32 [2, 2, 1024], P(None, None, 'col')
- norm_bias_grad: float32 [2, 2, 1024], P(None, None, 'col')
- in_weight_grad: float32 [2, 1024, 3, 1024], P(None, 'row', None, 'col')
- in_bias_grad: float32 [2, 2, 1024], P(None, None, 'col')
- proj_weight_grad: float32 [2, 1024, 1024], P(None, 'col', 'row')
- proj_bias_grad: float32 [2, 1024], P(None, 'col')
- up_weight_grad: float32 [2, 1024, 4096], P(None, 'row', 'col')
- up_bias_grad: float32 [2, 4096], P(None, 'col')
- down_weight_grad: float32 [2, 4096, 1024], P(None, 'col', 'row')
- down_bias_grad: float32 [2, 1024], P(None, 'col')
The draws below stay inside these ranges and needn't reach their ends.
Inputs may be any that keep to these rules, and one draw needn't show every extreme that they name: `lengths`: number of valid slots of a sequence; slots from that number on are padding.
All inputs are finite; a program needn't handle non-finite values.
Results may differ from the reference program's by a relative error of at most 0.013.
Values may be sent and summed in bfloat16 or wider, within the bound.
No kernel may reach another device: no remote copies, remote signals or barrier semaphores. Data moves between devices by JAX's collectives and lax.ppermute only.
A program may use at most 192 MiB of HBM per device.

```python
import jax
import jax.numpy as jnp
from jax import lax

D = 1024
FF = 4096
HEADS = 16
HEAD_DIM = 64
SLOTS = 320
BUFFER = 64
LAYERS = 2
SEQS = 16
TOKENS = 5120


def set_ends(array, rng, smallest, high):
    index_at = [jax.random.randint(jax.random.fold_in(rng, axis), (), 0, length) for axis, length in enumerate(array.shape)]
    main_axis = array.shape.index(max(array.shape))
    next_to = index_at[:main_axis] + [(index_at[main_axis] + 1) % array.shape[main_axis]] + index_at[main_axis + 1:]
    return array.at[tuple(index_at)].set(smallest).at[tuple(next_to)].set(high)


def block_scale(stream_key, dims, cuts, smallest, high):
    def one(axis_at, blocks):
        draws = jax.random.uniform(jax.random.fold_in(jax.random.fold_in(stream_key, 6), axis_at), (blocks,), jnp.float32, smallest / len(cuts), high / len(cuts))
        return jnp.repeat(jnp.exp(draws), dims[axis_at] // blocks).reshape((-1,) + (1,) * (len(dims) - axis_at - 1))

    level = one(*cuts[0])
    for cut in cuts[1:]:
        level = level * one(*cut)
    return level


def centred(stream_key, extent, width, limit, split=(), kind=jnp.bfloat16):
    drawn = jax.random.normal(stream_key, extent, jnp.float32) * width
    if len(split) > 0:
        drawn = block_scale(stream_key, extent, split, -0.22, 0.18) * drawn
    return jnp.clip(drawn, min=-limit, max=limit).astype(kind)


def setup_inputs(seed: int = 0) -> dict:
    key_of = jax.random.split(jax.random.key(seed), 15)
    states = centred(key_of[0], (TOKENS, D), 1.0, 6.0, ((0, 8), (1, 4)), jnp.float32)
    teacher = centred(key_of[1], (TOKENS, D), 1.0, 6.0, ((0, 8), (1, 4)))
    cotangent = centred(key_of[2], (TOKENS, D), 1.0, 6.0, ((0, 8), (1, 4)), jnp.float32)
    lengths = set_ends(jax.random.randint(key_of[3], (SEQS,), SLOTS - BUFFER, SLOTS + 1), jax.random.fold_in(key_of[3], 1), SLOTS - BUFFER, SLOTS).astype(jnp.int32)
    norm_gain = jnp.clip(1.0 + 0.1 * jax.random.normal(key_of[4], (LAYERS, 2, D), jnp.float32), 0.5, 1.5)
    norm_bias = centred(key_of[5], (LAYERS, 2, D), 0.3, 2.0, ((2, 4),), jnp.float32)
    in_weight = centred(key_of[6], (LAYERS, D, 3, D), D ** -0.5, 0.1875, ((1, 4), (3, 4)))
    in_bias = centred(key_of[7], (LAYERS, 2, D), 0.3, 2.0, ((2, 4),), jnp.float32)
    proj_weight = centred(key_of[8], (LAYERS, D, D), (D // 16) ** -0.5, 0.75, ((1, 4), (2, 4)))
    proj_bias = centred(key_of[9], (LAYERS, D), 0.3, 2.0, ((1, 4),), jnp.float32)
    up_weight = centred(key_of[10], (LAYERS, D, FF), D ** -0.5, 0.1875, ((1, 4), (2, 4)))
    up_bias = centred(key_of[11], (LAYERS, FF), 0.3, 2.0, ((1, 4),), jnp.float32)
    down_weight = centred(key_of[12], (LAYERS, FF, D), (FF // 2) ** -0.5, 0.125, ((1, 4), (2, 4)))
    down_bias = centred(key_of[13], (LAYERS, D), 0.3, 2.0, ((1, 4),), jnp.float32)
    return {"states": states, "teacher": teacher, "cotangent": cotangent, "lengths": lengths, "norm_gain": norm_gain, "norm_bias": norm_bias, "in_weight": in_weight, "in_bias": in_bias, "proj_weight": proj_weight, "proj_bias": proj_bias, "up_weight": up_weight, "up_bias": up_bias, "down_weight": down_weight, "down_bias": down_bias}


epsilon = 1e-06
fill_value = -1e+30
highest = lax.Precision.HIGHEST

@jax.custom_vjp
def low(v):
    return lax.optimization_barrier(v.astype(jnp.bfloat16)).astype(jnp.float32)

@jax.custom_vjp
def low_back(v):
    return v

def low_keep(v):
    return (low(v), None)

def low_pass(kept, grad):
    return (grad,)

def back_keep(v):
    return (v, None)

def back_low(kept, grad):
    return (low(grad),)
low.defvjp(low_keep, low_pass)
low_back.defvjp(back_keep, back_low)

def layer_norm(inputs, gains, shifts):
    centre = lax.optimization_barrier(jnp.mean(inputs, axis=-1, keepdims=True))
    centered = inputs - centre
    spread = lax.optimization_barrier(jnp.mean(centered * centered, axis=-1, keepdims=True))
    return centered * lax.rsqrt(spread + epsilon) * gains + shifts

def block_forward(inputs, validity, layer_params):
    gains, shifts, w_in, b_in, w_proj, b_proj, w_up, b_up, w_down, b_down = layer_params
    tokens = inputs.shape[0]
    group_count = validity.shape[0]
    score_scale = HEAD_DIM ** (-0.5)
    shape_four = (group_count, SLOTS, HEADS, HEAD_DIM)
    normed_one = low(layer_norm(inputs, gains[0], shifts[0]))
    projected = jnp.einsum('td,dpe->tpe', normed_one, w_in, precision=highest)
    queries = low(low_back(projected[:, 0] + b_in[0]))
    key_block = low(low_back(projected[:, 1]))
    values = low(low_back(projected[:, 2] + b_in[1]))
    scores = jnp.einsum('sqhe,skhe->shqk', queries.reshape(shape_four), key_block.reshape(shape_four), precision=highest) * score_scale
    scores = low_back(jnp.where(validity[:, None, None, :], scores, fill_value))
    maximum = lax.optimization_barrier(jnp.max(scores, axis=-1, keepdims=True))
    exponent = jnp.exp(scores - maximum)
    attention = exponent / lax.optimization_barrier(jnp.sum(exponent, axis=-1, keepdims=True))
    mixture = jnp.einsum('shqk,skhe->sqhe', low(attention), values.reshape(shape_four), precision=highest)
    attended = low(low_back(mixture.reshape(tokens, HEADS * HEAD_DIM)))
    middle = inputs + low_back(jnp.dot(attended, w_proj, precision=highest) + b_proj)
    normed_two = low(layer_norm(middle, gains[1], shifts[1]))
    hidden_pre = low_back(jnp.dot(normed_two, w_up, precision=highest) + b_up)
    hidden = low(jax.nn.gelu(hidden_pre, approximate=False))
    branch = low_back(jnp.dot(hidden, w_down, precision=highest) + b_down)
    return (middle + branch) * validity.reshape(tokens, 1).astype(inputs.dtype)

def reference(states, teacher, cotangent, lengths, norm_gain, norm_bias, in_weight, in_bias, proj_weight, proj_bias, up_weight, up_bias, down_weight, down_bias):
    positions = jnp.arange(SLOTS, dtype=jnp.int32)
    validity = positions[None, :] < lengths[:, None]
    token_total = jnp.sum(validity.astype(jnp.float32))
    params = tuple((source.astype(jnp.float32) for source in (norm_gain, norm_bias, in_weight, in_bias, proj_weight, proj_bias, up_weight, up_bias, down_weight, down_bias)))
    group_count = 8
    block_count = SEQS // group_count
    group_rows = group_count * SLOTS
    inputs_all = states.astype(jnp.float32).reshape(block_count, group_rows, D)
    targets_all = teacher.astype(jnp.float32).reshape(block_count, group_rows, D)
    seeds_all = cotangent.astype(jnp.float32).reshape(block_count, group_rows, D)
    validity_all = validity.reshape(block_count, group_count, SLOTS)
    objective_weight = TOKENS / token_total

    def forward(layer_stack, input_rows, validity_block, targets):
        current = input_rows
        for layer_index in range(LAYERS):
            current = block_forward(current, validity_block, tuple((piece[layer_index] for piece in layer_stack)))
        residue = current - targets
        squared = jnp.sum(residue * residue * validity_block.reshape(-1, 1).astype(jnp.float32))
        return (current, squared)

    def group_step(running, pieces):
        input_rows, targets, seeds, validity_block = pieces
        outputs, pullback = jax.vjp(lambda layer_stack, rows_in: forward(layer_stack, rows_in, validity_block, targets), params, input_rows)
        grads_params, grads_inputs = pullback((seeds, objective_weight))
        summed = jax.tree.map(jnp.add, running[0], grads_params)
        return ((summed, running[1] + outputs[1]), (outputs[0], grads_inputs))
    zeros_start = jax.tree.map(jnp.zeros_like, params)
    finals, stacked = lax.scan(group_step, (zeros_start, jnp.zeros((), jnp.float32)), (inputs_all, targets_all, seeds_all, validity_all))
    grads_total, squared_total = finals
    output_rows, input_rows = stacked
    loss_value = squared_total / (token_total * D)
    return (loss_value, output_rows.reshape(TOKENS, D), input_rows.reshape(TOKENS, D), grads_total[0], grads_total[1], grads_total[2], grads_total[3], grads_total[4], grads_total[5], grads_total[6], grads_total[7], grads_total[8], grads_total[9])
```

```python
import jax
import jax.numpy as jnp
from jax import lax
from jax.sharding import PartitionSpec as P

HEAD_DIM = 64
LAYERS = 2

epsilon = 1e-06
fill_value = -1e30
low_type = jnp.bfloat16


def gelu_exact(inputs):
    return jax.nn.gelu(inputs, approximate=False)


def flip_col(value):
    count = lax.axis_size("col")
    return lax.ppermute(value, "col", [(i, count - 1 - i) for i in range(count)])


def swap_core(value):
    count = lax.axis_size("dp")
    return lax.ppermute(value, "dp", [(i, count - 1 - i) for i in range(count)])


def group_shift(value, step):
    count = lax.axis_size("col")
    half = count // 2
    pairs = [(i, i // half * half + (i % half + step) % half) for i in range(count)]
    return lax.ppermute(value, "col", pairs)


def group_sum(partial_value):
    low = partial_value.astype(low_type)
    total = partial_value
    for step in range(1, lax.axis_size("col") // 2):
        total = total + group_shift(low, step).astype(jnp.float32)
    return total


def butterfly_sum(value, axes):
    for axis in axes:
        count = lax.axis_size(axis)
        step = 1
        while step < count:
            value = value + lax.ppermute(value, axis, [(i, i ^ step) for i in range(count)])
            step *= 2
    return value


def gather_row_direct(shard):
    count = lax.axis_size("row")
    if count > 4:
        return lax.all_gather(shard, "row", axis=0, tiled=False)
    mine = lax.axis_index("row")
    whole = jnp.zeros((count,) + shard.shape, shard.dtype)
    whole = lax.dynamic_update_index_in_dim(whole, shard, mine, 0)
    for step in range(1, count):
        piece = lax.ppermute(shard, "row", [(i, i ^ step) for i in range(count)])
        whole = lax.dynamic_update_index_in_dim(whole, piece, mine ^ step, 0)
    return whole


def gather_row(shard):
    return lax.all_gather(shard, "row", axis=0, tiled=False)


def scatter_row(blocks):
    return lax.psum_scatter(blocks, "row", scatter_dimension=0, tiled=False)


def place_blocks(pair, mine_first):
    count = lax.axis_size("col")
    half = count // 2
    col_index = lax.axis_index("col")
    base = col_index // half * half
    whole = jnp.zeros((count,) + pair.shape[1:], pair.dtype)
    for step in range(half):
        piece = pair if step == 0 else group_shift(pair, step)
        source = base + (col_index - base + half - step) % half
        whole = lax.dynamic_update_index_in_dim(whole, piece[0], source, 0)
        whole = lax.dynamic_update_index_in_dim(whole, piece[1], count - 1 - source, 0)
    return whole


def norm_rows(inputs, gains, shifts, model_width):
    centre = jnp.sum(inputs, axis=1, keepdims=True) / model_width
    centred = inputs - centre
    spread = jnp.sum(centred * centred, axis=1, keepdims=True) / model_width
    rscale = lax.rsqrt(spread + epsilon)
    standard = centred * rscale
    return ((standard * gains + shifts).astype(low_type), standard, rscale)


def norm_backward(grad_rows, standard, rscale, gains, model_width):
    scaled = grad_rows * gains
    first = jnp.sum(scaled, axis=1, keepdims=True) / model_width
    second = jnp.sum(scaled * standard, axis=1, keepdims=True) / model_width
    grad_input = rscale * (scaled - first - standard * second)
    return (grad_input, jnp.sum(grad_rows * standard, axis=0), jnp.sum(grad_rows, axis=0))


def dot(left, right, spec):
    return jnp.einsum(spec, left, right, preferred_element_type=jnp.float32)


def split_heads(flat_rows, seqs):
    return flat_rows.reshape(
        seqs, flat_rows.shape[0] // seqs, flat_rows.shape[1] // HEAD_DIM, HEAD_DIM
    )


def attention_scores(queries, key_block, validity, score_scale):
    scores = dot(queries, key_block, "sqhe,skhe->shqk") * score_scale
    return jnp.where(validity[:, None, None, :], scores, fill_value)


def attend(queries, key_block, values, validity, score_scale):
    scores = attention_scores(queries, key_block, validity, score_scale)
    maximum = jnp.max(scores, axis=-1, keepdims=True)
    exponent = jnp.exp(scores - maximum)
    total_mass = jnp.sum(exponent, axis=-1, keepdims=True)
    attention = (exponent / total_mass).astype(low_type)
    mixture = dot(attention, values, "shqk,skhe->sqhe")
    return (mixture, maximum + jnp.log(total_mass))


def attend_back(queries, key_block, values, validity, score_scale, logsum, grad_mixture):
    scores = attention_scores(queries, key_block, validity, score_scale)
    chance = jnp.exp(scores - logsum)
    grad_values = dot(chance.astype(low_type), grad_mixture, "shqk,sqhe->skhe")
    grad_chance = dot(grad_mixture, values, "sqhe,skhe->shqk")
    grad_scores = (
        chance * (grad_chance - jnp.sum(grad_chance * chance, axis=-1, keepdims=True))
    ).astype(low_type)
    grad_queries = dot(grad_scores, key_block, "shqk,skhe->sqhe") * score_scale
    grad_keys = dot(grad_scores, queries, "shqk,sqhe->skhe") * score_scale
    return (grad_queries, grad_keys, grad_values)


def body(
    states,
    teacher,
    cotangent,
    lengths,
    norm_gain,
    norm_bias,
    in_weight,
    in_bias,
    proj_weight,
    proj_bias,
    up_weight,
    up_bias,
    down_weight,
    down_bias,
):
    col_count = lax.axis_size("col")
    row_count = lax.axis_size("row")
    core_count = lax.axis_size("dp")
    half_group = col_count // 2
    col_index = lax.axis_index("col")
    core_index = lax.axis_index("dp")
    group_index = col_index // half_group
    first_core = core_index == 0
    token_rows, width = states.shape
    model_width = width * col_count
    seqs = lengths.shape[0] // 2
    rows = token_rows // 2
    slot_count = rows // seqs
    hidden_width = up_bias.shape[1]
    score_scale = HEAD_DIM ** (-0.5)

    weight_pairs = [
        (d * col_count + i, d * col_count + (i if d == 0 else col_count - 1 - i))
        for d in range(core_count)
        for i in range(col_count)
    ]

    def fetch(shard, gather):
        moved = lax.ppermute(shard, ("dp", "col"), weight_pairs)
        whole = gather(moved)
        return (whole, swap_core(whole))

    in_full = [None] * LAYERS
    proj_full = [None] * LAYERS
    up_full = [None] * LAYERS
    down_full = [None] * LAYERS
    for layer in range(LAYERS):
        in_full[layer] = fetch(in_weight[layer], gather_row_direct)
        proj_full[layer] = fetch(proj_weight[layer], gather_row_direct)
        up_full[layer] = fetch(up_weight[layer], gather_row)
        down_full[layer] = fetch(down_weight[layer], gather_row)

    feature_pack = jnp.concatenate(
        [norm_gain.reshape(-1, width), norm_bias.reshape(-1, width), proj_bias, down_bias]
    )
    hidden_pack = jnp.concatenate([in_bias.reshape(-1, width), up_bias.reshape(-1, width)])
    feature_rows = feature_pack.shape[0]
    small = jnp.concatenate([feature_pack, hidden_pack])
    small_pair = jnp.stack([small, flip_col(small)])
    feature_all = place_blocks(small_pair[:, :feature_rows], True)
    feature_all = jnp.transpose(feature_all, (1, 0, 2)).reshape(feature_rows, model_width)
    gains = feature_all[: 2 * LAYERS].reshape(LAYERS, 2, model_width)
    shifts = feature_all[2 * LAYERS : 4 * LAYERS].reshape(LAYERS, 2, model_width)
    proj_shift = feature_all[4 * LAYERS : 5 * LAYERS]
    down_shift = feature_all[5 * LAYERS :]
    hidden_pair = small_pair[:, feature_rows:]
    hidden_pair = jnp.where(first_core, hidden_pair, hidden_pair[::-1])
    in_shift = hidden_pair[:, : 2 * LAYERS].reshape(2, LAYERS, 2, width)
    up_shift = hidden_pair[:, 2 * LAYERS :].reshape(2, LAYERS, hidden_width)

    def own_half(value):
        return lax.dynamic_slice_in_dim(value, group_index * rows, rows, 0)

    def other_half(value):
        return lax.dynamic_slice_in_dim(value, (1 - group_index) * rows, rows, 0)

    def whole_rows(value):
        pair = jnp.stack([own_half(value), flip_col(other_half(value))])
        blocks = place_blocks(pair, True)
        return jnp.transpose(blocks, (1, 0, 2)).reshape(rows, model_width)

    def share_rows(value):
        own = lax.dynamic_slice_in_dim(value, col_index * width, width, 1)
        other = lax.dynamic_slice_in_dim(value, (col_count - 1 - col_index) * width, width, 1)
        received = flip_col(other)
        lower = jnp.where(group_index == 0, own, received)
        upper = jnp.where(group_index == 0, received, own)
        return jnp.concatenate([lower, upper])

    current = whole_rows(states)
    token_total = butterfly_sum(jnp.sum(lengths), ("dp", "row")).astype(jnp.float32)
    factor = token_rows * core_count * row_count / token_total

    positions = jnp.arange(slot_count, dtype=jnp.int32)
    all_validity = positions[None, :] < lengths[:, None]
    all_mask = all_validity.reshape(token_rows, 1).astype(jnp.float32)
    own_lengths = lax.dynamic_slice_in_dim(lengths, group_index * seqs, seqs, 0)
    validity = positions[None, :] < own_lengths[:, None]
    row_mask = validity.reshape(rows, 1).astype(jnp.float32)

    teacher_wide = teacher.astype(jnp.float32)
    seed_share = cotangent - 2.0 * factor * all_mask * teacher_wide
    seeds = whole_rows(seed_share)

    records = []
    for layer in range(LAYERS):
        normed_one, standard_one, rscale_one = norm_rows(
            current, gains[layer, 0], shifts[layer, 0], model_width
        )
        queries, key_block, values = [], [], []
        for side in range(2):
            weight = in_full[layer][side].reshape(model_width, 3, width)
            projected = dot(normed_one, weight, "td,dpe->tpe")
            queries.append((projected[:, 0] + in_shift[side, layer, 0]).astype(low_type))
            key_block.append(projected[:, 1].astype(low_type))
            values.append((projected[:, 2] + in_shift[side, layer, 1]).astype(low_type))
        queries = split_heads(jnp.concatenate(queries, 1), seqs)
        key_block = split_heads(jnp.concatenate(key_block, 1), seqs)
        values = split_heads(jnp.concatenate(values, 1), seqs)
        mixture, logsum = attend(queries, key_block, values, validity, score_scale)
        attended = mixture.reshape(rows, 2 * width).astype(low_type)
        attn_partial = 0.0
        for side in range(2):
            attn_partial = attn_partial + dot(
                attended[:, side * width : (side + 1) * width],
                proj_full[layer][side],
                "te,red->trd",
            ).reshape(rows, model_width)
        middle = current + group_sum(attn_partial) + proj_shift[layer]
        normed_two, standard_two, rscale_two = norm_rows(
            middle, gains[layer, 1], shifts[layer, 1], model_width
        )
        hidden_pre, hidden = [], []
        down_partial = 0.0
        for side in range(2):
            weight = up_full[layer][side].reshape(model_width, hidden_width)
            pre = dot(normed_two, weight, "td,df->tf") + up_shift[side, layer]
            hid = gelu_exact(pre).astype(low_type)
            hidden_pre.append(pre)
            hidden.append(hid)
            down_partial = down_partial + dot(
                hid, down_full[layer][side], "tf,rfd->trd"
            ).reshape(rows, model_width)
        records.append(
            (
                normed_one,
                standard_one,
                rscale_one,
                queries,
                key_block,
                values,
                logsum,
                attended,
                normed_two,
                standard_two,
                rscale_two,
                hidden_pre,
                hidden,
            )
        )
        current = (middle + group_sum(down_partial) + down_shift[layer]) * row_mask

    output_share = share_rows(current)
    residue = (output_share - teacher_wide) * all_mask
    squared = jnp.sum(residue * residue)
    grad_current = seeds + 2.0 * factor * current * row_mask

    in_blocks, proj_blocks, up_blocks, down_blocks = [], [], [], []
    feature_grads = {}
    hidden_grads = {}

    def send_back(pair):
        low = [piece.astype(low_type) for piece in pair]
        both = (low[0].astype(jnp.float32) + swap_core(low[1]).astype(jnp.float32)).astype(low_type)
        return scatter_row(both)

    def finish(block):
        pairs = [(col_count + i, col_count - 1 - i) for i in range(col_count)]
        arrived = lax.ppermute(block, ("dp", "col"), pairs)
        total = (block.astype(jnp.float32) + arrived.astype(jnp.float32)).astype(low_type)
        copied = lax.ppermute(total, "dp", [(0, 1)])
        return jnp.where(first_core, total, copied).astype(jnp.float32)

    def row_blocks(value):
        return value.reshape((row_count, value.shape[0] // row_count) + value.shape[1:])

    for layer in reversed(range(LAYERS)):
        (
            normed_one,
            standard_one,
            rscale_one,
            queries,
            key_block,
            values,
            logsum,
            attended,
            normed_two,
            standard_two,
            rscale_two,
            hidden_pre,
            hidden,
        ) = records[layer]
        grad_two = grad_current * row_mask
        grad_two_low = grad_two.astype(low_type)
        down_bias_part = jnp.sum(grad_two_low.astype(jnp.float32), axis=0)
        grad_two_blocks = grad_two_low.reshape(rows, row_count, model_width // row_count)
        grad_pre, up_bias_part, down_pair, up_pair = [], [], [], []
        normed_two_grad = 0.0
        for side in range(2):
            grad_hidden = dot(grad_two_blocks, down_full[layer][side], "trd,rfd->tf")
            ignored, gelu_pull = jax.vjp(gelu_exact, hidden_pre[side])
            pre_low = gelu_pull(grad_hidden)[0].astype(low_type)
            grad_pre.append(pre_low)
            up_bias_part.append(jnp.sum(pre_low.astype(jnp.float32), axis=0))
            weight = up_full[layer][side].reshape(model_width, hidden_width)
            normed_two_grad = normed_two_grad + dot(pre_low, weight, "tf,df->td")
        normed_two_grad = group_sum(normed_two_grad)
        for side in range(2):
            down_pair.append(dot(hidden[side], grad_two_blocks, "tf,trd->rfd"))
            up_pair.append(row_blocks(dot(normed_two, grad_pre[side], "td,tf->df")))
        down_blocks.append(send_back(down_pair))
        up_blocks.append(send_back(up_pair))
        grad_norm_two, gain_part_two, shift_part_two = norm_backward(
            normed_two_grad, standard_two, rscale_two, gains[layer, 1], model_width
        )
        grad_middle = grad_two + grad_norm_two
        grad_one_low = grad_middle.astype(low_type)
        proj_bias_part = jnp.sum(grad_one_low.astype(jnp.float32), axis=0)
        grad_one_blocks = grad_one_low.reshape(rows, row_count, model_width // row_count)
        grad_attended, proj_pair = [], []
        for side in range(2):
            grad_attended.append(
                dot(grad_one_blocks, proj_full[layer][side], "trd,red->te").astype(low_type)
            )
            proj_pair.append(
                dot(attended[:, side * width : (side + 1) * width], grad_one_blocks, "te,trd->red")
            )
        proj_blocks.append(send_back(proj_pair))
        grad_queries, grad_keys, grad_values = attend_back(
            queries,
            key_block,
            values,
            validity,
            score_scale,
            logsum,
            split_heads(jnp.concatenate(grad_attended, 1), seqs),
        )
        grad_triple = jnp.stack(
            [
                grad_queries.reshape(rows, 2, width),
                grad_keys.reshape(rows, 2, width),
                grad_values.reshape(rows, 2, width),
            ],
            axis=2,
        ).astype(low_type)
        in_bias_part = jnp.sum(grad_triple.astype(jnp.float32), axis=0)[:, ::2]
        in_pair = []
        normed_one_grad = 0.0
        for side in range(2):
            weight = in_full[layer][side].reshape(model_width, 3, width)
            normed_one_grad = normed_one_grad + dot(grad_triple[:, side], weight, "tpe,dpe->td")
        normed_one_grad = group_sum(normed_one_grad)
        for side in range(2):
            in_pair.append(row_blocks(dot(normed_one, grad_triple[:, side], "td,tpe->dpe")))
        in_blocks.append(send_back(in_pair))
        grad_norm_one, gain_part_one, shift_part_one = norm_backward(
            normed_one_grad, standard_one, rscale_one, gains[layer, 0], model_width
        )
        grad_current = grad_middle + grad_norm_one
        feature_grads[layer] = (
            gain_part_one,
            gain_part_two,
            shift_part_one,
            shift_part_two,
            proj_bias_part,
            down_bias_part,
        )
        hidden_grads[layer] = jnp.concatenate(
            [in_bias_part, jnp.stack(up_bias_part).reshape(2, -1, width)], axis=1
        )

    input_share = share_rows(grad_current)

    def together(blocks):
        return jnp.stack([finish(block) for block in blocks[::-1]])

    in_grad = together(in_blocks)
    proj_grad = together(proj_blocks)
    up_grad = together(up_blocks)
    down_grad = together(down_blocks)

    feature_parts = jnp.stack([part for layer in range(LAYERS) for part in feature_grads[layer]])
    feature_parts = feature_parts.reshape(-1, col_count, width)
    own_parts = lax.dynamic_index_in_dim(feature_parts, col_index, 1, False)
    other_parts = lax.dynamic_index_in_dim(feature_parts, col_count - 1 - col_index, 1, False)
    hidden_parts = jnp.concatenate([hidden_grads[layer] for layer in range(LAYERS)], axis=1)
    hidden_parts = jnp.where(first_core, hidden_parts, hidden_parts[::-1])
    extra = jnp.zeros((1, width), jnp.float32).at[0, 0].set(squared)
    packed = jnp.concatenate(
        [jnp.stack([own_parts, other_parts]), hidden_parts, jnp.stack([extra, extra])], axis=1
    )
    packed = butterfly_sum(packed, ("dp", "row"))
    vectors = packed[0] + flip_col(packed[1])
    squared_total = packed[0, -1, 0]
    squared_total = butterfly_sum(squared_total, ("col",))
    loss_value = squared_total / (token_total * model_width)
    per_layer = len(feature_grads[0])
    features = vectors[: LAYERS * per_layer].reshape(LAYERS, per_layer, width)
    hiddens = vectors[LAYERS * per_layer : -1].reshape(LAYERS, -1, width)
    return (
        loss_value,
        output_share,
        input_share,
        features[:, 0:2],
        features[:, 2:4],
        in_grad,
        hiddens[:, 0:2],
        proj_grad,
        features[:, 4],
        up_grad,
        hiddens[:, 2:].reshape(LAYERS, hidden_width),
        down_grad,
        features[:, 5],
    )


def solution(mesh):
    in_specs = (
        P(("dp", "row"), "col"),
        P(("dp", "row"), "col"),
        P(("dp", "row"), "col"),
        P(("dp", "row")),
        P(None, None, "col"),
        P(None, None, "col"),
        P(None, "row", None, "col"),
        P(None, None, "col"),
        P(None, "col", "row"),
        P(None, "col"),
        P(None, "row", "col"),
        P(None, "col"),
        P(None, "col", "row"),
        P(None, "col"),
    )
    out_specs = (
        P(),
        P(("dp", "row"), "col"),
        P(("dp", "row"), "col"),
        P(None, None, "col"),
        P(None, None, "col"),
        P(None, "row", None, "col"),
        P(None, None, "col"),
        P(None, "col", "row"),
        P(None, "col"),
        P(None, "row", "col"),
        P(None, "col"),
        P(None, "col", "row"),
        P(None, "col"),
    )
    return jax.shard_map(body, mesh=mesh, in_specs=in_specs, out_specs=out_specs, check_vma=False)
```

```python
import functools

import jax
import jax.numpy as jnp
from jax import lax
from jax.experimental import pallas as pl
from jax.experimental.pallas import tpu as pltpu
from jax.sharding import PartitionSpec as P

HEAD_DIM = 64
LAYERS = 2

epsilon = 1e-06
fill_value = -1e30
score_scale = HEAD_DIM ** (-0.5)
low_type = jnp.bfloat16
wide_type = jnp.float32
VMEM = pl.BlockSpec(memory_space=pltpu.VMEM)
SMEM = pl.BlockSpec(memory_space=pltpu.SMEM)
ANY = pl.BlockSpec(memory_space=pl.ANY)
vmem_bytes = 56 * 1024 * 1024


def dot(left, right):
    return lax.dot_general(
        left, right, (((1,), (0,)), ((), ())), preferred_element_type=wide_type
    )


def dot_right(left, right):
    return lax.dot_general(
        left, right, (((1,), (1,)), ((), ())), preferred_element_type=wide_type
    )


def dot_left(left, right):
    return lax.dot_general(
        left, right, (((0,), (0,)), ((), ())), preferred_element_type=wide_type
    )


def piece_copies(meta, refs, offset, tiles, target, sems):
    if len(refs) == 1:
        return [pltpu.make_async_copy(refs[0], target(None, None), sems.at[0])]
    copies = []
    core = meta[4]
    for place in range(3):
        for block in range(2):
            source = refs[place].at[block, pl.ds(offset, tiles)]
            copies.append((source, target(block, meta[place])))
    copies.append((refs[3].at[pl.ds(offset, tiles)], target(core, meta[3])))
    copies.append((refs[4].at[pl.ds(offset, tiles)], target(1 - core, meta[3])))
    return [
        pltpu.make_async_copy(source, place, sems.at[index])
        for index, (source, place) in enumerate(copies)
    ]


def in_copies(meta, refs, offset, weight, sems):
    def target(block, row_block):
        if block is None:
            return weight
        return weight.at[:, pl.ds(row_block * 256, 256), pl.ds(block * 256, 256)]

    return piece_copies(meta, refs, offset, 3, target, sems)


def proj_copies(meta, refs, offset, weight, sems):
    def target(block, row_block):
        if block is None:
            return weight
        return weight.at[pl.ds(block, 1), :, pl.ds(row_block * 256, 256)]

    return piece_copies(meta, refs, offset, 1, target, sems)


def up_copies(meta, refs, offset, weight, sems):
    def target(block, row_block):
        if block is None:
            return weight
        return weight.at[pl.ds(block * 4, 4), pl.ds(row_block * 256, 256), :]

    return piece_copies(meta, refs, offset, 4, target, sems)


def down_copies(meta, refs, offset, weight, sems):
    def target(block, row_block):
        if block is None:
            return weight
        return weight.at[pl.ds(block * 4, 4), :, pl.ds(row_block * 256, 256)]

    return piece_copies(meta, refs, offset, 4, target, sems)


def start_all(copies):
    for copy in copies:
        copy.start()


def wait_all(copies):
    for copy in copies:
        copy.wait()


def standardize(inputs):
    width = inputs.shape[1]
    centre = jnp.sum(inputs, axis=1, keepdims=True) / width
    centred = inputs - centre
    spread = jnp.sum(centred * centred, axis=1, keepdims=True) / width
    rscale = lax.rsqrt(spread + epsilon)
    return centred * rscale, rscale


def mask_rows(meta, rows, slots):
    parts = []
    for seq in range(rows // slots):
        place = lax.broadcasted_iota(jnp.int32, (slots, 1), 0)
        parts.append(jnp.where(place < meta[5 + seq], 1.0, 0.0).astype(wide_type))
    return parts[0] if len(parts) == 1 else jnp.concatenate(parts, axis=0)


def gelu_and_slope(u):
    size = jnp.abs(u) * 0.7071067811865476
    t = 1.0 / (1.0 + 0.3275911 * size)
    bell = jnp.exp(-size * size)
    tail = t * (
        0.254829592
        + t * (-0.284496736 + t * (1.421413741 + t * (-1.453152027 + t * 1.061405429)))
    )
    tail = 0.5 * tail * bell
    share = jnp.where(u >= 0.0, 1.0 - tail, tail)
    return u * share, share + u * bell * 0.3989422804014327


def place_blocks(meta, place, blocks, target):
    width = blocks[0].shape[1]
    for index, block in enumerate(blocks):
        at = pl.multiple_of(meta[place + index] * width, width)
        target[:, pl.ds(at, width)] = block[...]


def key_bias(meta, seq, slots):
    place = lax.broadcasted_iota(jnp.int32, (1, slots), 1)
    return place < meta[5 + seq]


def split_refs(refs, counts):
    out = []
    at = 0
    for count in counts:
        out.append(refs[at : at + count])
        at += count
    return out


def attend_kernel(first, slots, counts, offsets, meta, *refs):
    (base, sums, params, in_refs, proj_refs, outs, scratch) = split_refs(refs, counts)
    gains, shifts, query_shift, value_shift = params
    x_ref, normed_ref, query_ref, key_ref, value_ref, lse_ref, mixed_ref, wide_ref, low_ref = outs
    in_weight, proj_weight, in_sems, proj_sems = scratch
    in_moves = in_copies(meta, in_refs, offsets[0], in_weight, in_sems)
    proj_moves = proj_copies(meta, proj_refs, offsets[1], proj_weight, proj_sems)
    start_all(in_moves)
    start_all(proj_moves)
    rows = x_ref.shape[0]
    if first:
        place_blocks(meta, 5 + rows // slots, base, x_ref)
        current = x_ref[...]
    else:
        own, arrived, bias = sums
        current = base[0][...] + own[...] + arrived[...].astype(wide_type) + bias[...]
        current = current * mask_rows(meta, rows, slots)
        x_ref[...] = current
    standard, _ = standardize(current)
    normed = (standard * gains[...] + shifts[...]).astype(low_type)
    normed_ref[...] = normed
    wait_all(in_moves)
    query_ref[...] = (dot(normed, in_weight[0]) + query_shift[...]).astype(low_type)
    key_ref[...] = dot(normed, in_weight[1]).astype(low_type)
    value_ref[...] = (dot(normed, in_weight[2]) + value_shift[...]).astype(low_type)
    heads = query_ref.shape[1] // HEAD_DIM
    for seq in range(rows // slots):
        span = slice(seq * slots, (seq + 1) * slots)
        valid = key_bias(meta, seq, slots)
        for head in range(heads):
            lanes = slice(head * HEAD_DIM, (head + 1) * HEAD_DIM)
            scores = dot_right(query_ref[span, lanes], key_ref[span, lanes]) * score_scale
            scores = jnp.where(valid, scores, fill_value)
            maximum = jnp.max(scores, axis=1, keepdims=True)
            exponent = jnp.exp(scores - maximum)
            mass = jnp.sum(exponent, axis=1, keepdims=True)
            attention = (exponent * (1.0 / mass)).astype(low_type)
            mixed_ref[span, lanes] = dot(attention, value_ref[span, lanes]).astype(low_type)
            lse_ref[span, head : head + 1] = maximum + jnp.log(mass)
    wait_all(proj_moves)
    block = proj_weight.shape[1]
    total = dot(mixed_ref[:, :block], proj_weight[0])
    for index in range(1, proj_weight.shape[0]):
        total = total + dot(
            mixed_ref[:, index * block : (index + 1) * block], proj_weight[index]
        )
    wide_ref[...] = total
    low_ref[...] = total.astype(low_type)


def feed_kernel(counts, offsets, meta, *refs):
    (sums, params, up_refs, down_refs, outs, scratch) = split_refs(refs, counts)
    base, own, arrived, bias = sums
    gains, shifts, up_shift = params
    middle_ref, normed_ref, hidden_ref, slope_ref, wide_ref, low_ref = outs
    up_weight, down_weight, up_sems, down_sems = scratch
    up_moves = up_copies(meta, up_refs, offsets[0], up_weight, up_sems)
    down_moves = down_copies(meta, down_refs, offsets[1], down_weight, down_sems)
    start_all(up_moves)
    start_all(down_moves)
    middle = base[...] + own[...] + arrived[...].astype(wide_type) + bias[...]
    middle_ref[...] = middle
    standard, _ = standardize(middle)
    normed = (standard * gains[...] + shifts[...]).astype(low_type)
    normed_ref[...] = normed
    wait_all(up_moves)
    width = up_weight.shape[2]
    for index in range(up_weight.shape[0]):
        lanes = slice(index * width, (index + 1) * width)
        pre = dot(normed_ref[...], up_weight[index]) + up_shift[:, lanes]
        hidden, slope = gelu_and_slope(pre)
        hidden_ref[:, lanes] = hidden.astype(low_type)
        slope_ref[:, lanes] = slope.astype(low_type)
    wait_all(down_moves)
    rows = down_weight.shape[0] * down_weight.shape[1]
    total = dot(hidden_ref[...], down_weight[...].reshape(rows, down_weight.shape[2]))
    wide_ref[...] = total
    low_ref[...] = total.astype(low_type)


def norm_back(grad_rows, inputs, gains):
    standard, rscale = standardize(inputs)
    width = inputs.shape[1]
    scaled = grad_rows * gains
    first = jnp.sum(scaled, axis=1, keepdims=True) / width
    second = jnp.sum(scaled * standard, axis=1, keepdims=True) / width
    grad_input = rscale * (scaled - first - standard * second)
    return (
        grad_input,
        jnp.sum(grad_rows * standard, axis=0, keepdims=True),
        jnp.sum(grad_rows, axis=0, keepdims=True),
    )


def last_kernel(slots, meta, factor, base, own, arrived, bias, *refs):
    seeds, (current_ref, grad_ref) = refs[:-2], refs[-2:]
    rows = base.shape[0]
    mask = mask_rows(meta, rows, slots)
    place_blocks(meta, 5 + rows // slots, seeds, grad_ref)
    current = base[...] + own[...] + arrived[...].astype(wide_type) + bias[...]
    current = current * mask
    current_ref[...] = current
    grad_ref[...] = grad_ref[...] + factor[0] * current


def pull_kernel(inputs, gains, base, own, arrived, grad_ref, gain_ref, shift_ref):
    summed = own[...] + arrived[...].astype(wide_type)
    grad, gain, shift = norm_back(summed, inputs[...], gains[...])
    grad_ref[...] = base[...] + grad
    gain_ref[...] = gain
    shift_ref[...] = shift


def feed_back_kernel(slots, counts, offsets, meta, *refs):
    (sums, up_refs, down_refs, outs, scratch) = split_refs(refs, counts)
    grad, slope_ref = sums
    masked_ref, masked_low_ref, pre_ref, down_bias_ref, up_bias_ref, wide_ref, low_ref = outs
    up_weight, down_weight, up_sems, down_sems = scratch
    up_moves = up_copies(meta, up_refs, offsets[0], up_weight, up_sems)
    down_moves = down_copies(meta, down_refs, offsets[1], down_weight, down_sems)
    start_all(down_moves)
    start_all(up_moves)
    masked = grad[...] * mask_rows(meta, grad.shape[0], slots)
    masked_ref[...] = masked
    masked_low = masked.astype(low_type)
    masked_low_ref[...] = masked_low
    down_bias_ref[...] = jnp.sum(masked_low.astype(wide_type), axis=0, keepdims=True)
    wait_all(down_moves)
    width = up_weight.shape[2]
    for index in range(up_weight.shape[0]):
        lanes = slice(index * width, (index + 1) * width)
        hidden = dot_right(masked_low_ref[...], down_weight[index])
        pre = (hidden * slope_ref[:, lanes].astype(wide_type)).astype(low_type)
        pre_ref[:, lanes] = pre
        up_bias_ref[:, lanes] = jnp.sum(pre.astype(wide_type), axis=0, keepdims=True)
    wait_all(up_moves)
    total = dot_right(pre_ref[:, :width], up_weight[0])
    for index in range(1, up_weight.shape[0]):
        lanes = slice(index * width, (index + 1) * width)
        total = total + dot_right(pre_ref[:, lanes], up_weight[index])
    wide_ref[...] = total
    low_ref[...] = total.astype(low_type)


def attend_back_kernel(slots, counts, offsets, meta, *refs):
    (sums, params, saved, in_refs, proj_refs, outs, scratch) = split_refs(refs, counts)
    own, arrived, middle, masked = sums
    (gains,) = params
    query_ref, key_ref, value_ref, lse_ref = saved
    (
        grad_ref,
        low_grad_ref,
        gain_ref,
        shift_ref,
        proj_bias_ref,
        triple_ref,
        in_bias_ref,
        wide_ref,
        low_ref,
    ) = outs
    in_weight, proj_weight, mixed_grad, in_sems, proj_sems = scratch
    in_moves = in_copies(meta, in_refs, offsets[0], in_weight, in_sems)
    proj_moves = proj_copies(meta, proj_refs, offsets[1], proj_weight, proj_sems)
    start_all(proj_moves)
    start_all(in_moves)
    summed = own[...] + arrived[...].astype(wide_type)
    grad, gain, shift = norm_back(summed, middle[...], gains[...])
    grad = masked[...] + grad
    grad_ref[...] = grad
    gain_ref[...] = gain
    shift_ref[...] = shift
    grad_low = grad.astype(low_type)
    low_grad_ref[...] = grad_low
    proj_bias_ref[...] = jnp.sum(grad_low.astype(wide_type), axis=0, keepdims=True)
    wait_all(proj_moves)
    block = proj_weight.shape[1]
    for index in range(proj_weight.shape[0]):
        mixed_grad[:, index * block : (index + 1) * block] = dot_right(
            low_grad_ref[...], proj_weight[index]
        ).astype(low_type)
    heads = query_ref.shape[1] // HEAD_DIM
    rows = query_ref.shape[0]
    for seq in range(rows // slots):
        span = slice(seq * slots, (seq + 1) * slots)
        valid = key_bias(meta, seq, slots)
        for head in range(heads):
            lanes = slice(head * HEAD_DIM, (head + 1) * HEAD_DIM)
            queries = query_ref[span, lanes]
            keys = key_ref[span, lanes]
            outer = mixed_grad[span, lanes]
            scores = dot_right(queries, keys) * score_scale
            scores = jnp.where(valid, scores, fill_value)
            chance = jnp.exp(scores - lse_ref[span, head : head + 1])
            grad_chance = dot_right(outer, value_ref[span, lanes])
            inner = jnp.sum(grad_chance * chance, axis=1, keepdims=True)
            grad_scores = (chance * (grad_chance - inner)).astype(low_type)
            triple_ref[2, span, lanes] = dot_left(chance.astype(low_type), outer).astype(low_type)
            triple_ref[0, span, lanes] = (dot(grad_scores, keys) * score_scale).astype(low_type)
            triple_ref[1, span, lanes] = (dot_left(grad_scores, queries) * score_scale).astype(
                low_type
            )
    in_bias_ref[0:1, :] = jnp.sum(triple_ref[0].astype(wide_type), axis=0, keepdims=True)
    in_bias_ref[1:2, :] = jnp.sum(triple_ref[2].astype(wide_type), axis=0, keepdims=True)
    wait_all(in_moves)
    total = dot_right(triple_ref[0], in_weight[0])
    total = total + dot_right(triple_ref[1], in_weight[1])
    total = total + dot_right(triple_ref[2], in_weight[2])
    wide_ref[...] = total
    low_ref[...] = total.astype(low_type)


def feed_weight_kernel(meta, normed, pre, hidden, masked_low, *outs):
    def write(place, block, row_block):
        columns = pl.ds(pl.multiple_of(row_block * 256, 256), 256)
        for tile in range(4):
            lanes = pl.ds(pl.multiple_of(block * 1024 + tile * 256, 256), 256)
            place[tile] = dot_left(normed[:, columns], pre[:, lanes]).astype(low_type)
            place[4 + tile] = dot_left(hidden[:, lanes], masked_low[:, columns]).astype(low_type)

    write_pieces(meta, outs, write)


def attend_weight_kernel(meta, normed, triple, mixed, grad_low, *outs):
    def write(place, block, row_block):
        columns = pl.ds(pl.multiple_of(row_block * 256, 256), 256)
        lanes = pl.ds(pl.multiple_of(block * 256, 256), 256)
        for kind in range(3):
            place[kind] = dot_left(normed[:, columns], triple[kind, :, lanes]).astype(low_type)
        place[3] = dot_left(mixed[:, lanes], grad_low[:, columns]).astype(low_type)

    write_pieces(meta, outs, write)


def write_pieces(meta, outs, write):
    core = meta[4]
    for place in range(3):
        for block in range(2):
            write(outs[place].at[block], block, meta[place])
    write(outs[3], core, meta[3])
    write(outs[4], 1 - core, meta[3])


def flip_col(value):
    count = lax.axis_size("col")
    return lax.ppermute(value, "col", [(i, count - 1 - i) for i in range(count)])


def swap_core(value):
    count = lax.axis_size("dp")
    return lax.ppermute(value, "dp", [(i, count - 1 - i) for i in range(count)])


def group_shift(value, step):
    count = lax.axis_size("col")
    half = count // 2
    pairs = [(i, i // half * half + (i % half + step) % half) for i in range(count)]
    return lax.ppermute(value, "col", pairs)


def cross_row(value, first_step, second_step):
    rows = lax.axis_size("row")
    cols = lax.axis_size("col")
    pairs = []
    for core, step in ((0, first_step), (1, second_step)):
        for row in range(rows):
            for col in range(cols):
                source = (core * rows + row) * cols + col
                pairs.append((source, (core * rows + (row ^ step)) * cols + col))
    return lax.ppermute(value, ("dp", "row", "col"), pairs)


def group_total(wide, low):
    arrived = group_shift(low, 1)
    for step in range(2, lax.axis_size("col") // 2):
        wide = wide + group_shift(low, step).astype(wide_type)
    return wide, arrived


def butterfly_sum(value, axes):
    for axis in axes:
        count = lax.axis_size(axis)
        step = 1
        while step < count:
            value = value + lax.ppermute(value, axis, [(i, i ^ step) for i in range(count)])
            step *= 2
    return value


def after(value, *events):
    return lax.optimization_barrier((value,) + events)[0]


def order_blocks(pair):
    count = lax.axis_size("col")
    half = count // 2
    col_index = lax.axis_index("col")
    base = col_index // half * half
    wanted = lax.broadcasted_iota(jnp.int32, (count,) + pair.shape[1:], 0)
    whole = jnp.zeros((count,) + pair.shape[1:], pair.dtype)
    for step in range(half):
        piece = pair if step == 0 else group_shift(pair, step)
        source = base + (col_index - base + half - step) % half
        whole = jnp.where(wanted == source, piece[0][None], whole)
        whole = jnp.where(wanted == count - 1 - source, piece[1][None], whole)
    return whole


def add(left, right):
    return (left.astype(wide_type) + right.astype(wide_type)).astype(low_type)


def gather_near(own):
    return cross_row(own, 1, 2)


def gather_far(near, first_core):
    return cross_row(jnp.where(first_core, near[0], near[1]), 2, 1)


def gather_pieces(own, near, far):
    return (own, near, swap_core(near), far, swap_core(far))


def flip_tiles(shard, first_core):
    half = shard.shape[0] // 2
    got = flip_col(jnp.where(first_core, shard[:half], shard[half:]))
    return got, swap_core(got)


def join_tiles(shard, got, other, first_core):
    halves = jnp.where(first_core, jnp.stack([got, other]), jnp.stack([other, got]))
    return jnp.stack([shard, halves.reshape(shard.shape)])


def scatter_first(pieces):
    own, near, near_other, far, far_other = pieces
    return own, near, swap_core(near_other), add(far, swap_core(far_other))


def scatter_second(own, near, near_arrived, far, moved, first_core):
    moved = moved.astype(wide_type)
    total = near.astype(wide_type) + near_arrived.astype(wide_type)
    lower = total[0] + jnp.where(first_core, moved, 0.0)
    upper = total[1] + jnp.where(first_core, 0.0, moved)
    return own, jnp.stack([lower, upper]).astype(low_type)


def scatter_third(own, near, first_core):
    own = add(own, cross_row(near, 1, 2))
    half = own.shape[1] // 2
    lower, upper = own[:, :half], own[:, half:]
    arrived = swap_core(jnp.where(first_core, upper, lower))
    return add(jnp.where(first_core, lower, upper), arrived)


def scatter_fourth(part, first_core):
    part = add(part[0], flip_col(part[1]))
    other = swap_core(part)
    halves = jnp.where(first_core, jnp.stack([part, other]), jnp.stack([other, part]))
    return halves.reshape((-1,) + part.shape[1:]).astype(wide_type)


def body(
    states,
    teacher,
    cotangent,
    lengths,
    norm_gain,
    norm_bias,
    in_weight,
    in_bias,
    proj_weight,
    proj_bias,
    up_weight,
    up_bias,
    down_weight,
    down_bias,
):
    col_count = lax.axis_size("col")
    row_count = lax.axis_size("row")
    core_count = lax.axis_size("dp")
    half_group = col_count // 2
    col_index = lax.axis_index("col")
    row_index = lax.axis_index("row")
    core_index = lax.axis_index("dp")
    group_index = col_index // half_group
    first_core = core_index == 0
    token_rows, width = states.shape
    model_width = width * col_count
    seqs = lengths.shape[0] // 2
    rows = token_rows // 2
    slots = rows // seqs
    hidden_width = up_bias.shape[1]
    tiled = row_count == 4 and width == 256 and hidden_width == 1024 and model_width == 1024
    row_width = model_width // row_count
    heads_width = 2 * width
    feed_width = 2 * hidden_width
    in_thirds = jnp.transpose(in_weight, (0, 2, 1, 3))

    def own_half(value):
        return lax.dynamic_slice_in_dim(value, group_index * rows, rows, 0)

    def other_half(value):
        return lax.dynamic_slice_in_dim(value, (1 - group_index) * rows, rows, 0)

    def row_blocks(own, flipped, event):
        blocks = [own, flipped]
        for step in range(1, half_group):
            blocks = blocks + [group_shift(own, step), group_shift(after(flipped, event), step)]
        return blocks

    block_places = []
    for step in range(half_group):
        base = group_index * half_group
        source = base + (col_index - base + half_group - step) % half_group
        block_places = block_places + [source, col_count - 1 - source]

    def share_rows(value, kind=wide_type):
        own = lax.dynamic_slice_in_dim(value, col_index * width, width, 1)
        other = lax.dynamic_slice_in_dim(value, (col_count - 1 - col_index) * width, width, 1)
        received = flip_col(other.astype(kind)).astype(wide_type)
        lower = jnp.where(group_index == 0, own, received)
        upper = jnp.where(group_index == 0, received, own)
        return jnp.concatenate([lower, upper])

    own_lengths = lax.dynamic_slice_in_dim(lengths, group_index * seqs, seqs, 0)
    meta = jnp.concatenate(
        [
            jnp.stack(
                [
                    row_index,
                    row_index ^ (1 + core_index),
                    row_index ^ (2 - core_index),
                    row_index ^ 3,
                    core_index,
                ]
            ),
            own_lengths,
            jnp.stack(block_places),
        ]
    ).astype(jnp.int32)

    in_full, proj_full, up_full, down_full = ([None] * LAYERS for kind in range(4))
    feature_pack = jnp.concatenate(
        [norm_gain.reshape(-1, width), norm_bias.reshape(-1, width), proj_bias, down_bias]
    )
    hidden_pack = jnp.concatenate([in_bias.reshape(-1, width), up_bias.reshape(-1, width)])
    feature_rows = feature_pack.shape[0]
    small = jnp.concatenate([feature_pack, hidden_pack])
    small_flipped = flip_col(small)
    states_own, states_other = own_half(states), other_half(states)
    if tiled:

        def up_tiles(weight):
            return jnp.transpose(weight.reshape(256, 4, 256), (1, 0, 2))

        def down_tiles(weight):
            return weight.reshape(4, 256, 256)

        def attend_tiles(thirds, square):
            return jnp.concatenate([thirds, square[None]])

        count = 6
        shards, flips, owns, nears, fars = ([None] * count for kind in range(5))

        def flip(place, *events):
            layer = place // 3
            if place % 3 == 0:
                thirds, square = in_thirds[layer], proj_weight[layer]
                if events:
                    thirds, square = after(thirds, *events), after(square, *events)
                shards[place] = attend_tiles(thirds, square)
            elif place % 3 == 1:
                shards[place] = up_tiles(after(up_weight[layer], *events))
            else:
                shards[place] = down_tiles(after(down_weight[layer], *events))
            flips[place] = flip_tiles(shards[place], first_core)
            return flips[place][0]

        def near(place, *events):
            owns[place] = join_tiles(shards[place], *flips[place], first_core)
            nears[place] = gather_near(after(owns[place], *events))
            return nears[place]

        def far(place, *events):
            fars[place] = gather_far(after(nears[place], *events), first_core)
            return fars[place]

        def pieces(place):
            return gather_pieces(owns[place], nears[place], fars[place])

        slot = [flip(0)]
        states_flipped = flip_col(after(states_other, *slot))
        slot = [near(0), states_flipped]
        states_blocks = row_blocks(states_own, states_flipped, slot[0])
        slot = [far(0, *slot), flip(1, *slot), *states_blocks[2:]]
        slot = [near(1, *slot), flip(2, *slot)]
        states_blocks[0] = after(states_blocks[0], *slot)
        slot = [far(1, *slot), near(2, *slot), flip(3, *slot)]
        in_full[0], proj_full[0] = (pieces(0), 0), (pieces(0), 3)
    else:

        def both_blocks(shard):
            own = lax.all_gather(shard, "row", axis=0, tiled=False)
            return jnp.stack([own, flip_col(own)])

        for layer in range(LAYERS):
            whole = jnp.transpose(both_blocks(in_thirds[layer]), (2, 1, 3, 0, 4))
            in_full[layer] = ((whole.reshape(3, model_width, heads_width),), 0)
            whole = jnp.transpose(both_blocks(proj_weight[layer]), (0, 2, 1, 3))
            proj_full[layer] = ((whole.reshape(2, width, model_width),), 0)
            whole = both_blocks(up_weight[layer]).reshape(2, model_width, -1, 256)
            whole = jnp.transpose(whole, (0, 2, 1, 3))
            up_full[layer] = ((whole.reshape(-1, model_width, 256),), 0)
            whole = jnp.transpose(both_blocks(down_weight[layer]), (0, 2, 1, 3))
            down_full[layer] = ((whole.reshape(-1, 256, model_width),), 0)
        states_blocks = row_blocks(states_own, flip_col(states_other), states)

    small_pair = jnp.stack([small, small_flipped])
    feature_all = order_blocks(small_pair[:, :feature_rows])
    feature_all = jnp.transpose(feature_all, (1, 0, 2)).reshape(feature_rows, model_width)
    gains = feature_all[: 2 * LAYERS].reshape(LAYERS, 2, 1, model_width)
    shifts = feature_all[2 * LAYERS : 4 * LAYERS].reshape(LAYERS, 2, 1, model_width)
    proj_shift = feature_all[4 * LAYERS : 5 * LAYERS].reshape(LAYERS, 1, model_width)
    down_shift = feature_all[5 * LAYERS :].reshape(LAYERS, 1, model_width)
    hidden_pair = small_pair[:, feature_rows:]
    in_shift = hidden_pair[:, : 2 * LAYERS].reshape(2, LAYERS, 2, width)
    in_shift = jnp.transpose(in_shift, (1, 2, 0, 3)).reshape(LAYERS, 2, 1, heads_width)
    up_shift = hidden_pair[:, 2 * LAYERS :].reshape(2, LAYERS, hidden_width)
    up_shift = jnp.transpose(up_shift, (1, 0, 2)).reshape(LAYERS, 1, feed_width)


    def shape(*dims, kind=wide_type):
        return jax.ShapeDtypeStruct(dims, kind)

    def call(kernel, cost, operands, specs, outs, scratch=()):
        return pl.pallas_call(
            kernel,
            out_shape=outs,
            in_specs=specs,
            out_specs=[VMEM] * len(outs),
            scratch_shapes=list(scratch),
            compiler_params=pltpu.CompilerParams(vmem_limit_bytes=vmem_bytes),
            cost_estimate=pl.CostEstimate(
                flops=int(cost * 1.15e9), bytes_accessed=1024 * 1024, transcendentals=0
            ),
        )(*operands)

    wide_rows = shape(rows, model_width)
    low_rows = shape(rows, model_width, kind=low_type)
    low_heads = shape(rows, heads_width, kind=low_type)
    heads = heads_width // HEAD_DIM
    feed_tiles = feed_width // 256
    attend_scratch = [
        pltpu.VMEM((3, model_width, heads_width), low_type),
        pltpu.VMEM((2, width, model_width), low_type),
    ]
    feed_scratch = [
        pltpu.VMEM((feed_tiles, model_width, 256), low_type),
        pltpu.VMEM((feed_tiles, 256, model_width), low_type),
    ]
    sems = [pltpu.SemaphoreType.DMA((8,)), pltpu.SemaphoreType.DMA((8,))]

    def attend(layer, base, sums):
        first = len(sums) == 0
        params = [gains[layer, 0], shifts[layer, 0], in_shift[layer, 0], in_shift[layer, 1]]
        in_refs, in_offset = in_full[layer]
        proj_refs, proj_offset = proj_full[layer]
        counts = (len(base), len(sums), 4, len(in_refs), len(proj_refs), 9, 4)
        operands = [meta, *base, *sums, *params, *in_refs, *proj_refs]
        specs = [SMEM] + [VMEM] * (4 + len(base) + len(sums)) + [ANY] * (len(in_refs) + len(proj_refs))
        kernel = functools.partial(attend_kernel, first, slots, counts, (in_offset, proj_offset))
        outs = [
            wide_rows,
            low_rows,
            low_heads,
            low_heads,
            low_heads,
            shape(rows, heads),
            low_heads,
            wide_rows,
            low_rows,
        ]
        return call(kernel, 10.5, operands, specs, outs, attend_scratch + sems)

    def feed(layer, base, sums):
        params = [gains[layer, 1], shifts[layer, 1], up_shift[layer]]
        up_refs, up_offset = up_full[layer]
        down_refs, down_offset = down_full[layer]
        counts = (4, 3, len(up_refs), len(down_refs), 6, 4)
        operands = [meta, base, *sums, *params, *up_refs, *down_refs]
        specs = [SMEM] + [VMEM] * 7 + [ANY] * (len(up_refs) + len(down_refs))
        kernel = functools.partial(feed_kernel, counts, (up_offset, down_offset))
        low_feed = shape(rows, feed_width, kind=low_type)
        outs = [wide_rows, low_rows, low_feed, low_feed, wide_rows, low_rows]
        return call(kernel, 12.0, operands, specs, outs, feed_scratch + sems)

    def feed_back(layer, grad, slope):
        up_refs, up_offset = up_full[layer]
        down_refs, down_offset = down_full[layer]
        counts = (2, len(up_refs), len(down_refs), 7, 4)
        operands = [meta, grad, slope, *up_refs, *down_refs]
        specs = [SMEM] + [VMEM] * 2 + [ANY] * (len(up_refs) + len(down_refs))
        kernel = functools.partial(feed_back_kernel, slots, counts, (up_offset, down_offset))
        outs = [
            wide_rows,
            low_rows,
            shape(rows, feed_width, kind=low_type),
            shape(1, model_width),
            shape(1, feed_width),
            wide_rows,
            low_rows,
        ]
        return call(kernel, 10.0, operands, specs, outs, feed_scratch + sems)

    def attend_back(layer, sums, middle, masked, saved):
        in_refs, in_offset = in_full[layer]
        proj_refs, proj_offset = proj_full[layer]
        counts = (4, 1, 4, len(in_refs), len(proj_refs), 9, 5)
        operands = [meta, *sums, middle, masked, gains[layer, 1], *saved, *in_refs, *proj_refs]
        specs = [SMEM] + [VMEM] * 9 + [ANY] * (len(in_refs) + len(proj_refs))
        kernel = functools.partial(attend_back_kernel, slots, counts, (in_offset, proj_offset))
        outs = [
            wide_rows,
            low_rows,
            shape(1, model_width),
            shape(1, model_width),
            shape(1, model_width),
            shape(3, rows, heads_width, kind=low_type),
            shape(2, heads_width),
            wide_rows,
            low_rows,
        ]
        scratch = attend_scratch + [pltpu.VMEM((rows, heads_width), low_type)] + sems
        return call(kernel, 12.0, operands, specs, outs, scratch)

    def weight_tiles(kernel, tiles, cost, *operands):
        outs = [shape(2, tiles, 256, 256, kind=low_type)] * 3
        outs = outs + [shape(tiles, 256, 256, kind=low_type)] * 2
        specs = [SMEM] + [VMEM] * len(operands)
        return call(kernel, cost, (meta,) + operands, specs, outs)

    positions = jnp.arange(slots, dtype=jnp.int32)
    all_mask = (positions[None, :] < lengths[:, None]).reshape(token_rows, 1).astype(wide_type)
    teacher_wide = teacher.astype(wide_type)

    saved = []
    base, sums = states_blocks, ()
    for layer in range(LAYERS):
        if layer > 0:
            sums = (*sums, down_shift[layer - 1])
        current, normed_one, queries, keys, values, lse, mixed, wide, low = attend(
            layer, base, sums
        )
        event = wide
        if layer == 0 and tiled:
            slot = [event, *slot]
            slot = [far(2, *slot), near(3, *slot), flip(4, *slot)]
            up_full[0], down_full[0] = (pieces(1), 0), (pieces(2), 0)
        wide, arrived = group_total(wide, low)
        if layer == 0:
            token_total = butterfly_sum(after(jnp.sum(lengths), event), ("dp", "row"))
            token_total = token_total.astype(wide_type)
            factor = 2.0 * token_rows * core_count * row_count / token_total
            seed_share = cotangent - factor * all_mask * teacher_wide
            seed_own, seed_other = own_half(seed_share), other_half(seed_share)
            if tiled:
                arrived = after(arrived, *slot)
                slot = [far(3, *slot), near(4, *slot), flip(5, *slot)]
            else:
                seed_flipped = flip_col(seed_other)
        else:
            if tiled:
                slot = [event, *slot]
                slot = [far(5, *slot), seed_flipped]
                up_full[1], down_full[1] = (pieces(4), 0), (pieces(5), 0)
                arrived = after(arrived, seed_flipped)
            seed_blocks = row_blocks(after(seed_own, arrived), seed_flipped, arrived)
        middle, normed_two, hidden, slope, wide, low = feed(
            layer, current, (wide, arrived, proj_shift[layer])
        )
        event = wide
        if layer == 1:
            low = after(low, *seed_blocks)
        wide, arrived = group_total(wide, low)
        if layer == 0 and tiled:
            slot = [event, *slot]
            seed_flipped = flip_col(after(seed_other, *slot))
            slot = [far(4, *slot), near(5, *slot)]
            in_full[1], proj_full[1] = (pieces(3), 0), (pieces(3), 3)
        base, sums = [middle], (wide, arrived)
        saved.append(
            (current, normed_one, queries, keys, values, lse, mixed, middle, normed_two, hidden, slope)
        )
    final, grad = call(
        functools.partial(last_kernel, slots),
        4.3,
        (meta, factor.reshape(1), *base, *sums, down_shift[LAYERS - 1], *seed_blocks),
        [SMEM, SMEM] + [VMEM] * (4 + len(seed_blocks)),
        [wide_rows, wide_rows],
    )
    output_share = share_rows(final)
    residue = (output_share - teacher_wide) * all_mask
    squared = jnp.sum(residue * residue)

    feature_grads = {}
    hidden_grads = {}
    in_grads, proj_grads, up_grads, down_grads = ([None] * LAYERS for kind in range(4))

    def keep_feed(layer, tiles):
        up_grads[layer] = jnp.transpose(tiles[:4], (1, 0, 2)).reshape(256, 1024)
        down_grads[layer] = tiles[4:].reshape(1024, 256)

    def keep_attend(layer, tiles):
        in_grads[layer] = tiles[:3]
        proj_grads[layer] = tiles[3]

    def before_swap(low):
        for item in under_way:
            if item[0] == 1:
                item[0] = 2
                item[1] = item[1] + (cross_row(item[1][3], 2, 1),)
                low = after(low, item[1][4])
        return low

    def beside_swap(arrived, pieces, keep):
        value = scatter_first(pieces)
        events = [*pieces, *value]
        for item in under_way:
            if item[0] == 2:
                item[1] = scatter_second(*item[1], first_core)
                events.append(item[1][1])
            elif item[0] == 3:
                item[1] = scatter_third(*item[1], first_core)
                events.append(item[1])
            elif item[0] == 4:
                item[1] = scatter_fourth(item[1], first_core)
                events.append(item[1])
                item[2](item[1])
            item[0] += 1
        under_way.append([1, value, keep])
        return after(arrived, *events)

    under_way = []
    for layer in reversed(range(LAYERS)):
        current, normed_one, queries, keys, values, lse, mixed, middle, normed_two, hidden, slope = (
            saved[layer]
        )
        masked, masked_low, pre, down_bias_part, up_bias_part, wide, low = feed_back(
            layer, grad, slope
        )
        if tiled:
            low = before_swap(low)
        wide, arrived = group_total(wide, low)
        if tiled:
            if layer == LAYERS - 1:
                arrived = after(arrived, output_share)
            pieces = weight_tiles(
                feed_weight_kernel, 8, 9.0, normed_two, pre, hidden, masked_low
            )
            arrived = beside_swap(arrived, pieces, functools.partial(keep_feed, layer))
        (
            grad,
            grad_low,
            gain_two,
            shift_two,
            proj_bias_part,
            triple,
            in_bias_part,
            wide,
            low,
        ) = attend_back(layer, (wide, arrived), middle, masked, (queries, keys, values, lse))
        if tiled:
            low = before_swap(low)
        wide, arrived = group_total(wide, low)
        if tiled:
            pieces = weight_tiles(
                attend_weight_kernel, 4, 5.5, normed_one, triple, mixed, grad_low
            )
            arrived = beside_swap(arrived, pieces, functools.partial(keep_attend, layer))
        else:

            def product(spec, left, right):
                return jnp.einsum(spec, left, right, preferred_element_type=wide_type)

            def own_block(blocks):
                part = lax.psum_scatter(
                    blocks.astype(low_type), "row", scatter_dimension=1, tiled=False
                )
                mine = add(part[0], flip_col(part[1]))
                return mine.astype(wide_type) + swap_core(mine).astype(wide_type)

            def by_row(value):
                return value.reshape(rows, row_count, row_width)

            def by_block(value):
                return value.reshape(value.shape[:-1] + (2, -1))

            in_grads[layer] = own_block(
                product("trd,ptbe->brpde", by_row(normed_one), by_block(triple))
            )
            proj_grads[layer] = own_block(
                product("tbe,trd->bred", by_block(mixed), by_row(grad_low))
            )
            up_grads[layer] = own_block(product("trd,tbe->brde", by_row(normed_two), by_block(pre)))
            down_grads[layer] = own_block(
                product("tbe,trd->bred", by_block(hidden), by_row(masked_low))
            )
        grad, gain_one, shift_one = call(
            pull_kernel,
            4.3,
            (current, gains[layer, 0], grad, wide, arrived),
            [VMEM] * 5,
            [wide_rows, shape(1, model_width), shape(1, model_width)],
        )
        feature_grads[layer] = (
            gain_one,
            gain_two,
            shift_one,
            shift_two,
            proj_bias_part,
            down_bias_part,
        )
        hidden_grads[layer] = jnp.concatenate(
            [
                jnp.transpose(in_bias_part.reshape(2, 2, width), (1, 0, 2)),
                up_bias_part.reshape(2, -1, width),
            ],
            axis=1,
        )

    for step, value, saver in under_way:
        if step <= 1:
            value = value + (cross_row(value[3], 2, 1),)
        if step <= 2:
            value = scatter_second(*value, first_core)
        if step <= 3:
            value = scatter_third(*value, first_core)
        if step <= 4:
            saver(scatter_fourth(value, first_core))
    input_share = share_rows(grad, low_type)

    feature_parts = jnp.concatenate(
        [part for layer in range(LAYERS) for part in feature_grads[layer]]
    )
    feature_parts = feature_parts.reshape(-1, col_count, width)
    own_parts = lax.dynamic_index_in_dim(feature_parts, col_index, 1, False)
    other_parts = lax.dynamic_index_in_dim(feature_parts, col_count - 1 - col_index, 1, False)
    hidden_parts = jnp.concatenate([hidden_grads[layer] for layer in range(LAYERS)], axis=1)
    extra = jnp.zeros((1, width), wide_type).at[0, 0].set(squared)
    packed = jnp.concatenate(
        [jnp.stack([own_parts, other_parts]), hidden_parts, jnp.stack([extra, extra])], axis=1
    )
    packed = butterfly_sum(packed, ("dp", "row"))
    vectors = packed[0] + flip_col(packed[1])
    squared_total = butterfly_sum(packed[0, -1, 0], ("col",))
    loss_value = squared_total / (token_total * model_width)
    per_layer = len(feature_grads[0])
    features = vectors[: LAYERS * per_layer].reshape(LAYERS, per_layer, width)
    hiddens = vectors[LAYERS * per_layer : -1].reshape(LAYERS, -1, width)
    return (
        loss_value,
        output_share,
        input_share,
        features[:, 0:2],
        features[:, 2:4],
        jnp.transpose(jnp.stack(in_grads), (0, 2, 1, 3)),
        hiddens[:, 0:2],
        jnp.stack(proj_grads),
        features[:, 4],
        jnp.stack(up_grads),
        hiddens[:, 2:].reshape(LAYERS, hidden_width),
        jnp.stack(down_grads),
        features[:, 5],
    )


def solution(mesh):
    in_specs = (
        P(("dp", "row"), "col"),
        P(("dp", "row"), "col"),
        P(("dp", "row"), "col"),
        P(("dp", "row")),
        P(None, None, "col"),
        P(None, None, "col"),
        P(None, "row", None, "col"),
        P(None, None, "col"),
        P(None, "col", "row"),
        P(None, "col"),
        P(None, "row", "col"),
        P(None, "col"),
        P(None, "col", "row"),
        P(None, "col"),
    )
    out_specs = (
        P(),
        P(("dp", "row"), "col"),
        P(("dp", "row"), "col"),
        P(None, None, "col"),
        P(None, None, "col"),
        P(None, "row", None, "col"),
        P(None, None, "col"),
        P(None, "col", "row"),
        P(None, "col"),
        P(None, "row", "col"),
        P(None, "col"),
        P(None, "col", "row"),
        P(None, "col"),
    )
    return jax.shard_map(body, mesh=mesh, in_specs=in_specs, out_specs=out_specs, check_vma=False)
```

```python
import functools

import jax
import jax.numpy as jnp
from jax import lax
from jax.experimental import pallas as pl
from jax.experimental.pallas import tpu as pltpu
from jax.sharding import PartitionSpec as P

HEAD_DIM = 64
LAYERS = 2

epsilon = 1e-06
fill_value = -1e30
score_scale = HEAD_DIM ** (-0.5)
low_type = jnp.bfloat16
wide_type = jnp.float32
VMEM = pl.BlockSpec(memory_space=pltpu.VMEM)
SMEM = pl.BlockSpec(memory_space=pltpu.SMEM)
ANY = pl.BlockSpec(memory_space=pl.ANY)
vmem_bytes = 56 * 1024 * 1024


def dot(left, right):
    return lax.dot_general(
        left, right, (((1,), (0,)), ((), ())), preferred_element_type=wide_type
    )


def dot_right(left, right):
    return lax.dot_general(
        left, right, (((1,), (1,)), ((), ())), preferred_element_type=wide_type
    )


def dot_left(left, right):
    return lax.dot_general(
        left, right, (((0,), (0,)), ((), ())), preferred_element_type=wide_type
    )


def piece_copies(meta, refs, offset, tiles, target, sems):
    if len(refs) == 1:
        return [pltpu.make_async_copy(refs[0], target(None, None), sems.at[0])]
    copies = []
    core = meta[4]
    for place in range(3):
        for block in range(2):
            source = refs[place].at[block, pl.ds(offset, tiles)]
            copies.append((source, target(block, meta[place])))
    copies.append((refs[3].at[pl.ds(offset, tiles)], target(core, meta[3])))
    copies.append((refs[4].at[pl.ds(offset, tiles)], target(1 - core, meta[3])))
    return [
        pltpu.make_async_copy(source, place, sems.at[index])
        for index, (source, place) in enumerate(copies)
    ]


def in_copies(meta, refs, offset, weight, sems):
    def target(block, row_block):
        if block is None:
            return weight
        return weight.at[:, pl.ds(row_block * 256, 256), pl.ds(block * 256, 256)]

    return piece_copies(meta, refs, offset, 3, target, sems)


def proj_copies(meta, refs, offset, weight, sems):
    def target(block, row_block):
        if block is None:
            return weight
        return weight.at[pl.ds(block, 1), :, pl.ds(row_block * 256, 256)]

    return piece_copies(meta, refs, offset, 1, target, sems)


def up_copies(meta, refs, offset, weight, sems):
    def target(block, row_block):
        if block is None:
            return weight
        return weight.at[pl.ds(block * 4, 4), pl.ds(row_block * 256, 256), :]

    return piece_copies(meta, refs, offset, 4, target, sems)


def down_copies(meta, refs, offset, weight, sems):
    def target(block, row_block):
        if block is None:
            return weight
        return weight.at[pl.ds(block * 4, 4), :, pl.ds(row_block * 256, 256)]

    return piece_copies(meta, refs, offset, 4, target, sems)


def start_all(copies):
    for copy in copies:
        copy.start()


def wait_all(copies):
    for copy in copies:
        copy.wait()


def standardize(inputs):
    width = inputs.shape[1]
    centre = jnp.sum(inputs, axis=1, keepdims=True) / width
    centred = inputs - centre
    spread = jnp.sum(centred * centred, axis=1, keepdims=True) / width
    rscale = lax.rsqrt(spread + epsilon)
    return centred * rscale, rscale


def mask_rows(meta, rows, slots):
    parts = []
    for seq in range(rows // slots):
        place = lax.broadcasted_iota(jnp.int32, (slots, 1), 0)
        parts.append(jnp.where(place < meta[5 + seq], 1.0, 0.0).astype(wide_type))
    return parts[0] if len(parts) == 1 else jnp.concatenate(parts, axis=0)


def gelu_and_slope(u):
    size = jnp.abs(u) * 0.7071067811865476
    t = 1.0 / (1.0 + 0.3275911 * size)
    bell = jnp.exp(-size * size)
    tail = t * (
        0.254829592
        + t * (-0.284496736 + t * (1.421413741 + t * (-1.453152027 + t * 1.061405429)))
    )
    tail = 0.5 * tail * bell
    share = jnp.where(u >= 0.0, 1.0 - tail, tail)
    return u * share, share + u * bell * 0.3989422804014327


def place_blocks(meta, place, blocks, target):
    width = blocks[0].shape[1]
    for index, block in enumerate(blocks):
        at = pl.multiple_of(meta[place + index] * width, width)
        target[:, pl.ds(at, width)] = block[...]


def key_bias(meta, seq, slots):
    place = lax.broadcasted_iota(jnp.int32, (1, slots), 1)
    return place < meta[5 + seq]


def split_refs(refs, counts):
    out = []
    at = 0
    for count in counts:
        out.append(refs[at : at + count])
        at += count
    return out


def attend_kernel(first, slots, counts, offsets, meta, *refs):
    (base, sums, params, in_refs, proj_refs, outs, scratch) = split_refs(refs, counts)
    gains, shifts, query_shift, value_shift = params
    x_ref, normed_ref, query_ref, key_ref, value_ref, lse_ref, mixed_ref, wide_ref, low_ref = outs
    in_weight, proj_weight, in_sems, proj_sems = scratch
    in_moves = in_copies(meta, in_refs, offsets[0], in_weight, in_sems)
    proj_moves = proj_copies(meta, proj_refs, offsets[1], proj_weight, proj_sems)
    start_all(in_moves)
    start_all(proj_moves)
    rows = x_ref.shape[0]
    if first:
        place_blocks(meta, 5 + rows // slots, base, x_ref)
        current = x_ref[...]
    else:
        own, arrived, bias = sums
        current = base[0][...] + own[...] + arrived[...].astype(wide_type) + bias[...]
        current = current * mask_rows(meta, rows, slots)
        x_ref[...] = current
    standard, _ = standardize(current)
    normed = (standard * gains[...] + shifts[...]).astype(low_type)
    normed_ref[...] = normed
    wait_all(in_moves)
    query_ref[...] = (dot(normed, in_weight[0]) + query_shift[...]).astype(low_type)
    key_ref[...] = dot(normed, in_weight[1]).astype(low_type)
    value_ref[...] = (dot(normed, in_weight[2]) + value_shift[...]).astype(low_type)
    heads = query_ref.shape[1] // HEAD_DIM
    for seq in range(rows // slots):
        span = slice(seq * slots, (seq + 1) * slots)
        valid = key_bias(meta, seq, slots)
        for head in range(heads):
            lanes = slice(head * HEAD_DIM, (head + 1) * HEAD_DIM)
            scores = dot_right(query_ref[span, lanes], key_ref[span, lanes]) * score_scale
            scores = jnp.where(valid, scores, fill_value)
            maximum = jnp.max(scores, axis=1, keepdims=True)
            exponent = jnp.exp(scores - maximum)
            mass = jnp.sum(exponent, axis=1, keepdims=True)
            attention = (exponent * (1.0 / mass)).astype(low_type)
            mixed_ref[span, lanes] = dot(attention, value_ref[span, lanes]).astype(low_type)
            lse_ref[span, head : head + 1] = maximum + jnp.log(mass)
    wait_all(proj_moves)
    block = proj_weight.shape[1]
    total = dot(mixed_ref[:, :block], proj_weight[0])
    for index in range(1, proj_weight.shape[0]):
        total = total + dot(
            mixed_ref[:, index * block : (index + 1) * block], proj_weight[index]
        )
    wide_ref[...] = total
    low_ref[...] = total.astype(low_type)


def feed_kernel(counts, offsets, meta, *refs):
    (sums, params, up_refs, down_refs, outs, scratch) = split_refs(refs, counts)
    base, own, arrived, bias = sums
    gains, shifts, up_shift = params
    middle_ref, normed_ref, hidden_ref, slope_ref, wide_ref, low_ref = outs
    up_weight, down_weight, up_sems, down_sems = scratch
    up_moves = up_copies(meta, up_refs, offsets[0], up_weight, up_sems)
    down_moves = down_copies(meta, down_refs, offsets[1], down_weight, down_sems)
    start_all(up_moves)
    start_all(down_moves)
    middle = base[...] + own[...] + arrived[...].astype(wide_type) + bias[...]
    middle_ref[...] = middle
    standard, _ = standardize(middle)
    normed = (standard * gains[...] + shifts[...]).astype(low_type)
    normed_ref[...] = normed
    wait_all(up_moves)
    width = up_weight.shape[2]
    for index in range(up_weight.shape[0]):
        lanes = slice(index * width, (index + 1) * width)
        pre = dot(normed_ref[...], up_weight[index]) + up_shift[:, lanes]
        hidden, slope = gelu_and_slope(pre)
        hidden_ref[:, lanes] = hidden.astype(low_type)
        slope_ref[:, lanes] = slope.astype(low_type)
    wait_all(down_moves)
    rows = down_weight.shape[0] * down_weight.shape[1]
    total = dot(hidden_ref[...], down_weight[...].reshape(rows, down_weight.shape[2]))
    wide_ref[...] = total
    low_ref[...] = total.astype(low_type)


def norm_back(grad_rows, inputs, gains):
    standard, rscale = standardize(inputs)
    width = inputs.shape[1]
    scaled = grad_rows * gains
    first = jnp.sum(scaled, axis=1, keepdims=True) / width
    second = jnp.sum(scaled * standard, axis=1, keepdims=True) / width
    grad_input = rscale * (scaled - first - standard * second)
    return (
        grad_input,
        jnp.sum(grad_rows * standard, axis=0, keepdims=True),
        jnp.sum(grad_rows, axis=0, keepdims=True),
    )


def last_kernel(slots, meta, factor, base, own, arrived, bias, *refs):
    seeds, (current_ref, grad_ref) = refs[:-2], refs[-2:]
    rows = base.shape[0]
    mask = mask_rows(meta, rows, slots)
    place_blocks(meta, 5 + rows // slots, seeds, grad_ref)
    current = base[...] + own[...] + arrived[...].astype(wide_type) + bias[...]
    current = current * mask
    current_ref[...] = current
    grad_ref[...] = grad_ref[...] + factor[0] * current


def pull_kernel(inputs, gains, base, own, arrived, grad_ref, gain_ref, shift_ref):
    summed = own[...] + arrived[...].astype(wide_type)
    grad, gain, shift = norm_back(summed, inputs[...], gains[...])
    grad_ref[...] = base[...] + grad
    gain_ref[...] = gain
    shift_ref[...] = shift


def feed_back_kernel(slots, counts, offsets, meta, *refs):
    (sums, up_refs, down_refs, outs, scratch) = split_refs(refs, counts)
    grad, slope_ref = sums
    masked_ref, masked_low_ref, pre_ref, down_bias_ref, up_bias_ref, wide_ref, low_ref = outs
    up_weight, down_weight, up_sems, down_sems = scratch
    up_moves = up_copies(meta, up_refs, offsets[0], up_weight, up_sems)
    down_moves = down_copies(meta, down_refs, offsets[1], down_weight, down_sems)
    start_all(down_moves)
    start_all(up_moves)
    masked = grad[...] * mask_rows(meta, grad.shape[0], slots)
    masked_ref[...] = masked
    masked_low = masked.astype(low_type)
    masked_low_ref[...] = masked_low
    down_bias_ref[...] = jnp.sum(masked_low.astype(wide_type), axis=0, keepdims=True)
    wait_all(down_moves)
    width = up_weight.shape[2]
    for index in range(up_weight.shape[0]):
        lanes = slice(index * width, (index + 1) * width)
        hidden = dot_right(masked_low_ref[...], down_weight[index])
        pre = (hidden * slope_ref[:, lanes].astype(wide_type)).astype(low_type)
        pre_ref[:, lanes] = pre
        up_bias_ref[:, lanes] = jnp.sum(pre.astype(wide_type), axis=0, keepdims=True)
    wait_all(up_moves)
    total = dot_right(pre_ref[:, :width], up_weight[0])
    for index in range(1, up_weight.shape[0]):
        lanes = slice(index * width, (index + 1) * width)
        total = total + dot_right(pre_ref[:, lanes], up_weight[index])
    wide_ref[...] = total
    low_ref[...] = total.astype(low_type)


def attend_back_kernel(slots, counts, offsets, meta, *refs):
    (sums, params, saved, in_refs, proj_refs, outs, scratch) = split_refs(refs, counts)
    own, arrived, middle, masked = sums
    (gains,) = params
    query_ref, key_ref, value_ref, lse_ref = saved
    (
        grad_ref,
        low_grad_ref,
        gain_ref,
        shift_ref,
        proj_bias_ref,
        triple_ref,
        in_bias_ref,
        wide_ref,
        low_ref,
    ) = outs
    in_weight, proj_weight, mixed_grad, in_sems, proj_sems = scratch
    in_moves = in_copies(meta, in_refs, offsets[0], in_weight, in_sems)
    proj_moves = proj_copies(meta, proj_refs, offsets[1], proj_weight, proj_sems)
    start_all(proj_moves)
    start_all(in_moves)
    summed = own[...] + arrived[...].astype(wide_type)
    grad, gain, shift = norm_back(summed, middle[...], gains[...])
    grad = masked[...] + grad
    grad_ref[...] = grad
    gain_ref[...] = gain
    shift_ref[...] = shift
    grad_low = grad.astype(low_type)
    low_grad_ref[...] = grad_low
    proj_bias_ref[...] = jnp.sum(grad_low.astype(wide_type), axis=0, keepdims=True)
    wait_all(proj_moves)
    block = proj_weight.shape[1]
    for index in range(proj_weight.shape[0]):
        mixed_grad[:, index * block : (index + 1) * block] = dot_right(
            low_grad_ref[...], proj_weight[index]
        ).astype(low_type)
    heads = query_ref.shape[1] // HEAD_DIM
    rows = query_ref.shape[0]
    for seq in range(rows // slots):
        span = slice(seq * slots, (seq + 1) * slots)
        valid = key_bias(meta, seq, slots)
        for head in range(heads):
            lanes = slice(head * HEAD_DIM, (head + 1) * HEAD_DIM)
            queries = query_ref[span, lanes]
            keys = key_ref[span, lanes]
            outer = mixed_grad[span, lanes]
            scores = dot_right(queries, keys) * score_scale
            scores = jnp.where(valid, scores, fill_value)
            chance = jnp.exp(scores - lse_ref[span, head : head + 1])
            grad_chance = dot_right(outer, value_ref[span, lanes])
            inner = jnp.sum(grad_chance * chance, axis=1, keepdims=True)
            grad_scores = (chance * (grad_chance - inner)).astype(low_type)
            triple_ref[2, span, lanes] = dot_left(chance.astype(low_type), outer).astype(low_type)
            triple_ref[0, span, lanes] = (dot(grad_scores, keys) * score_scale).astype(low_type)
            triple_ref[1, span, lanes] = (dot_left(grad_scores, queries) * score_scale).astype(
                low_type
            )
    in_bias_ref[0:1, :] = jnp.sum(triple_ref[0].astype(wide_type), axis=0, keepdims=True)
    in_bias_ref[1:2, :] = jnp.sum(triple_ref[2].astype(wide_type), axis=0, keepdims=True)
    wait_all(in_moves)
    total = dot_right(triple_ref[0], in_weight[0])
    total = total + dot_right(triple_ref[1], in_weight[1])
    total = total + dot_right(triple_ref[2], in_weight[2])
    wide_ref[...] = total
    low_ref[...] = total.astype(low_type)


def feed_weight_kernel(meta, normed, pre, hidden, masked_low, *outs):
    def write(place, block, row_block):
        columns = pl.ds(pl.multiple_of(row_block * 256, 256), 256)
        for tile in range(4):
            lanes = pl.ds(pl.multiple_of(block * 1024 + tile * 256, 256), 256)
            place[tile] = dot_left(normed[:, columns], pre[:, lanes]).astype(low_type)
            place[4 + tile] = dot_left(hidden[:, lanes], masked_low[:, columns]).astype(low_type)

    write_pieces(meta, outs, write)


def attend_weight_kernel(meta, normed, triple, mixed, grad_low, *outs):
    def write(place, block, row_block):
        columns = pl.ds(pl.multiple_of(row_block * 256, 256), 256)
        lanes = pl.ds(pl.multiple_of(block * 256, 256), 256)
        for kind in range(3):
            place[kind] = dot_left(normed[:, columns], triple[kind, :, lanes]).astype(low_type)
        place[3] = dot_left(mixed[:, lanes], grad_low[:, columns]).astype(low_type)

    write_pieces(meta, outs, write)


def write_pieces(meta, outs, write):
    core = meta[4]
    for place in range(3):
        for block in range(2):
            write(outs[place].at[block], block, meta[place])
    write(outs[3], core, meta[3])
    write(outs[4], 1 - core, meta[3])


def near_add_kernel(meta, near, arrived, moved, out):
    for block in range(2):
        extra = jnp.where(meta[4] == block, moved[...].astype(wide_type), 0.0)
        total = near[block].astype(wide_type) + arrived[block].astype(wide_type) + extra
        out[block] = total.astype(low_type)


def finish_feed_kernel(meta, *refs):
    halves, (up, down) = refs[:-2], refs[-2:]
    first = meta[4] == 0
    for layer in range(len(halves) // 2):
        part, other = halves[2 * layer], halves[2 * layer + 1]
        for tile in range(4):
            mine, its = part[tile].astype(wide_type), other[tile].astype(wide_type)
            up[layer, :, tile * 256 : (tile + 1) * 256] = jnp.where(first, mine, its)
            down[layer, tile * 256 : (tile + 1) * 256, :] = jnp.where(first, its, mine)


def finish_attend_kernel(meta, *refs):
    halves, (thirds, square) = refs[:-2], refs[-2:]
    first = meta[4] == 0
    for layer in range(len(halves) // 2):
        part, other = halves[2 * layer], halves[2 * layer + 1]
        mine, its = part[...].astype(wide_type), other[...].astype(wide_type)
        thirds[layer, 0] = jnp.where(first, mine[0], its[0])
        thirds[layer, 1] = jnp.where(first, mine[1], its[1])
        thirds[layer, 2] = jnp.where(first, its[0], mine[0])
        square[layer] = jnp.where(first, its[1], mine[1])


def flip_col(value):
    count = lax.axis_size("col")
    return lax.ppermute(value, "col", [(i, count - 1 - i) for i in range(count)])


def swap_core(value):
    count = lax.axis_size("dp")
    return lax.ppermute(value, "dp", [(i, count - 1 - i) for i in range(count)])


def group_shift(value, step):
    count = lax.axis_size("col")
    half = count // 2
    pairs = [(i, i // half * half + (i % half + step) % half) for i in range(count)]
    return lax.ppermute(value, "col", pairs)


def cross_row(value, first_step, second_step):
    rows = lax.axis_size("row")
    cols = lax.axis_size("col")
    pairs = []
    for core, step in ((0, first_step), (1, second_step)):
        for row in range(rows):
            for col in range(cols):
                source = (core * rows + row) * cols + col
                pairs.append((source, (core * rows + (row ^ step)) * cols + col))
    return lax.ppermute(value, ("dp", "row", "col"), pairs)


def group_total(wide, low):
    arrived = group_shift(low, 1)
    for step in range(2, lax.axis_size("col") // 2):
        wide = wide + group_shift(low, step).astype(wide_type)
    return wide, arrived


def butterfly_sum(value, axes):
    for axis in axes:
        count = lax.axis_size(axis)
        step = 1
        while step < count:
            value = value + lax.ppermute(value, axis, [(i, i ^ step) for i in range(count)])
            step *= 2
    return value


def after(value, *events):
    return lax.optimization_barrier((value,) + events)[0]


def order_blocks(pair):
    count = lax.axis_size("col")
    half = count // 2
    col_index = lax.axis_index("col")
    base = col_index // half * half
    wanted = lax.broadcasted_iota(jnp.int32, (count,) + pair.shape[1:], 0)
    whole = jnp.zeros((count,) + pair.shape[1:], pair.dtype)
    for step in range(half):
        piece = pair if step == 0 else group_shift(pair, step)
        source = base + (col_index - base + half - step) % half
        whole = jnp.where(wanted == source, piece[0][None], whole)
        whole = jnp.where(wanted == count - 1 - source, piece[1][None], whole)
    return whole


def add(left, right):
    return (left.astype(wide_type) + right.astype(wide_type)).astype(low_type)


def gather_near(own):
    return cross_row(own, 1, 2)


def gather_far(near, first_core):
    return cross_row(jnp.where(first_core, near[0], near[1]), 2, 1)


def gather_pieces(own, near, far):
    return (own, near, swap_core(near), far, swap_core(far))


def flip_tiles(shard, first_core):
    half = shard.shape[0] // 2
    got = flip_col(jnp.where(first_core, shard[:half], shard[half:]))
    return got, swap_core(got)


def join_tiles(shard, got, other, first_core):
    halves = jnp.where(first_core, jnp.stack([got, other]), jnp.stack([other, got]))
    return jnp.stack([shard, halves.reshape(shard.shape)])


def scatter_first(pieces):
    own, near, near_other, far, far_other = pieces
    return own, near, swap_core(near_other), add(far, swap_core(far_other))


def scatter_third(own, arrived, first_core):
    own = add(own, arrived)
    half = own.shape[1] // 2
    lower, upper = own[:, :half], own[:, half:]
    arrived = swap_core(jnp.where(first_core, upper, lower))
    return add(jnp.where(first_core, lower, upper), arrived)


def body(
    states,
    teacher,
    cotangent,
    lengths,
    norm_gain,
    norm_bias,
    in_weight,
    in_bias,
    proj_weight,
    proj_bias,
    up_weight,
    up_bias,
    down_weight,
    down_bias,
):
    col_count = lax.axis_size("col")
    row_count = lax.axis_size("row")
    core_count = lax.axis_size("dp")
    half_group = col_count // 2
    col_index = lax.axis_index("col")
    row_index = lax.axis_index("row")
    core_index = lax.axis_index("dp")
    group_index = col_index // half_group
    first_core = core_index == 0
    token_rows, width = states.shape
    model_width = width * col_count
    seqs = lengths.shape[0] // 2
    rows = token_rows // 2
    slots = rows // seqs
    hidden_width = up_bias.shape[1]
    tiled = row_count == 4 and width == 256 and hidden_width == 1024 and model_width == 1024
    row_width = model_width // row_count
    heads_width = 2 * width
    feed_width = 2 * hidden_width
    in_thirds = jnp.transpose(in_weight, (0, 2, 1, 3))

    def own_half(value):
        return lax.dynamic_slice_in_dim(value, group_index * rows, rows, 0)

    def other_half(value):
        return lax.dynamic_slice_in_dim(value, (1 - group_index) * rows, rows, 0)

    block_places = []
    for step in range(half_group):
        base = group_index * half_group
        source = base + (col_index - base + half_group - step) % half_group
        block_places = block_places + [source, col_count - 1 - source]

    def join_rows(value, received):
        own = lax.dynamic_slice_in_dim(value, col_index * width, width, 1)
        lower = jnp.where(group_index == 0, own, received)
        upper = jnp.where(group_index == 0, received, own)
        return jnp.concatenate([lower, upper])

    def share_rows(value, kind):
        other = lax.dynamic_slice_in_dim(value, (col_count - 1 - col_index) * width, width, 1)
        return join_rows(value, flip_col(other.astype(kind)).astype(wide_type))

    own_lengths = lax.dynamic_slice_in_dim(lengths, group_index * seqs, seqs, 0)
    meta = jnp.concatenate(
        [
            jnp.stack(
                [
                    row_index,
                    row_index ^ (1 + core_index),
                    row_index ^ (2 - core_index),
                    row_index ^ 3,
                    core_index,
                ]
            ),
            own_lengths,
            jnp.stack(block_places),
        ]
    ).astype(jnp.int32)

    in_full, proj_full, up_full, down_full = ([None] * LAYERS for kind in range(4))
    feature_pack = jnp.concatenate(
        [norm_gain.reshape(-1, width), norm_bias.reshape(-1, width), proj_bias, down_bias]
    )
    hidden_pack = jnp.concatenate([in_bias.reshape(-1, width), up_bias.reshape(-1, width)])
    feature_rows = feature_pack.shape[0]
    small = jnp.concatenate([feature_pack, hidden_pack])
    states_own, states_other = own_half(states), other_half(states)
    gate = []

    def gated(value):
        return after(value, *gate) if gate else value

    def all_shifts(value):
        return [group_shift(value, step) for step in range(1, half_group)]

    def all_blocks(own, own_shifts, flipped, flipped_shifts):
        blocks = [own, flipped]
        for pair in zip(own_shifts, flipped_shifts):
            blocks = blocks + list(pair)
        return blocks

    total_steps = [
        (axis, 2**bit)
        for axis in ("dp", "row")
        for bit in range(lax.axis_size(axis).bit_length() - 1)
    ]
    token_total = jnp.sum(lengths)

    def count_step(value, axis, step):
        size = lax.axis_size(axis)
        return value + lax.ppermute(value, axis, [(i, i ^ step) for i in range(size)])

    if tiled:
        count = 6
        shards, flips, owns, nears, near_others, fars, far_others = (
            [None] * count for kind in range(7)
        )

        def up_tiles(weight):
            return jnp.transpose(weight.reshape(256, 4, 256), (1, 0, 2))

        def flip(place):
            layer = place // 3
            if place % 3 == 0:
                square = gated(proj_weight[layer])[None]
                shards[place] = jnp.concatenate([gated(in_thirds[layer]), square])
            elif place % 3 == 1:
                shards[place] = up_tiles(gated(up_weight[layer]))
            else:
                shards[place] = gated(down_weight[layer]).reshape(4, 256, 256)
            flips[place] = flip_tiles(shards[place], first_core)
            return flips[place][0]

        def near(place):
            owns[place] = join_tiles(shards[place], *flips[place], first_core)
            nears[place] = cross_row(gated(owns[place]), 1, 2)
            return nears[place]

        def near_swap(place):
            near_others[place] = swap_core(gated(nears[place]))
            return near_others[place]

        def far(place):
            value = gated(nears[place])
            fars[place] = cross_row(jnp.where(first_core, value[0], value[1]), 2, 1)
            return fars[place]

        def far_swap(place):
            far_others[place] = swap_core(gated(fars[place]))
            return far_others[place]

        def pieces(place):
            return (
                owns[place],
                nears[place],
                near_others[place],
                fars[place],
                far_others[place],
            )

        gate = [flip(0)]
        states_flipped = flip_col(gated(states_other))
        shifts_own = all_shifts(gated(states_own))
        small_flipped = flip_col(gated(small))
        gate = [near(0), states_flipped, small_flipped, *shifts_own]
        small_pair = jnp.stack([small, gated(small_flipped)])
        feature_all = order_blocks(small_pair[:, :feature_rows])
        shifts_flipped = all_shifts(gated(states_flipped))
        token_total = count_step(gated(token_total), *total_steps[0])
        gate = [far(0), flip(1), near_swap(0), token_total, feature_all, *shifts_flipped]
        states_blocks = all_blocks(states_own, shifts_own, states_flipped, shifts_flipped)
        token_total = count_step(gated(token_total), *total_steps[1])
        first_slot = [near(1), flip(2), token_total]
        far_swap(0)
        in_full[0], proj_full[0] = (pieces(0), 0), (pieces(0), 3)
    else:

        def both_blocks(shard):
            own = lax.all_gather(shard, "row", axis=0, tiled=False)
            return jnp.stack([own, flip_col(own)])

        for layer in range(LAYERS):
            whole = jnp.transpose(both_blocks(in_thirds[layer]), (2, 1, 3, 0, 4))
            in_full[layer] = ((whole.reshape(3, model_width, heads_width),), 0)
            whole = jnp.transpose(both_blocks(proj_weight[layer]), (0, 2, 1, 3))
            proj_full[layer] = ((whole.reshape(2, width, model_width),), 0)
            whole = both_blocks(up_weight[layer]).reshape(2, model_width, -1, 256)
            whole = jnp.transpose(whole, (0, 2, 1, 3))
            up_full[layer] = ((whole.reshape(-1, model_width, 256),), 0)
            whole = jnp.transpose(both_blocks(down_weight[layer]), (0, 2, 1, 3))
            down_full[layer] = ((whole.reshape(-1, 256, model_width),), 0)
        states_flipped = flip_col(states_other)
        small_flipped = flip_col(small)
        states_blocks = all_blocks(
            states_own, all_shifts(states_own), states_flipped, all_shifts(states_flipped)
        )
        for step in total_steps:
            token_total = count_step(token_total, *step)
        small_pair = jnp.stack([small, small_flipped])
        feature_all = order_blocks(small_pair[:, :feature_rows])

    feature_all = jnp.transpose(feature_all, (1, 0, 2)).reshape(feature_rows, model_width)
    gains = feature_all[: 2 * LAYERS].reshape(LAYERS, 2, 1, model_width)
    shifts = feature_all[2 * LAYERS : 4 * LAYERS].reshape(LAYERS, 2, 1, model_width)
    proj_shift = feature_all[4 * LAYERS : 5 * LAYERS].reshape(LAYERS, 1, model_width)
    down_shift = feature_all[5 * LAYERS :].reshape(LAYERS, 1, model_width)
    hidden_pair = small_pair[:, feature_rows:]
    in_shift = hidden_pair[:, : 2 * LAYERS].reshape(2, LAYERS, 2, width)
    in_shift = jnp.transpose(in_shift, (1, 2, 0, 3)).reshape(LAYERS, 2, 1, heads_width)
    up_shift = hidden_pair[:, 2 * LAYERS :].reshape(2, LAYERS, hidden_width)
    up_shift = jnp.transpose(up_shift, (1, 0, 2)).reshape(LAYERS, 1, feed_width)


    def shape(*dims, kind=wide_type):
        return jax.ShapeDtypeStruct(dims, kind)

    def call(kernel, cost, operands, specs, outs, scratch=()):
        return pl.pallas_call(
            kernel,
            out_shape=outs,
            in_specs=specs,
            out_specs=[VMEM] * len(outs),
            scratch_shapes=list(scratch),
            compiler_params=pltpu.CompilerParams(vmem_limit_bytes=vmem_bytes),
            cost_estimate=pl.CostEstimate(
                flops=int(cost * 9.2e9), bytes_accessed=1024 * 1024, transcendentals=0
            ),
        )(*operands)

    wide_rows = shape(rows, model_width)
    low_rows = shape(rows, model_width, kind=low_type)
    low_heads = shape(rows, heads_width, kind=low_type)
    heads = heads_width // HEAD_DIM
    feed_tiles = feed_width // 256
    attend_scratch = [
        pltpu.VMEM((3, model_width, heads_width), low_type),
        pltpu.VMEM((2, width, model_width), low_type),
    ]
    feed_scratch = [
        pltpu.VMEM((feed_tiles, model_width, 256), low_type),
        pltpu.VMEM((feed_tiles, 256, model_width), low_type),
    ]
    sems = [pltpu.SemaphoreType.DMA((8,)), pltpu.SemaphoreType.DMA((8,))]

    def attend(layer, base, sums):
        first = len(sums) == 0
        params = [gains[layer, 0], shifts[layer, 0], in_shift[layer, 0], in_shift[layer, 1]]
        in_refs, in_offset = in_full[layer]
        proj_refs, proj_offset = proj_full[layer]
        counts = (len(base), len(sums), 4, len(in_refs), len(proj_refs), 9, 4)
        operands = [meta, *base, *sums, *params, *in_refs, *proj_refs]
        specs = [SMEM] + [VMEM] * (4 + len(base) + len(sums)) + [ANY] * (len(in_refs) + len(proj_refs))
        kernel = functools.partial(attend_kernel, first, slots, counts, (in_offset, proj_offset))
        outs = [
            wide_rows,
            low_rows,
            low_heads,
            low_heads,
            low_heads,
            shape(rows, heads),
            low_heads,
            wide_rows,
            low_rows,
        ]
        return call(kernel, 10.5, operands, specs, outs, attend_scratch + sems)

    def feed(layer, base, sums):
        params = [gains[layer, 1], shifts[layer, 1], up_shift[layer]]
        up_refs, up_offset = up_full[layer]
        down_refs, down_offset = down_full[layer]
        counts = (4, 3, len(up_refs), len(down_refs), 6, 4)
        operands = [meta, base, *sums, *params, *up_refs, *down_refs]
        specs = [SMEM] + [VMEM] * 7 + [ANY] * (len(up_refs) + len(down_refs))
        kernel = functools.partial(feed_kernel, counts, (up_offset, down_offset))
        low_feed = shape(rows, feed_width, kind=low_type)
        outs = [wide_rows, low_rows, low_feed, low_feed, wide_rows, low_rows]
        return call(kernel, 12.0, operands, specs, outs, feed_scratch + sems)

    def feed_back(layer, grad, slope):
        up_refs, up_offset = up_full[layer]
        down_refs, down_offset = down_full[layer]
        counts = (2, len(up_refs), len(down_refs), 7, 4)
        operands = [meta, grad, slope, *up_refs, *down_refs]
        specs = [SMEM] + [VMEM] * 2 + [ANY] * (len(up_refs) + len(down_refs))
        kernel = functools.partial(feed_back_kernel, slots, counts, (up_offset, down_offset))
        outs = [
            wide_rows,
            low_rows,
            shape(rows, feed_width, kind=low_type),
            shape(1, model_width),
            shape(1, feed_width),
            wide_rows,
            low_rows,
        ]
        return call(kernel, 10.0, operands, specs, outs, feed_scratch + sems)

    def attend_back(layer, sums, middle, masked, saved):
        in_refs, in_offset = in_full[layer]
        proj_refs, proj_offset = proj_full[layer]
        counts = (4, 1, 4, len(in_refs), len(proj_refs), 9, 5)
        operands = [meta, *sums, middle, masked, gains[layer, 1], *saved, *in_refs, *proj_refs]
        specs = [SMEM] + [VMEM] * 9 + [ANY] * (len(in_refs) + len(proj_refs))
        kernel = functools.partial(attend_back_kernel, slots, counts, (in_offset, proj_offset))
        outs = [
            wide_rows,
            low_rows,
            shape(1, model_width),
            shape(1, model_width),
            shape(1, model_width),
            shape(3, rows, heads_width, kind=low_type),
            shape(2, heads_width),
            wide_rows,
            low_rows,
        ]
        scratch = attend_scratch + [pltpu.VMEM((rows, heads_width), low_type)] + sems
        return call(kernel, 12.0, operands, specs, outs, scratch)

    def weight_tiles(kernel, tiles, cost, *operands):
        outs = [shape(2, tiles, 256, 256, kind=low_type)] * 3
        outs = outs + [shape(tiles, 256, 256, kind=low_type)] * 2
        specs = [SMEM] + [VMEM] * len(operands)
        return call(kernel, cost, (meta,) + operands, specs, outs)

    positions = jnp.arange(slots, dtype=jnp.int32)
    all_mask = (positions[None, :] < lengths[:, None]).reshape(token_rows, 1).astype(wide_type)
    teacher_wide = teacher.astype(wide_type)

    def near_add(near, arrived, moved):
        tiles = moved.shape[0]
        both = pl.BlockSpec((2, 4, 256, 256), lambda index: (0, index, 0, 0))
        single = pl.BlockSpec((4, 256, 256), lambda index: (index, 0, 0))
        return pl.pallas_call(
            near_add_kernel,
            grid=(tiles // 4,),
            out_shape=shape(2, tiles, 256, 256, kind=low_type),
            in_specs=[SMEM, both, both, single],
            out_specs=both,
            cost_estimate=pl.CostEstimate(
                flops=int(tiles * 2.4e9), bytes_accessed=1024 * 1024, transcendentals=0
            ),
        )(meta, near, arrived, moved)

    def finish(kernel, cost, outs, parts):
        halves = []
        for part in parts:
            halves = halves + [part, swap_core(part)]
        return call(kernel, cost, (meta, *halves), [SMEM] + [VMEM] * len(halves), outs)

    saved = []
    base, sums = states_blocks, ()
    for layer in range(LAYERS):
        if layer > 0:
            sums = (*sums, down_shift[layer - 1])
        current, normed_one, queries, keys, values, lse, mixed, wide, low = attend(
            layer, base, sums
        )
        event = wide
        if layer == 0:
            if tiled:
                gate = [wide, *first_slot]
                token_total = count_step(gated(token_total), *total_steps[2])
                second_slot = [far(1), near(2), flip(3), near_swap(1), token_total]
            wide, arrived = group_total(wide, low)
            token_total = token_total.astype(wide_type)
            factor = 2.0 * token_rows * core_count * row_count / token_total
            seed_share = cotangent - factor * all_mask * teacher_wide
            seed_own, seed_other = own_half(seed_share), other_half(seed_share)
            if tiled:
                gate = [*second_slot, arrived]
                second_slot = [far(2), near(3), flip(4), far_swap(1), near_swap(2)]
                gate = [fars[2]]
                far_swap(2)
                up_full[0], down_full[0] = (pieces(1), 0), (pieces(2), 0)
        else:
            if tiled:
                low = after(low, seed_flipped)
                gate = [event, *second_slot, seed_flipped]
                second_slot = [far(5), far_swap(4), near_swap(5)]
                gate = [fars[5]]
                far_swap(5)
                up_full[1], down_full[1] = (pieces(4), 0), (pieces(5), 0)
            wide, arrived = group_total(wide, low)
            gate = [arrived]
            shifts_own, shifts_flipped = all_shifts(gated(seed_own)), all_shifts(gated(seed_flipped))
            seed_blocks = all_blocks(seed_own, shifts_own, seed_flipped, shifts_flipped)
        middle, normed_two, hidden, slope, wide, low = feed(
            layer, current, (wide, arrived, proj_shift[layer])
        )
        if layer == 1:
            low = after(low, *seed_blocks)
        event = wide
        wide, arrived = group_total(wide, low)
        if layer == 0:
            gate = [event, *second_slot] if tiled else []
            if tiled:
                second_slot = [far(3), near(4), flip(5), near_swap(3)]
                gate = [fars[3]]
                far_swap(3)
                in_full[1], proj_full[1] = (pieces(3), 0), (pieces(3), 3)
                gate = [arrived, *second_slot]
                second_slot = [near(5), far(4), near_swap(4)]
            seed_flipped = flip_col(gated(seed_other))
        base, sums = [middle], (wide, arrived)
        saved.append(
            (current, normed_one, queries, keys, values, lse, mixed, middle, normed_two, hidden, slope)
        )
    final, grad = call(
        functools.partial(last_kernel, slots),
        4.3,
        (meta, factor.reshape(1), *base, *sums, down_shift[LAYERS - 1], *seed_blocks),
        [SMEM, SMEM] + [VMEM] * (4 + len(seed_blocks)),
        [wide_rows, wide_rows],
    )
    output_other = lax.dynamic_slice_in_dim(
        final, (col_count - 1 - col_index) * width, width, 1
    )
    output_halves = [flip_col(output_other[: rows // 2])]

    feature_grads = {}
    hidden_grads = {}
    in_grads, proj_grads, up_grads, down_grads = ([None] * LAYERS for kind in range(4))

    way = []
    for layer in reversed(range(LAYERS)):
        current, normed_one, queries, keys, values, lse, mixed, middle, normed_two, hidden, slope = (
            saved[layer]
        )
        masked, masked_low, pre, down_bias_part, up_bias_part, wide, low = feed_back(
            layer, grad, slope
        )
        if tiled:
            if layer == LAYERS - 1:
                gate = [low, output_halves[0]]
            else:
                gate = [low, far_moved, near_moved]
        wide, arrived = group_total(wide, gated(low))
        if tiled:
            tiles = weight_tiles(
                feed_weight_kernel, 8, 9.0, normed_two, gated(pre), hidden, masked_low
            )
            way.append(scatter_first(tiles))
            gate = [arrived, *tiles, *way[-1]]
            if layer < LAYERS - 1:
                own, near_part, near_arrived, far_part = way[-2]
                near_sent = near_add(near_part, near_arrived, far_moved)
                part = scatter_third(way[-3][0], near_moved, first_core)
                gate = gate + [near_sent, part]
                near_moved = cross_row(near_sent, 1, 2)
                flip_moved = flip_col(after(part[1], *gate))
            arrived = gated(arrived)
            far_moved = cross_row(gated(way[-1][3]), 2, 1)
        (
            grad,
            grad_low,
            gain_two,
            shift_two,
            proj_bias_part,
            triple,
            in_bias_part,
            wide,
            low,
        ) = attend_back(layer, (wide, arrived), middle, masked, (queries, keys, values, lse))
        if layer == LAYERS - 1:
            output_halves.append(flip_col(gated(output_other[rows // 2 :])))
        if tiled:
            gate = [low, far_moved] + (output_halves[1:] if layer == LAYERS - 1 else [])
        wide, arrived = group_total(wide, gated(low))
        if tiled:
            own, near_part, near_arrived, far_part = way[-1]
            near_sent = near_add(near_part, near_arrived, far_moved)
            if layer < LAYERS - 1:
                gate = [*gate, near_sent]
            tiles = weight_tiles(
                attend_weight_kernel, 4, 5.5, normed_one, gated(triple), mixed, grad_low
            )
            way.append(scatter_first(tiles))
            gate = [arrived, *tiles, *way[-1], near_sent]
            if layer < LAYERS - 1:
                feed_parts = [add(part[0], flip_moved)]
                part = scatter_third(way[-3][0], near_moved, first_core)
                gate = gate + [part, *feed_parts]
                flip_moved = flip_col(after(part[1], *gate))
            near_moved = cross_row(near_sent, 1, 2)
            arrived = gated(arrived)
            far_moved = cross_row(gated(way[-1][3]), 2, 1)
        else:

            def product(spec, left, right):
                return jnp.einsum(spec, left, right, preferred_element_type=wide_type)

            def own_block(blocks):
                part = lax.psum_scatter(
                    blocks.astype(low_type), "row", scatter_dimension=1, tiled=False
                )
                mine = add(part[0], flip_col(part[1]))
                return mine.astype(wide_type) + swap_core(mine).astype(wide_type)

            def by_row(value):
                return value.reshape(rows, row_count, row_width)

            def by_block(value):
                return value.reshape(value.shape[:-1] + (2, -1))

            in_grads[layer] = own_block(
                product("trd,ptbe->brpde", by_row(normed_one), by_block(triple))
            )
            proj_grads[layer] = own_block(
                product("tbe,trd->bred", by_block(mixed), by_row(grad_low))
            )
            up_grads[layer] = own_block(product("trd,tbe->brde", by_row(normed_two), by_block(pre)))
            down_grads[layer] = own_block(
                product("tbe,trd->bred", by_block(hidden), by_row(masked_low))
            )
        grad, gain_one, shift_one = call(
            pull_kernel,
            4.3,
            (current, gains[layer, 0], grad, wide, arrived),
            [VMEM] * 5,
            [wide_rows, shape(1, model_width), shape(1, model_width)],
        )
        feature_grads[layer] = (
            gain_one,
            gain_two,
            shift_one,
            shift_two,
            proj_bias_part,
            down_bias_part,
        )
        hidden_grads[layer] = jnp.concatenate(
            [
                jnp.transpose(in_bias_part.reshape(2, 2, width), (1, 0, 2)),
                up_bias_part.reshape(2, -1, width),
            ],
            axis=1,
        )

    if tiled:
        gate = [grad, far_moved]
        input_share = share_rows(gated(grad), low_type)
        own, near_part, near_arrived, far_part = way[-1]
        near_sent = near_add(near_part, near_arrived, far_moved)
        attend_parts = [add(part[0], flip_moved)]
        part = scatter_third(way[-2][0], near_moved, first_core)
        last_moved = cross_row(after(near_sent, part), 1, 2)
        feed_parts.append(add(part[0], flip_col(part[1])))
        part = scatter_third(way[-1][0], last_moved, first_core)
        gate = [part]
        attend_parts.append(add(part[0], flip_col(part[1])))
        up_grad, down_grad = finish(
            finish_feed_kernel,
            3.0,
            [shape(LAYERS, 256, 1024), shape(LAYERS, 1024, 256)],
            feed_parts[::-1],
        )
        in_grad, proj_grad = finish(
            finish_attend_kernel,
            2.0,
            [shape(LAYERS, 3, 256, 256), shape(LAYERS, 256, 256)],
            attend_parts[::-1],
        )
    else:
        input_share = share_rows(grad, low_type)
        up_grad, down_grad = jnp.stack(up_grads), jnp.stack(down_grads)
        in_grad, proj_grad = jnp.stack(in_grads), jnp.stack(proj_grads)
    output_share = join_rows(gated(final), gated(jnp.concatenate(output_halves)))
    residue = (output_share - teacher_wide) * all_mask
    squared = jnp.sum(residue * residue)

    feature_parts = jnp.concatenate(
        [part for layer in range(LAYERS) for part in feature_grads[layer]]
    )
    feature_parts = gated(feature_parts).reshape(-1, col_count, width)
    own_parts = lax.dynamic_index_in_dim(feature_parts, col_index, 1, False)
    other_parts = lax.dynamic_index_in_dim(feature_parts, col_count - 1 - col_index, 1, False)
    hidden_parts = jnp.concatenate([hidden_grads[layer] for layer in range(LAYERS)], axis=1)
    extra = jnp.zeros((1, width), wide_type).at[0, 0].set(squared)
    packed = jnp.concatenate(
        [jnp.stack([own_parts, other_parts]), hidden_parts, jnp.stack([extra, extra])], axis=1
    )
    packed = butterfly_sum(packed, ("dp", "row"))
    vectors = packed[0] + flip_col(packed[1])
    squared_total = butterfly_sum(packed[0, -1, 0], ("col",))
    loss_value = squared_total / (token_total * model_width)
    per_layer = len(feature_grads[0])
    features = vectors[: LAYERS * per_layer].reshape(LAYERS, per_layer, width)
    hiddens = vectors[LAYERS * per_layer : -1].reshape(LAYERS, -1, width)
    return (
        loss_value,
        output_share,
        input_share,
        features[:, 0:2],
        features[:, 2:4],
        jnp.transpose(in_grad, (0, 2, 1, 3)),
        hiddens[:, 0:2],
        proj_grad,
        features[:, 4],
        up_grad,
        hiddens[:, 2:].reshape(LAYERS, hidden_width),
        down_grad,
        features[:, 5],
    )


def solution(mesh):
    in_specs = (
        P(("dp", "row"), "col"),
        P(("dp", "row"), "col"),
        P(("dp", "row"), "col"),
        P(("dp", "row")),
        P(None, None, "col"),
        P(None, None, "col"),
        P(None, "row", None, "col"),
        P(None, None, "col"),
        P(None, "col", "row"),
        P(None, "col"),
        P(None, "row", "col"),
        P(None, "col"),
        P(None, "col", "row"),
        P(None, "col"),
    )
    out_specs = (
        P(),
        P(("dp", "row"), "col"),
        P(("dp", "row"), "col"),
        P(None, None, "col"),
        P(None, None, "col"),
        P(None, "row", None, "col"),
        P(None, None, "col"),
        P(None, "col", "row"),
        P(None, "col"),
        P(None, "row", "col"),
        P(None, "col"),
        P(None, "col", "row"),
        P(None, "col"),
    )
    return jax.shard_map(body, mesh=mesh, in_specs=in_specs, out_specs=out_specs, check_vma=False)
```

```python
import functools

import jax
import jax.numpy as jnp
from jax import lax
from jax.experimental import pallas as pl
from jax.experimental.pallas import tpu as pltpu
from jax.sharding import PartitionSpec as P

HEAD_DIM = 64
LAYERS = 2

epsilon = 1e-06
fill_value = -1e30
score_scale = HEAD_DIM ** (-0.5)
low_type = jnp.bfloat16
wide_type = jnp.float32
VMEM = pl.BlockSpec(memory_space=pltpu.VMEM)
SMEM = pl.BlockSpec(memory_space=pltpu.SMEM)
ANY = pl.BlockSpec(memory_space=pl.ANY)
vmem_bytes = 56 * 1024 * 1024


def dot(left, right):
    return lax.dot_general(
        left, right, (((1,), (0,)), ((), ())), preferred_element_type=wide_type
    )


def dot_right(left, right):
    return lax.dot_general(
        left, right, (((1,), (1,)), ((), ())), preferred_element_type=wide_type
    )


def dot_left(left, right):
    return lax.dot_general(
        left, right, (((0,), (0,)), ((), ())), preferred_element_type=wide_type
    )


def piece_copies(meta, refs, offset, tiles, target, sems):
    if len(refs) == 1:
        return [pltpu.make_async_copy(refs[0], target(None, None), sems.at[0])]
    copies = []
    core = meta[4]
    for place in range(3):
        for block in range(2):
            source = refs[place].at[block, pl.ds(offset, tiles)]
            copies.append((source, target(block, meta[place])))
    copies.append((refs[3].at[pl.ds(offset, tiles)], target(core, meta[3])))
    copies.append((refs[4].at[pl.ds(offset, tiles)], target(1 - core, meta[3])))
    return [
        pltpu.make_async_copy(source, place, sems.at[index])
        for index, (source, place) in enumerate(copies)
    ]


def in_copies(meta, refs, offset, weight, sems):
    def target(block, row_block):
        if block is None:
            return weight
        return weight.at[:, pl.ds(row_block * 256, 256), pl.ds(block * 256, 256)]

    return piece_copies(meta, refs, offset, 3, target, sems)


def proj_copies(meta, refs, offset, weight, sems):
    def target(block, row_block):
        if block is None:
            return weight
        return weight.at[pl.ds(block, 1), :, pl.ds(row_block * 256, 256)]

    return piece_copies(meta, refs, offset, 1, target, sems)


def up_copies(meta, refs, offset, weight, sems):
    def target(block, row_block):
        if block is None:
            return weight
        return weight.at[pl.ds(block * 4, 4), pl.ds(row_block * 256, 256), :]

    return piece_copies(meta, refs, offset, 4, target, sems)


def down_copies(meta, refs, offset, weight, sems):
    def target(block, row_block):
        if block is None:
            return weight
        return weight.at[pl.ds(block * 4, 4), :, pl.ds(row_block * 256, 256)]

    return piece_copies(meta, refs, offset, 4, target, sems)


def start_all(copies):
    for copy in copies:
        copy.start()


def wait_all(copies):
    for copy in copies:
        copy.wait()


def standardize(inputs):
    width = inputs.shape[1]
    centre = jnp.sum(inputs, axis=1, keepdims=True) / width
    centred = inputs - centre
    spread = jnp.sum(centred * centred, axis=1, keepdims=True) / width
    rscale = lax.rsqrt(spread + epsilon)
    return centred * rscale, rscale


def mask_rows(meta, rows, slots):
    parts = []
    for seq in range(rows // slots):
        place = lax.broadcasted_iota(jnp.int32, (slots, 1), 0)
        parts.append(jnp.where(place < meta[5 + seq], 1.0, 0.0).astype(wide_type))
    return parts[0] if len(parts) == 1 else jnp.concatenate(parts, axis=0)


def gelu_and_slope(u):
    size = jnp.abs(u) * 0.7071067811865476
    t = 1.0 / (1.0 + 0.3275911 * size)
    bell = jnp.exp(-size * size)
    tail = t * (
        0.254829592
        + t * (-0.284496736 + t * (1.421413741 + t * (-1.453152027 + t * 1.061405429)))
    )
    tail = 0.5 * tail * bell
    share = jnp.where(u >= 0.0, 1.0 - tail, tail)
    return u * share, share + u * bell * 0.3989422804014327


def place_blocks(meta, place, blocks, target):
    width = blocks[0].shape[1]
    for index, block in enumerate(blocks):
        at = pl.multiple_of(meta[place + index] * width, width)
        target[:, pl.ds(at, width)] = block[...]


def key_bias(meta, seq, slots):
    place = lax.broadcasted_iota(jnp.int32, (1, slots), 1)
    return place < meta[5 + seq]


def split_refs(refs, counts):
    out = []
    at = 0
    for count in counts:
        out.append(refs[at : at + count])
        at += count
    return out


def attend_kernel(first, slots, counts, offsets, meta, *refs):
    (base, sums, params, in_refs, proj_refs, outs, scratch) = split_refs(refs, counts)
    gains, shifts, query_shift, value_shift = params
    x_ref, normed_ref, query_ref, key_ref, value_ref, lse_ref, mixed_ref, wide_ref, low_ref = outs
    in_weight, proj_weight, in_sems, proj_sems = scratch
    in_moves = in_copies(meta, in_refs, offsets[0], in_weight, in_sems)
    proj_moves = proj_copies(meta, proj_refs, offsets[1], proj_weight, proj_sems)
    start_all(in_moves)
    start_all(proj_moves)
    rows = x_ref.shape[0]
    if first:
        place_blocks(meta, 5 + rows // slots, base, x_ref)
        current = x_ref[...]
    else:
        own, arrived, bias = sums
        current = base[0][...] + own[...] + arrived[...].astype(wide_type) + bias[...]
        current = current * mask_rows(meta, rows, slots)
        x_ref[...] = current
    standard, _ = standardize(current)
    normed = (standard * gains[...] + shifts[...]).astype(low_type)
    normed_ref[...] = normed
    wait_all(in_moves)
    query_ref[...] = (dot(normed, in_weight[0]) + query_shift[...]).astype(low_type)
    key_ref[...] = dot(normed, in_weight[1]).astype(low_type)
    value_ref[...] = (dot(normed, in_weight[2]) + value_shift[...]).astype(low_type)
    heads = query_ref.shape[1] // HEAD_DIM
    for seq in range(rows // slots):
        span = slice(seq * slots, (seq + 1) * slots)
        valid = key_bias(meta, seq, slots)
        for head in range(heads):
            lanes = slice(head * HEAD_DIM, (head + 1) * HEAD_DIM)
            scores = dot_right(query_ref[span, lanes], key_ref[span, lanes]) * score_scale
            scores = jnp.where(valid, scores, fill_value)
            maximum = jnp.max(scores, axis=1, keepdims=True)
            exponent = jnp.exp(scores - maximum)
            mass = jnp.sum(exponent, axis=1, keepdims=True)
            attention = (exponent * (1.0 / mass)).astype(low_type)
            mixed_ref[span, lanes] = dot(attention, value_ref[span, lanes]).astype(low_type)
            lse_ref[span, head : head + 1] = maximum + jnp.log(mass)
    wait_all(proj_moves)
    block = proj_weight.shape[1]
    total = dot(mixed_ref[:, :block], proj_weight[0])
    for index in range(1, proj_weight.shape[0]):
        total = total + dot(
            mixed_ref[:, index * block : (index + 1) * block], proj_weight[index]
        )
    wide_ref[...] = total
    low_ref[...] = total.astype(low_type)


def feed_kernel(counts, offsets, meta, *refs):
    (sums, params, up_refs, down_refs, outs, scratch) = split_refs(refs, counts)
    base, own, arrived, bias = sums
    gains, shifts, up_shift = params
    middle_ref, normed_ref, hidden_ref, slope_ref, wide_ref, low_ref = outs
    up_weight, down_weight, up_sems, down_sems = scratch
    up_moves = up_copies(meta, up_refs, offsets[0], up_weight, up_sems)
    down_moves = down_copies(meta, down_refs, offsets[1], down_weight, down_sems)
    start_all(up_moves)
    start_all(down_moves)
    middle = base[...] + own[...] + arrived[...].astype(wide_type) + bias[...]
    middle_ref[...] = middle
    standard, _ = standardize(middle)
    normed = (standard * gains[...] + shifts[...]).astype(low_type)
    normed_ref[...] = normed
    wait_all(up_moves)
    width = up_weight.shape[2]
    for index in range(up_weight.shape[0]):
        lanes = slice(index * width, (index + 1) * width)
        pre = dot(normed_ref[...], up_weight[index]) + up_shift[:, lanes]
        hidden, slope = gelu_and_slope(pre)
        hidden_ref[:, lanes] = hidden.astype(low_type)
        slope_ref[:, lanes] = slope.astype(low_type)
    wait_all(down_moves)
    rows = down_weight.shape[0] * down_weight.shape[1]
    total = dot(hidden_ref[...], down_weight[...].reshape(rows, down_weight.shape[2]))
    wide_ref[...] = total
    low_ref[...] = total.astype(low_type)


def norm_back(grad_rows, inputs, gains):
    standard, rscale = standardize(inputs)
    width = inputs.shape[1]
    scaled = grad_rows * gains
    first = jnp.sum(scaled, axis=1, keepdims=True) / width
    second = jnp.sum(scaled * standard, axis=1, keepdims=True) / width
    grad_input = rscale * (scaled - first - standard * second)
    return (
        grad_input,
        jnp.sum(grad_rows * standard, axis=0, keepdims=True),
        jnp.sum(grad_rows, axis=0, keepdims=True),
    )


def last_kernel(slots, meta, factor, base, own, arrived, bias, *refs):
    seeds, (current_ref, grad_ref) = refs[:-2], refs[-2:]
    rows = base.shape[0]
    mask = mask_rows(meta, rows, slots)
    place_blocks(meta, 5 + rows // slots, seeds, grad_ref)
    current = base[...] + own[...] + arrived[...].astype(wide_type) + bias[...]
    current = current * mask
    current_ref[...] = current
    grad_ref[...] = grad_ref[...] + factor[0] * current


def pull_kernel(inputs, gains, base, own, arrived, grad_ref, gain_ref, shift_ref):
    summed = own[...] + arrived[...].astype(wide_type)
    grad, gain, shift = norm_back(summed, inputs[...], gains[...])
    grad_ref[...] = base[...] + grad
    gain_ref[...] = gain
    shift_ref[...] = shift


def feed_back_kernel(slots, counts, offsets, meta, *refs):
    (sums, up_refs, down_refs, outs, scratch) = split_refs(refs, counts)
    grad, slope_ref = sums
    masked_ref, masked_low_ref, pre_ref, down_bias_ref, up_bias_ref, wide_ref, low_ref = outs
    up_weight, down_weight, up_sems, down_sems = scratch
    up_moves = up_copies(meta, up_refs, offsets[0], up_weight, up_sems)
    down_moves = down_copies(meta, down_refs, offsets[1], down_weight, down_sems)
    start_all(down_moves)
    start_all(up_moves)
    masked = grad[...] * mask_rows(meta, grad.shape[0], slots)
    masked_ref[...] = masked
    masked_low = masked.astype(low_type)
    masked_low_ref[...] = masked_low
    down_bias_ref[...] = jnp.sum(masked_low.astype(wide_type), axis=0, keepdims=True)
    wait_all(down_moves)
    width = up_weight.shape[2]
    for index in range(up_weight.shape[0]):
        lanes = slice(index * width, (index + 1) * width)
        hidden = dot_right(masked_low_ref[...], down_weight[index])
        pre = (hidden * slope_ref[:, lanes].astype(wide_type)).astype(low_type)
        pre_ref[:, lanes] = pre
        up_bias_ref[:, lanes] = jnp.sum(pre.astype(wide_type), axis=0, keepdims=True)
    wait_all(up_moves)
    total = dot_right(pre_ref[:, :width], up_weight[0])
    for index in range(1, up_weight.shape[0]):
        lanes = slice(index * width, (index + 1) * width)
        total = total + dot_right(pre_ref[:, lanes], up_weight[index])
    wide_ref[...] = total
    low_ref[...] = total.astype(low_type)


def attend_back_kernel(slots, counts, offsets, meta, *refs):
    (sums, params, saved, in_refs, proj_refs, outs, scratch) = split_refs(refs, counts)
    own, arrived, middle, masked = sums
    (gains,) = params
    query_ref, key_ref, value_ref, lse_ref = saved
    (
        grad_ref,
        low_grad_ref,
        gain_ref,
        shift_ref,
        proj_bias_ref,
        triple_ref,
        in_bias_ref,
        wide_ref,
        low_ref,
    ) = outs
    in_weight, proj_weight, mixed_grad, in_sems, proj_sems = scratch
    in_moves = in_copies(meta, in_refs, offsets[0], in_weight, in_sems)
    proj_moves = proj_copies(meta, proj_refs, offsets[1], proj_weight, proj_sems)
    start_all(proj_moves)
    start_all(in_moves)
    summed = own[...] + arrived[...].astype(wide_type)
    grad, gain, shift = norm_back(summed, middle[...], gains[...])
    grad = masked[...] + grad
    grad_ref[...] = grad
    gain_ref[...] = gain
    shift_ref[...] = shift
    grad_low = grad.astype(low_type)
    low_grad_ref[...] = grad_low
    proj_bias_ref[...] = jnp.sum(grad_low.astype(wide_type), axis=0, keepdims=True)
    wait_all(proj_moves)
    block = proj_weight.shape[1]
    for index in range(proj_weight.shape[0]):
        mixed_grad[:, index * block : (index + 1) * block] = dot_right(
            low_grad_ref[...], proj_weight[index]
        ).astype(low_type)
    heads = query_ref.shape[1] // HEAD_DIM
    rows = query_ref.shape[0]
    for seq in range(rows // slots):
        span = slice(seq * slots, (seq + 1) * slots)
        valid = key_bias(meta, seq, slots)
        for head in range(heads):
            lanes = slice(head * HEAD_DIM, (head + 1) * HEAD_DIM)
            queries = query_ref[span, lanes]
            keys = key_ref[span, lanes]
            outer = mixed_grad[span, lanes]
            scores = dot_right(queries, keys) * score_scale
            scores = jnp.where(valid, scores, fill_value)
            chance = jnp.exp(scores - lse_ref[span, head : head + 1])
            grad_chance = dot_right(outer, value_ref[span, lanes])
            inner = jnp.sum(grad_chance * chance, axis=1, keepdims=True)
            grad_scores = (chance * (grad_chance - inner)).astype(low_type)
            triple_ref[2, span, lanes] = dot_left(chance.astype(low_type), outer).astype(low_type)
            triple_ref[0, span, lanes] = (dot(grad_scores, keys) * score_scale).astype(low_type)
            triple_ref[1, span, lanes] = (dot_left(grad_scores, queries) * score_scale).astype(
                low_type
            )
    in_bias_ref[0:1, :] = jnp.sum(triple_ref[0].astype(wide_type), axis=0, keepdims=True)
    in_bias_ref[1:2, :] = jnp.sum(triple_ref[2].astype(wide_type), axis=0, keepdims=True)
    wait_all(in_moves)
    total = dot_right(triple_ref[0], in_weight[0])
    total = total + dot_right(triple_ref[1], in_weight[1])
    total = total + dot_right(triple_ref[2], in_weight[2])
    wide_ref[...] = total
    low_ref[...] = total.astype(low_type)


def feed_weight_kernel(meta, normed, pre, hidden, masked_low, *outs):
    def write(place, block, row_block):
        columns = pl.ds(pl.multiple_of(row_block * 256, 256), 256)
        for tile in range(4):
            lanes = pl.ds(pl.multiple_of(block * 1024 + tile * 256, 256), 256)
            place[tile] = dot_left(normed[:, columns], pre[:, lanes]).astype(low_type)
            place[4 + tile] = dot_left(hidden[:, lanes], masked_low[:, columns]).astype(low_type)

    write_pieces(meta, outs, write)


def attend_weight_kernel(meta, normed, triple, mixed, grad_low, *outs):
    def write(place, block, row_block):
        columns = pl.ds(pl.multiple_of(row_block * 256, 256), 256)
        lanes = pl.ds(pl.multiple_of(block * 256, 256), 256)
        for kind in range(3):
            place[kind] = dot_left(normed[:, columns], triple[kind, :, lanes]).astype(low_type)
        place[3] = dot_left(mixed[:, lanes], grad_low[:, columns]).astype(low_type)

    write_pieces(meta, outs, write)


def write_pieces(meta, outs, write):
    core = meta[4]
    for place in range(3):
        for block in range(2):
            write(outs[place].at[block], block, meta[place])
    write(outs[3], core, meta[3])
    write(outs[4], 1 - core, meta[3])


def near_add_kernel(meta, near, arrived, moved, out):
    for block in range(2):
        extra = jnp.where(meta[4] == block, moved[...].astype(wide_type), 0.0)
        total = near[block].astype(wide_type) + arrived[block].astype(wide_type) + extra
        out[block] = total.astype(low_type)


def finish_feed_kernel(meta, *refs):
    halves, (up, down) = refs[:-2], refs[-2:]
    first = meta[4] == 0
    for layer in range(len(halves) // 2):
        part, other = halves[2 * layer], halves[2 * layer + 1]
        for tile in range(4):
            mine, its = part[tile].astype(wide_type), other[tile].astype(wide_type)
            up[layer, :, tile * 256 : (tile + 1) * 256] = jnp.where(first, mine, its)
            down[layer, tile * 256 : (tile + 1) * 256, :] = jnp.where(first, its, mine)


def finish_attend_kernel(meta, *refs):
    halves, (thirds, square) = refs[:-2], refs[-2:]
    first = meta[4] == 0
    for layer in range(len(halves) // 2):
        part, other = halves[2 * layer], halves[2 * layer + 1]
        mine, its = part[...].astype(wide_type), other[...].astype(wide_type)
        thirds[layer, 0] = jnp.where(first, mine[0], its[0])
        thirds[layer, 1] = jnp.where(first, mine[1], its[1])
        thirds[layer, 2] = jnp.where(first, its[0], mine[0])
        square[layer] = jnp.where(first, its[1], mine[1])


def flip_col(value):
    count = lax.axis_size("col")
    return lax.ppermute(value, "col", [(i, count - 1 - i) for i in range(count)])


def swap_core(value):
    count = lax.axis_size("dp")
    return lax.ppermute(value, "dp", [(i, count - 1 - i) for i in range(count)])


def group_shift(value, step):
    count = lax.axis_size("col")
    half = count // 2
    pairs = [(i, i // half * half + (i % half + step) % half) for i in range(count)]
    return lax.ppermute(value, "col", pairs)


def cross_row(value, first_step, second_step):
    rows = lax.axis_size("row")
    cols = lax.axis_size("col")
    pairs = []
    for core, step in ((0, first_step), (1, second_step)):
        for row in range(rows):
            for col in range(cols):
                source = (core * rows + row) * cols + col
                pairs.append((source, (core * rows + (row ^ step)) * cols + col))
    return lax.ppermute(value, ("dp", "row", "col"), pairs)


def group_total(wide, low):
    arrived = group_shift(low, 1)
    for step in range(2, lax.axis_size("col") // 2):
        wide = wide + group_shift(low, step).astype(wide_type)
    return wide, arrived


def butterfly_sum(value, axes):
    for axis in axes:
        count = lax.axis_size(axis)
        step = 1
        while step < count:
            value = value + lax.ppermute(value, axis, [(i, i ^ step) for i in range(count)])
            step *= 2
    return value


def after(value, *events):
    return lax.optimization_barrier((value,) + events)[0]


def order_blocks(pair):
    count = lax.axis_size("col")
    half = count // 2
    col_index = lax.axis_index("col")
    base = col_index // half * half
    wanted = lax.broadcasted_iota(jnp.int32, (count,) + pair.shape[1:], 0)
    whole = jnp.zeros((count,) + pair.shape[1:], pair.dtype)
    for step in range(half):
        piece = pair if step == 0 else group_shift(pair, step)
        source = base + (col_index - base + half - step) % half
        whole = jnp.where(wanted == source, piece[0][None], whole)
        whole = jnp.where(wanted == count - 1 - source, piece[1][None], whole)
    return whole


def add(left, right):
    return (left.astype(wide_type) + right.astype(wide_type)).astype(low_type)


def gather_near(own):
    return cross_row(own, 1, 2)


def gather_far(near, first_core):
    return cross_row(jnp.where(first_core, near[0], near[1]), 2, 1)


def gather_pieces(own, near, far):
    return (own, near, swap_core(near), far, swap_core(far))


def flip_tiles(shard, first_core):
    half = shard.shape[0] // 2
    return flip_col(jnp.where(first_core, shard[:half], shard[half:]))


def join_tiles(shard, got, other, first_core):
    halves = jnp.where(first_core, jnp.stack([got, other]), jnp.stack([other, got]))
    return jnp.stack([shard, halves.reshape(shard.shape)])


def scatter_first(pieces):
    own, near, near_other, far, far_other = pieces
    return own, near, swap_core(near_other), add(far, swap_core(far_other))


def scatter_third(own, arrived, first_core):
    own = add(own, arrived)
    half = own.shape[1] // 2
    lower, upper = own[:, :half], own[:, half:]
    arrived = swap_core(jnp.where(first_core, upper, lower))
    return add(jnp.where(first_core, lower, upper), arrived)


def body(
    states,
    teacher,
    cotangent,
    lengths,
    norm_gain,
    norm_bias,
    in_weight,
    in_bias,
    proj_weight,
    proj_bias,
    up_weight,
    up_bias,
    down_weight,
    down_bias,
):
    col_count = lax.axis_size("col")
    row_count = lax.axis_size("row")
    core_count = lax.axis_size("dp")
    half_group = col_count // 2
    col_index = lax.axis_index("col")
    row_index = lax.axis_index("row")
    core_index = lax.axis_index("dp")
    group_index = col_index // half_group
    first_core = core_index == 0
    token_rows, width = states.shape
    model_width = width * col_count
    seqs = lengths.shape[0] // 2
    rows = token_rows // 2
    slots = rows // seqs
    hidden_width = up_bias.shape[1]
    tiled = row_count == 4 and width == 256 and hidden_width == 1024 and model_width == 1024
    row_width = model_width // row_count
    heads_width = 2 * width
    feed_width = 2 * hidden_width
    in_thirds = jnp.transpose(in_weight, (0, 2, 1, 3))

    def own_half(value):
        return lax.dynamic_slice_in_dim(value, group_index * rows, rows, 0)

    def other_half(value):
        return lax.dynamic_slice_in_dim(value, (1 - group_index) * rows, rows, 0)

    block_places = []
    for step in range(half_group):
        base = group_index * half_group
        source = base + (col_index - base + half_group - step) % half_group
        block_places = block_places + [source, col_count - 1 - source]

    def join_rows(value, received):
        own = lax.dynamic_slice_in_dim(value, col_index * width, width, 1)
        lower = jnp.where(group_index == 0, own, received)
        upper = jnp.where(group_index == 0, received, own)
        return jnp.concatenate([lower, upper])

    def share_rows(value, kind):
        other = lax.dynamic_slice_in_dim(value, (col_count - 1 - col_index) * width, width, 1)
        return join_rows(value, flip_col(other.astype(kind)).astype(wide_type))

    own_lengths = lax.dynamic_slice_in_dim(lengths, group_index * seqs, seqs, 0)
    meta = jnp.concatenate(
        [
            jnp.stack(
                [
                    row_index,
                    row_index ^ (1 + core_index),
                    row_index ^ (2 - core_index),
                    row_index ^ 3,
                    core_index,
                ]
            ),
            own_lengths,
            jnp.stack(block_places),
        ]
    ).astype(jnp.int32)

    in_full, proj_full, up_full, down_full = ([None] * LAYERS for kind in range(4))
    feature_pack = jnp.concatenate(
        [norm_gain.reshape(-1, width), norm_bias.reshape(-1, width), proj_bias, down_bias]
    )
    hidden_pack = jnp.concatenate([in_bias.reshape(-1, width), up_bias.reshape(-1, width)])
    feature_rows = feature_pack.shape[0]
    small = jnp.concatenate([feature_pack, hidden_pack])
    states_own, states_other = own_half(states), other_half(states)
    gate = []

    def gated(value):
        return after(value, *gate) if gate else value

    def all_shifts(value):
        return [group_shift(value, step) for step in range(1, half_group)]

    def all_blocks(own, own_shifts, flipped, flipped_shifts):
        blocks = [own, flipped]
        for pair in zip(own_shifts, flipped_shifts):
            blocks = blocks + list(pair)
        return blocks

    total_steps = [
        (axis, 2**bit)
        for axis in ("dp", "row")
        for bit in range(lax.axis_size(axis).bit_length() - 1)
    ]
    token_total = jnp.sum(lengths)

    def count_step(value, axis, step):
        size = lax.axis_size(axis)
        return value + lax.ppermute(value, axis, [(i, i ^ step) for i in range(size)])

    if tiled:
        count = 6
        shards, flips, owns, nears, near_others, fars, far_others = (
            [None] * count for kind in range(7)
        )

        def up_tiles(weight):
            return jnp.transpose(weight.reshape(256, 4, 256), (1, 0, 2))

        def flip(place):
            layer = place // 3
            if place % 3 == 0:
                square = gated(proj_weight[layer])[None]
                shards[place] = jnp.concatenate([gated(in_thirds[layer]), square])
            elif place % 3 == 1:
                shards[place] = up_tiles(gated(up_weight[layer]))
            else:
                shards[place] = gated(down_weight[layer]).reshape(4, 256, 256)
            flips[place] = flip_tiles(shards[place], first_core)
            return flips[place]

        def near(place):
            got = gated(flips[place])
            owns[place] = join_tiles(shards[place], got, swap_core(got), first_core)
            nears[place] = cross_row(owns[place], 1, 2)
            return nears[place]

        def near_swap(place):
            near_others[place] = swap_core(gated(nears[place]))
            return near_others[place]

        def far(place):
            value = gated(nears[place])
            fars[place] = cross_row(jnp.where(first_core, value[0], value[1]), 2, 1)
            return fars[place]

        def far_swap(place):
            far_others[place] = swap_core(gated(fars[place]))
            return far_others[place]

        def pieces(place):
            return (
                owns[place],
                nears[place],
                near_others[place],
                fars[place],
                far_others[place],
            )

        gate = [flip(0)]
        states_flipped = flip_col(gated(states_other))
        shifts_own = all_shifts(gated(states_own))
        small_flipped = flip_col(gated(small))
        token_total = count_step(gated(token_total), *total_steps[0])
        gate = [near(0), states_flipped, small_flipped, token_total, *shifts_own]
        small_pair = jnp.stack([small, gated(small_flipped)])
        feature_all = order_blocks(small_pair[:, :feature_rows])
        shifts_flipped = all_shifts(gated(states_flipped))
        token_total = count_step(gated(token_total), *total_steps[1])
        gate = [far(0), flip(1), near_swap(0), token_total, feature_all, *shifts_flipped]
        states_blocks = all_blocks(states_own, shifts_own, states_flipped, shifts_flipped)
        token_total = count_step(gated(token_total), *total_steps[2])
        first_slot = [near(1), flip(2), token_total]
        far_swap(0)
        in_full[0], proj_full[0] = (pieces(0), 0), (pieces(0), 3)
    else:

        def both_blocks(shard):
            own = lax.all_gather(shard, "row", axis=0, tiled=False)
            return jnp.stack([own, flip_col(own)])

        for layer in range(LAYERS):
            whole = jnp.transpose(both_blocks(in_thirds[layer]), (2, 1, 3, 0, 4))
            in_full[layer] = ((whole.reshape(3, model_width, heads_width),), 0)
            whole = jnp.transpose(both_blocks(proj_weight[layer]), (0, 2, 1, 3))
            proj_full[layer] = ((whole.reshape(2, width, model_width),), 0)
            whole = both_blocks(up_weight[layer]).reshape(2, model_width, -1, 256)
            whole = jnp.transpose(whole, (0, 2, 1, 3))
            up_full[layer] = ((whole.reshape(-1, model_width, 256),), 0)
            whole = jnp.transpose(both_blocks(down_weight[layer]), (0, 2, 1, 3))
            down_full[layer] = ((whole.reshape(-1, 256, model_width),), 0)
        states_flipped = flip_col(states_other)
        small_flipped = flip_col(small)
        states_blocks = all_blocks(
            states_own, all_shifts(states_own), states_flipped, all_shifts(states_flipped)
        )
        for step in total_steps:
            token_total = count_step(token_total, *step)
        small_pair = jnp.stack([small, small_flipped])
        feature_all = order_blocks(small_pair[:, :feature_rows])

    feature_all = jnp.transpose(feature_all, (1, 0, 2)).reshape(feature_rows, model_width)
    gains = feature_all[: 2 * LAYERS].reshape(LAYERS, 2, 1, model_width)
    shifts = feature_all[2 * LAYERS : 4 * LAYERS].reshape(LAYERS, 2, 1, model_width)
    proj_shift = feature_all[4 * LAYERS : 5 * LAYERS].reshape(LAYERS, 1, model_width)
    down_shift = feature_all[5 * LAYERS :].reshape(LAYERS, 1, model_width)
    hidden_pair = small_pair[:, feature_rows:]
    in_shift = hidden_pair[:, : 2 * LAYERS].reshape(2, LAYERS, 2, width)
    in_shift = jnp.transpose(in_shift, (1, 2, 0, 3)).reshape(LAYERS, 2, 1, heads_width)
    up_shift = hidden_pair[:, 2 * LAYERS :].reshape(2, LAYERS, hidden_width)
    up_shift = jnp.transpose(up_shift, (1, 0, 2)).reshape(LAYERS, 1, feed_width)


    def shape(*dims, kind=wide_type):
        return jax.ShapeDtypeStruct(dims, kind)

    def call(kernel, cost, operands, specs, outs, scratch=()):
        return pl.pallas_call(
            kernel,
            out_shape=outs,
            in_specs=specs,
            out_specs=[VMEM] * len(outs),
            scratch_shapes=list(scratch),
            compiler_params=pltpu.CompilerParams(vmem_limit_bytes=vmem_bytes),
            cost_estimate=pl.CostEstimate(
                flops=int(cost * 9.2e9), bytes_accessed=1024 * 1024, transcendentals=0
            ),
        )(*operands)

    wide_rows = shape(rows, model_width)
    low_rows = shape(rows, model_width, kind=low_type)
    low_heads = shape(rows, heads_width, kind=low_type)
    heads = heads_width // HEAD_DIM
    feed_tiles = feed_width // 256
    attend_scratch = [
        pltpu.VMEM((3, model_width, heads_width), low_type),
        pltpu.VMEM((2, width, model_width), low_type),
    ]
    feed_scratch = [
        pltpu.VMEM((feed_tiles, model_width, 256), low_type),
        pltpu.VMEM((feed_tiles, 256, model_width), low_type),
    ]
    sems = [pltpu.SemaphoreType.DMA((8,)), pltpu.SemaphoreType.DMA((8,))]

    def attend(layer, base, sums):
        first = len(sums) == 0
        params = [gains[layer, 0], shifts[layer, 0], in_shift[layer, 0], in_shift[layer, 1]]
        in_refs, in_offset = in_full[layer]
        proj_refs, proj_offset = proj_full[layer]
        counts = (len(base), len(sums), 4, len(in_refs), len(proj_refs), 9, 4)
        operands = [meta, *base, *sums, *params, *in_refs, *proj_refs]
        specs = [SMEM] + [VMEM] * (4 + len(base) + len(sums)) + [ANY] * (len(in_refs) + len(proj_refs))
        kernel = functools.partial(attend_kernel, first, slots, counts, (in_offset, proj_offset))
        outs = [
            wide_rows,
            low_rows,
            low_heads,
            low_heads,
            low_heads,
            shape(rows, heads),
            low_heads,
            wide_rows,
            low_rows,
        ]
        return call(kernel, 10.5, operands, specs, outs, attend_scratch + sems)

    def feed(layer, base, sums):
        params = [gains[layer, 1], shifts[layer, 1], up_shift[layer]]
        up_refs, up_offset = up_full[layer]
        down_refs, down_offset = down_full[layer]
        counts = (4, 3, len(up_refs), len(down_refs), 6, 4)
        operands = [meta, base, *sums, *params, *up_refs, *down_refs]
        specs = [SMEM] + [VMEM] * 7 + [ANY] * (len(up_refs) + len(down_refs))
        kernel = functools.partial(feed_kernel, counts, (up_offset, down_offset))
        low_feed = shape(rows, feed_width, kind=low_type)
        outs = [wide_rows, low_rows, low_feed, low_feed, wide_rows, low_rows]
        return call(kernel, 12.0, operands, specs, outs, feed_scratch + sems)

    def feed_back(layer, grad, slope):
        up_refs, up_offset = up_full[layer]
        down_refs, down_offset = down_full[layer]
        counts = (2, len(up_refs), len(down_refs), 7, 4)
        operands = [meta, grad, slope, *up_refs, *down_refs]
        specs = [SMEM] + [VMEM] * 2 + [ANY] * (len(up_refs) + len(down_refs))
        kernel = functools.partial(feed_back_kernel, slots, counts, (up_offset, down_offset))
        outs = [
            wide_rows,
            low_rows,
            shape(rows, feed_width, kind=low_type),
            shape(1, model_width),
            shape(1, feed_width),
            wide_rows,
            low_rows,
        ]
        return call(kernel, 10.0, operands, specs, outs, feed_scratch + sems)

    def attend_back(layer, sums, middle, masked, saved):
        in_refs, in_offset = in_full[layer]
        proj_refs, proj_offset = proj_full[layer]
        counts = (4, 1, 4, len(in_refs), len(proj_refs), 9, 5)
        operands = [meta, *sums, middle, masked, gains[layer, 1], *saved, *in_refs, *proj_refs]
        specs = [SMEM] + [VMEM] * 9 + [ANY] * (len(in_refs) + len(proj_refs))
        kernel = functools.partial(attend_back_kernel, slots, counts, (in_offset, proj_offset))
        outs = [
            wide_rows,
            low_rows,
            shape(1, model_width),
            shape(1, model_width),
            shape(1, model_width),
            shape(3, rows, heads_width, kind=low_type),
            shape(2, heads_width),
            wide_rows,
            low_rows,
        ]
        scratch = attend_scratch + [pltpu.VMEM((rows, heads_width), low_type)] + sems
        return call(kernel, 12.0, operands, specs, outs, scratch)

    def weight_tiles(kernel, tiles, cost, *operands):
        outs = [shape(2, tiles, 256, 256, kind=low_type)] * 3
        outs = outs + [shape(tiles, 256, 256, kind=low_type)] * 2
        specs = [SMEM] + [VMEM] * len(operands)
        return call(kernel, cost, (meta,) + operands, specs, outs)

    positions = jnp.arange(slots, dtype=jnp.int32)
    all_mask = (positions[None, :] < lengths[:, None]).reshape(token_rows, 1).astype(wide_type)
    teacher_wide = teacher.astype(wide_type)

    def near_add(near, arrived, moved):
        tiles = moved.shape[0]
        both = pl.BlockSpec((2, 4, 256, 256), lambda index: (0, index, 0, 0))
        single = pl.BlockSpec((4, 256, 256), lambda index: (index, 0, 0))
        return pl.pallas_call(
            near_add_kernel,
            grid=(tiles // 4,),
            out_shape=shape(2, tiles, 256, 256, kind=low_type),
            in_specs=[SMEM, both, both, single],
            out_specs=both,
            cost_estimate=pl.CostEstimate(
                flops=int(tiles * 2.4e9), bytes_accessed=1024 * 1024, transcendentals=0
            ),
        )(meta, near, arrived, moved)

    def finish(kernel, cost, outs, parts):
        halves = []
        for part in parts:
            halves = halves + [part, swap_core(part)]
        return call(kernel, cost, (meta, *halves), [SMEM] + [VMEM] * len(halves), outs)

    saved = []
    base, sums = states_blocks, ()
    for layer in range(LAYERS):
        if layer > 0:
            sums = (*sums, down_shift[layer - 1])
        current, normed_one, queries, keys, values, lse, mixed, wide, low = attend(
            layer, base, sums
        )
        event = wide
        if layer == 0:
            if tiled:
                gate = [wide, *first_slot]
                second_slot = [far(1), near(2), flip(3), near_swap(1)]
            wide, arrived = group_total(wide, low)
            token_total = token_total.astype(wide_type)
            factor = 2.0 * token_rows * core_count * row_count / token_total
            seed_share = cotangent - factor * all_mask * teacher_wide
            seed_own, seed_other = own_half(seed_share), other_half(seed_share)
            if tiled:
                gate = [*second_slot, arrived]
                second_slot = [far(2), near(3), flip(4), far_swap(1), near_swap(2)]
                gate = [fars[2]]
                far_swap(2)
                up_full[0], down_full[0] = (pieces(1), 0), (pieces(2), 0)
        else:
            if tiled:
                low = after(low, seed_flipped)
                gate = [event, *second_slot, seed_flipped]
                second_slot = [far(5), far_swap(4), near_swap(5)]
                gate = [fars[5]]
                far_swap(5)
                up_full[1], down_full[1] = (pieces(4), 0), (pieces(5), 0)
            wide, arrived = group_total(wide, low)
            gate = [arrived]
            shifts_own, shifts_flipped = all_shifts(gated(seed_own)), all_shifts(gated(seed_flipped))
            seed_blocks = all_blocks(seed_own, shifts_own, seed_flipped, shifts_flipped)
        middle, normed_two, hidden, slope, wide, low = feed(
            layer, current, (wide, arrived, proj_shift[layer])
        )
        if layer == 1:
            low = after(low, *seed_blocks)
        event = wide
        wide, arrived = group_total(wide, low)
        if layer == 0:
            gate = [event, *second_slot] if tiled else []
            if tiled:
                second_slot = [far(3), near(4), flip(5), near_swap(3)]
                gate = [fars[3]]
                far_swap(3)
                in_full[1], proj_full[1] = (pieces(3), 0), (pieces(3), 3)
                gate = [arrived, *second_slot]
                second_slot = [near(5), far(4), near_swap(4)]
            seed_flipped = flip_col(gated(seed_other))
        base, sums = [middle], (wide, arrived)
        saved.append(
            (current, normed_one, queries, keys, values, lse, mixed, middle, normed_two, hidden, slope)
        )
    final, grad = call(
        functools.partial(last_kernel, slots),
        4.3,
        (meta, factor.reshape(1), *base, *sums, down_shift[LAYERS - 1], *seed_blocks),
        [SMEM, SMEM] + [VMEM] * (4 + len(seed_blocks)),
        [wide_rows, wide_rows],
    )
    output_other = lax.dynamic_slice_in_dim(
        final, (col_count - 1 - col_index) * width, width, 1
    )
    output_halves = [flip_col(output_other[: rows // 2])]

    feature_grads = {}
    hidden_grads = {}
    in_grads, proj_grads, up_grads, down_grads = ([None] * LAYERS for kind in range(4))

    way = []
    for layer in reversed(range(LAYERS)):
        current, normed_one, queries, keys, values, lse, mixed, middle, normed_two, hidden, slope = (
            saved[layer]
        )
        masked, masked_low, pre, down_bias_part, up_bias_part, wide, low = feed_back(
            layer, grad, slope
        )
        if tiled:
            if layer == LAYERS - 1:
                gate = [low, output_halves[0]]
            else:
                gate = [low, far_moved]
        wide, arrived = group_total(wide, gated(low))
        if tiled:
            tiles = weight_tiles(
                feed_weight_kernel, 8, 9.0, normed_two, gated(pre), hidden, masked_low
            )
            way.append(scatter_first(tiles))
            gate = [arrived, *tiles, *way[-1]]
            if layer < LAYERS - 1:
                own, near_part, near_arrived, far_part = way[-2]
                near_sent = near_add(near_part, near_arrived, far_moved)
                part = scatter_third(way[-3][0], near_moved, first_core)
                gate = gate + [near_sent, part]
                near_moved = cross_row(near_sent, 1, 2)
                flip_moved = flip_col(after(part[1], *gate))
            arrived = gated(arrived)
            far_moved = cross_row(gated(way[-1][3]), 2, 1)
        (
            grad,
            grad_low,
            gain_two,
            shift_two,
            proj_bias_part,
            triple,
            in_bias_part,
            wide,
            low,
        ) = attend_back(layer, (wide, arrived), middle, masked, (queries, keys, values, lse))
        if layer == LAYERS - 1:
            output_halves.append(flip_col(gated(output_other[rows // 2 :])))
        if tiled:
            gate = [low, far_moved] + (output_halves[1:] if layer == LAYERS - 1 else [])
        wide, arrived = group_total(wide, gated(low))
        if tiled:
            own, near_part, near_arrived, far_part = way[-1]
            near_sent = near_add(near_part, near_arrived, far_moved)
            if layer < LAYERS - 1:
                gate = [*gate, near_sent]
            else:
                received = gated(jnp.concatenate(output_halves))
            tiles = weight_tiles(
                attend_weight_kernel, 4, 5.5, normed_one, gated(triple), mixed, grad_low
            )
            way.append(scatter_first(tiles))
            gate = [arrived, *tiles, *way[-1], near_sent]
            if layer == LAYERS - 1:
                output_share = join_rows(final, received)
                residue = (output_share - teacher_wide) * all_mask
                squared = jnp.sum(residue * residue)
                gate = gate + [squared]
            if layer < LAYERS - 1:
                feed_parts = [add(part[0], flip_moved)]
                part = scatter_third(way[-3][0], near_moved, first_core)
                gate = gate + [part, *feed_parts]
                flip_moved = flip_col(after(part[1], *gate))
            near_moved = cross_row(near_sent, 1, 2)
            arrived = gated(arrived)
            far_moved = cross_row(gated(way[-1][3]), 2, 1)
        else:
            if layer == LAYERS - 1:
                output_share = join_rows(final, jnp.concatenate(output_halves))
                residue = (output_share - teacher_wide) * all_mask
                squared = jnp.sum(residue * residue)

            def product(spec, left, right):
                return jnp.einsum(spec, left, right, preferred_element_type=wide_type)

            def own_block(blocks):
                part = lax.psum_scatter(
                    blocks.astype(low_type), "row", scatter_dimension=1, tiled=False
                )
                mine = add(part[0], flip_col(part[1]))
                return mine.astype(wide_type) + swap_core(mine).astype(wide_type)

            def by_row(value):
                return value.reshape(rows, row_count, row_width)

            def by_block(value):
                return value.reshape(value.shape[:-1] + (2, -1))

            in_grads[layer] = own_block(
                product("trd,ptbe->brpde", by_row(normed_one), by_block(triple))
            )
            proj_grads[layer] = own_block(
                product("tbe,trd->bred", by_block(mixed), by_row(grad_low))
            )
            up_grads[layer] = own_block(product("trd,tbe->brde", by_row(normed_two), by_block(pre)))
            down_grads[layer] = own_block(
                product("tbe,trd->bred", by_block(hidden), by_row(masked_low))
            )
        grad, gain_one, shift_one = call(
            pull_kernel,
            4.3,
            (current, gains[layer, 0], grad, wide, arrived),
            [VMEM] * 5,
            [wide_rows, shape(1, model_width), shape(1, model_width)],
        )
        feature_grads[layer] = (
            gain_one,
            gain_two,
            shift_one,
            shift_two,
            proj_bias_part,
            down_bias_part,
        )
        hidden_grads[layer] = jnp.concatenate(
            [
                jnp.transpose(in_bias_part.reshape(2, 2, width), (1, 0, 2)),
                up_bias_part.reshape(2, -1, width),
            ],
            axis=1,
        )

    if tiled:
        gate = [grad, far_moved]
        input_share = share_rows(gated(grad), low_type)
        own, near_part, near_arrived, far_part = way[-1]
        near_sent = near_add(near_part, near_arrived, far_moved)
        attend_parts = [add(part[0], flip_moved)]
        part = scatter_third(way[-2][0], near_moved, first_core)
        last_moved = cross_row(after(near_sent, part), 1, 2)
        feed_parts.append(add(part[0], flip_col(part[1])))
        part = scatter_third(way[-1][0], last_moved, first_core)
        gate = [part]
        attend_parts.append(add(part[0], flip_col(part[1])))
        up_grad, down_grad = finish(
            finish_feed_kernel,
            3.0,
            [shape(LAYERS, 256, 1024), shape(LAYERS, 1024, 256)],
            feed_parts[::-1],
        )
        in_grad, proj_grad = finish(
            finish_attend_kernel,
            2.0,
            [shape(LAYERS, 3, 256, 256), shape(LAYERS, 256, 256)],
            attend_parts[::-1],
        )
    else:
        input_share = share_rows(grad, low_type)
        up_grad, down_grad = jnp.stack(up_grads), jnp.stack(down_grads)
        in_grad, proj_grad = jnp.stack(in_grads), jnp.stack(proj_grads)
    feature_parts = jnp.concatenate(
        [part for layer in range(LAYERS) for part in feature_grads[layer]]
    )
    feature_parts = gated(feature_parts).reshape(-1, col_count, width)
    own_parts = lax.dynamic_index_in_dim(feature_parts, col_index, 1, False)
    other_parts = lax.dynamic_index_in_dim(feature_parts, col_count - 1 - col_index, 1, False)
    hidden_parts = jnp.concatenate([hidden_grads[layer] for layer in range(LAYERS)], axis=1)
    extra = jnp.zeros((1, width), wide_type).at[0, 0].set(squared)
    packed = jnp.concatenate(
        [jnp.stack([own_parts, other_parts]), hidden_parts, jnp.stack([extra, extra])], axis=1
    )
    packed = butterfly_sum(packed, ("dp", "row"))
    vectors = packed[0] + flip_col(packed[1])
    squared_total = butterfly_sum(packed[0, -1, 0], ("col",))
    loss_value = squared_total / (token_total * model_width)
    per_layer = len(feature_grads[0])
    features = vectors[: LAYERS * per_layer].reshape(LAYERS, per_layer, width)
    hiddens = vectors[LAYERS * per_layer : -1].reshape(LAYERS, -1, width)
    return (
        loss_value,
        output_share,
        input_share,
        features[:, 0:2],
        features[:, 2:4],
        jnp.transpose(in_grad, (0, 2, 1, 3)),
        hiddens[:, 0:2],
        proj_grad,
        features[:, 4],
        up_grad,
        hiddens[:, 2:].reshape(LAYERS, hidden_width),
        down_grad,
        features[:, 5],
    )


def solution(mesh):
    in_specs = (
        P(("dp", "row"), "col"),
        P(("dp", "row"), "col"),
        P(("dp", "row"), "col"),
        P(("dp", "row")),
        P(None, None, "col"),
        P(None, None, "col"),
        P(None, "row", None, "col"),
        P(None, None, "col"),
        P(None, "col", "row"),
        P(None, "col"),
        P(None, "row", "col"),
        P(None, "col"),
        P(None, "col", "row"),
        P(None, "col"),
    )
    out_specs = (
        P(),
        P(("dp", "row"), "col"),
        P(("dp", "row"), "col"),
        P(None, None, "col"),
        P(None, None, "col"),
        P(None, "row", None, "col"),
        P(None, None, "col"),
        P(None, "col", "row"),
        P(None, "col"),
        P(None, "row", "col"),
        P(None, "col"),
        P(None, "col", "row"),
        P(None, "col"),
    )
    return jax.shard_map(body, mesh=mesh, in_specs=in_specs, out_specs=out_specs, check_vma=False)
```

```python
import functools

import jax
import jax.numpy as jnp
from jax import lax
from jax.experimental import pallas as pl
from jax.experimental.pallas import tpu as pltpu
from jax.sharding import PartitionSpec as P

HEAD_DIM = 64
LAYERS = 2

epsilon = 1e-06
fill_value = -1e30
score_scale = HEAD_DIM ** (-0.5)
low_type = jnp.bfloat16
wide_type = jnp.float32
VMEM = pl.BlockSpec(memory_space=pltpu.VMEM)
SMEM = pl.BlockSpec(memory_space=pltpu.SMEM)
ANY = pl.BlockSpec(memory_space=pl.ANY)
vmem_bytes = 56 * 1024 * 1024


def dot(left, right):
    return lax.dot_general(
        left, right, (((1,), (0,)), ((), ())), preferred_element_type=wide_type
    )


def dot_right(left, right):
    return lax.dot_general(
        left, right, (((1,), (1,)), ((), ())), preferred_element_type=wide_type
    )


def dot_left(left, right):
    return lax.dot_general(
        left, right, (((0,), (0,)), ((), ())), preferred_element_type=wide_type
    )


def piece_copies(meta, refs, offset, tiles, target, sems):
    if len(refs) == 1:
        return [pltpu.make_async_copy(refs[0], target(None, None), sems.at[0])]
    copies = []
    core = meta[4]
    for place in range(3):
        for block in range(2):
            source = refs[place].at[block, pl.ds(offset, tiles)]
            copies.append((source, target(block, meta[place])))
    copies.append((refs[3].at[pl.ds(offset, tiles)], target(core, meta[3])))
    copies.append((refs[4].at[pl.ds(offset, tiles)], target(1 - core, meta[3])))
    return [
        pltpu.make_async_copy(source, place, sems.at[index])
        for index, (source, place) in enumerate(copies)
    ]


def in_copies(meta, refs, offset, weight, sems):
    def target(block, row_block):
        if block is None:
            return weight
        return weight.at[:, pl.ds(row_block * 256, 256), pl.ds(block * 256, 256)]

    return piece_copies(meta, refs, offset, 3, target, sems)


def proj_copies(meta, refs, offset, weight, sems):
    def target(block, row_block):
        if block is None:
            return weight
        return weight.at[pl.ds(block, 1), :, pl.ds(row_block * 256, 256)]

    return piece_copies(meta, refs, offset, 1, target, sems)


def up_copies(meta, refs, offset, weight, sems):
    def target(block, row_block):
        if block is None:
            return weight
        return weight.at[pl.ds(block * 4, 4), pl.ds(row_block * 256, 256), :]

    return piece_copies(meta, refs, offset, 4, target, sems)


def down_copies(meta, refs, offset, weight, sems):
    def target(block, row_block):
        if block is None:
            return weight
        return weight.at[pl.ds(block * 4, 4), :, pl.ds(row_block * 256, 256)]

    return piece_copies(meta, refs, offset, 4, target, sems)


def start_all(copies):
    for copy in copies:
        copy.start()


def wait_all(copies):
    for copy in copies:
        copy.wait()


def standardize(inputs):
    width = inputs.shape[1]
    centre = jnp.sum(inputs, axis=1, keepdims=True) / width
    centred = inputs - centre
    spread = jnp.sum(centred * centred, axis=1, keepdims=True) / width
    rscale = lax.rsqrt(spread + epsilon)
    return centred * rscale, rscale


def mask_rows(meta, rows, slots):
    parts = []
    for seq in range(rows // slots):
        place = lax.broadcasted_iota(jnp.int32, (slots, 1), 0)
        parts.append(jnp.where(place < meta[5 + seq], 1.0, 0.0).astype(wide_type))
    return parts[0] if len(parts) == 1 else jnp.concatenate(parts, axis=0)


def gelu_and_slope(u):
    size = jnp.abs(u) * 0.7071067811865476
    t = 1.0 / (1.0 + 0.3275911 * size)
    bell = jnp.exp(-size * size)
    tail = t * (
        0.254829592
        + t * (-0.284496736 + t * (1.421413741 + t * (-1.453152027 + t * 1.061405429)))
    )
    tail = 0.5 * tail * bell
    share = jnp.where(u >= 0.0, 1.0 - tail, tail)
    return u * share, share + u * bell * 0.3989422804014327


def place_blocks(meta, place, blocks, target):
    width = blocks[0].shape[1]
    for index, block in enumerate(blocks):
        at = pl.multiple_of(meta[place + index] * width, width)
        target[:, pl.ds(at, width)] = block[...]


def key_bias(meta, seq, slots):
    place = lax.broadcasted_iota(jnp.int32, (1, slots), 1)
    return place < meta[5 + seq]


def split_refs(refs, counts):
    out = []
    at = 0
    for count in counts:
        out.append(refs[at : at + count])
        at += count
    return out


def attend_kernel(first, slots, counts, offsets, meta, *refs):
    (base, sums, params, in_refs, proj_refs, outs, scratch) = split_refs(refs, counts)
    gains, shifts, query_shift, value_shift = params
    x_ref, normed_ref, query_ref, key_ref, value_ref, lse_ref, mixed_ref, wide_ref, low_ref = outs
    in_weight, proj_weight, in_sems, proj_sems = scratch
    in_moves = in_copies(meta, in_refs, offsets[0], in_weight, in_sems)
    proj_moves = proj_copies(meta, proj_refs, offsets[1], proj_weight, proj_sems)
    start_all(in_moves)
    start_all(proj_moves)
    rows = x_ref.shape[0]
    if first:
        place_blocks(meta, 5 + rows // slots, base, x_ref)
        current = x_ref[...]
    else:
        own, arrived, bias = sums
        current = base[0][...] + own[...] + arrived[...].astype(wide_type) + bias[...]
        current = current * mask_rows(meta, rows, slots)
        x_ref[...] = current
    standard, _ = standardize(current)
    normed = (standard * gains[...] + shifts[...]).astype(low_type)
    normed_ref[...] = normed
    wait_all(in_moves)
    query_ref[...] = (dot(normed, in_weight[0]) + query_shift[...]).astype(low_type)
    key_ref[...] = dot(normed, in_weight[1]).astype(low_type)
    value_ref[...] = (dot(normed, in_weight[2]) + value_shift[...]).astype(low_type)
    heads = query_ref.shape[1] // HEAD_DIM
    for seq in range(rows // slots):
        span = slice(seq * slots, (seq + 1) * slots)
        valid = key_bias(meta, seq, slots)
        for head in range(heads):
            lanes = slice(head * HEAD_DIM, (head + 1) * HEAD_DIM)
            scores = dot_right(query_ref[span, lanes], key_ref[span, lanes]) * score_scale
            scores = jnp.where(valid, scores, fill_value)
            maximum = jnp.max(scores, axis=1, keepdims=True)
            exponent = jnp.exp(scores - maximum)
            mass = jnp.sum(exponent, axis=1, keepdims=True)
            attention = (exponent * (1.0 / mass)).astype(low_type)
            mixed_ref[span, lanes] = dot(attention, value_ref[span, lanes]).astype(low_type)
            lse_ref[span, head : head + 1] = maximum + jnp.log(mass)
    wait_all(proj_moves)
    block = proj_weight.shape[1]
    total = dot(mixed_ref[:, :block], proj_weight[0])
    for index in range(1, proj_weight.shape[0]):
        total = total + dot(
            mixed_ref[:, index * block : (index + 1) * block], proj_weight[index]
        )
    wide_ref[...] = total
    low_ref[...] = total.astype(low_type)


def feed_kernel(counts, offsets, meta, *refs):
    (sums, params, up_refs, down_refs, outs, scratch) = split_refs(refs, counts)
    base, own, arrived, bias = sums
    gains, shifts, up_shift = params
    middle_ref, normed_ref, hidden_ref, slope_ref, wide_ref, low_ref = outs
    up_weight, down_weight, up_sems, down_sems = scratch
    up_moves = up_copies(meta, up_refs, offsets[0], up_weight, up_sems)
    down_moves = down_copies(meta, down_refs, offsets[1], down_weight, down_sems)
    start_all(up_moves)
    start_all(down_moves)
    middle = base[...] + own[...] + arrived[...].astype(wide_type) + bias[...]
    middle_ref[...] = middle
    standard, _ = standardize(middle)
    normed = (standard * gains[...] + shifts[...]).astype(low_type)
    normed_ref[...] = normed
    wait_all(up_moves)
    width = up_weight.shape[2]
    for index in range(up_weight.shape[0]):
        lanes = slice(index * width, (index + 1) * width)
        pre = dot(normed_ref[...], up_weight[index]) + up_shift[:, lanes]
        hidden, slope = gelu_and_slope(pre)
        hidden_ref[:, lanes] = hidden.astype(low_type)
        slope_ref[:, lanes] = slope.astype(low_type)
    wait_all(down_moves)
    rows = down_weight.shape[0] * down_weight.shape[1]
    total = dot(hidden_ref[...], down_weight[...].reshape(rows, down_weight.shape[2]))
    wide_ref[...] = total
    low_ref[...] = total.astype(low_type)


def norm_back(grad_rows, inputs, gains):
    standard, rscale = standardize(inputs)
    width = inputs.shape[1]
    scaled = grad_rows * gains
    first = jnp.sum(scaled, axis=1, keepdims=True) / width
    second = jnp.sum(scaled * standard, axis=1, keepdims=True) / width
    grad_input = rscale * (scaled - first - standard * second)
    return (
        grad_input,
        jnp.sum(grad_rows * standard, axis=0, keepdims=True),
        jnp.sum(grad_rows, axis=0, keepdims=True),
    )


def last_kernel(slots, meta, factor, base, own, arrived, bias, *refs):
    seeds, (current_ref, grad_ref) = refs[:-2], refs[-2:]
    rows = base.shape[0]
    mask = mask_rows(meta, rows, slots)
    place_blocks(meta, 5 + rows // slots, seeds, grad_ref)
    current = base[...] + own[...] + arrived[...].astype(wide_type) + bias[...]
    current = current * mask
    current_ref[...] = current
    grad_ref[...] = grad_ref[...] + factor[0] * current


def pull_kernel(inputs, gains, base, own, arrived, grad_ref, gain_ref, shift_ref):
    summed = own[...] + arrived[...].astype(wide_type)
    grad, gain, shift = norm_back(summed, inputs[...], gains[...])
    grad_ref[...] = base[...] + grad
    gain_ref[...] = gain
    shift_ref[...] = shift


def feed_back_kernel(slots, counts, offsets, meta, *refs):
    (sums, up_refs, down_refs, outs, scratch) = split_refs(refs, counts)
    grad, slope_ref = sums
    masked_ref, masked_low_ref, pre_ref, down_bias_ref, up_bias_ref, wide_ref, low_ref = outs
    up_weight, down_weight, up_sems, down_sems = scratch
    up_moves = up_copies(meta, up_refs, offsets[0], up_weight, up_sems)
    down_moves = down_copies(meta, down_refs, offsets[1], down_weight, down_sems)
    start_all(down_moves)
    start_all(up_moves)
    masked = grad[...] * mask_rows(meta, grad.shape[0], slots)
    masked_ref[...] = masked
    masked_low = masked.astype(low_type)
    masked_low_ref[...] = masked_low
    down_bias_ref[...] = jnp.sum(masked_low.astype(wide_type), axis=0, keepdims=True)
    wait_all(down_moves)
    width = up_weight.shape[2]
    for index in range(up_weight.shape[0]):
        lanes = slice(index * width, (index + 1) * width)
        hidden = dot_right(masked_low_ref[...], down_weight[index])
        pre = (hidden * slope_ref[:, lanes].astype(wide_type)).astype(low_type)
        pre_ref[:, lanes] = pre
        up_bias_ref[:, lanes] = jnp.sum(pre.astype(wide_type), axis=0, keepdims=True)
    wait_all(up_moves)
    total = dot_right(pre_ref[:, :width], up_weight[0])
    for index in range(1, up_weight.shape[0]):
        lanes = slice(index * width, (index + 1) * width)
        total = total + dot_right(pre_ref[:, lanes], up_weight[index])
    wide_ref[...] = total
    low_ref[...] = total.astype(low_type)


def attend_back_kernel(slots, counts, offsets, meta, *refs):
    (sums, params, saved, in_refs, proj_refs, outs, scratch) = split_refs(refs, counts)
    own, arrived, middle, masked = sums
    (gains,) = params
    query_ref, key_ref, value_ref, lse_ref = saved
    (
        grad_ref,
        low_grad_ref,
        gain_ref,
        shift_ref,
        proj_bias_ref,
        triple_ref,
        in_bias_ref,
        wide_ref,
        low_ref,
    ) = outs
    in_weight, proj_weight, mixed_grad, in_sems, proj_sems = scratch
    in_moves = in_copies(meta, in_refs, offsets[0], in_weight, in_sems)
    proj_moves = proj_copies(meta, proj_refs, offsets[1], proj_weight, proj_sems)
    start_all(proj_moves)
    start_all(in_moves)
    summed = own[...] + arrived[...].astype(wide_type)
    grad, gain, shift = norm_back(summed, middle[...], gains[...])
    grad = masked[...] + grad
    grad_ref[...] = grad
    gain_ref[...] = gain
    shift_ref[...] = shift
    grad_low = grad.astype(low_type)
    low_grad_ref[...] = grad_low
    proj_bias_ref[...] = jnp.sum(grad_low.astype(wide_type), axis=0, keepdims=True)
    wait_all(proj_moves)
    block = proj_weight.shape[1]
    for index in range(proj_weight.shape[0]):
        mixed_grad[:, index * block : (index + 1) * block] = dot_right(
            low_grad_ref[...], proj_weight[index]
        ).astype(low_type)
    heads = query_ref.shape[1] // HEAD_DIM
    rows = query_ref.shape[0]
    for seq in range(rows // slots):
        span = slice(seq * slots, (seq + 1) * slots)
        valid = key_bias(meta, seq, slots)
        for head in range(heads):
            lanes = slice(head * HEAD_DIM, (head + 1) * HEAD_DIM)
            queries = query_ref[span, lanes]
            keys = key_ref[span, lanes]
            outer = mixed_grad[span, lanes]
            scores = dot_right(queries, keys) * score_scale
            scores = jnp.where(valid, scores, fill_value)
            chance = jnp.exp(scores - lse_ref[span, head : head + 1])
            grad_chance = dot_right(outer, value_ref[span, lanes])
            inner = jnp.sum(grad_chance * chance, axis=1, keepdims=True)
            grad_scores = (chance * (grad_chance - inner)).astype(low_type)
            triple_ref[2, span, lanes] = dot_left(chance.astype(low_type), outer).astype(low_type)
            triple_ref[0, span, lanes] = (dot(grad_scores, keys) * score_scale).astype(low_type)
            triple_ref[1, span, lanes] = (dot_left(grad_scores, queries) * score_scale).astype(
                low_type
            )
    in_bias_ref[0:1, :] = jnp.sum(triple_ref[0].astype(wide_type), axis=0, keepdims=True)
    in_bias_ref[1:2, :] = jnp.sum(triple_ref[2].astype(wide_type), axis=0, keepdims=True)
    wait_all(in_moves)
    total = dot_right(triple_ref[0], in_weight[0])
    total = total + dot_right(triple_ref[1], in_weight[1])
    total = total + dot_right(triple_ref[2], in_weight[2])
    wide_ref[...] = total
    low_ref[...] = total.astype(low_type)


def feed_weight_kernel(meta, normed, pre, hidden, masked_low, *outs):
    def write(place, block, row_block):
        columns = pl.ds(pl.multiple_of(row_block * 256, 256), 256)
        for tile in range(4):
            lanes = pl.ds(pl.multiple_of(block * 1024 + tile * 256, 256), 256)
            place[tile] = dot_left(normed[:, columns], pre[:, lanes]).astype(low_type)
            place[4 + tile] = dot_left(hidden[:, lanes], masked_low[:, columns]).astype(low_type)

    write_pieces(meta, outs, write)


def attend_weight_kernel(meta, normed, triple, mixed, grad_low, *outs):
    def write(place, block, row_block):
        columns = pl.ds(pl.multiple_of(row_block * 256, 256), 256)
        lanes = pl.ds(pl.multiple_of(block * 256, 256), 256)
        for kind in range(3):
            place[kind] = dot_left(normed[:, columns], triple[kind, :, lanes]).astype(low_type)
        place[3] = dot_left(mixed[:, lanes], grad_low[:, columns]).astype(low_type)

    write_pieces(meta, outs, write)


def write_pieces(meta, outs, write):
    core = meta[4]
    for place in range(3):
        for block in range(2):
            write(outs[place].at[block], block, meta[place])
    write(outs[3], core, meta[3])
    write(outs[4], 1 - core, meta[3])


def near_add_kernel(meta, near, arrived, moved, out):
    for block in range(2):
        extra = jnp.where(meta[4] == block, moved[...].astype(wide_type), 0.0)
        total = near[block].astype(wide_type) + arrived[block].astype(wide_type) + extra
        out[block] = total.astype(low_type)


def finish_feed_kernel(meta, *refs):
    halves, (up, down) = refs[:-2], refs[-2:]
    first = meta[4] == 0
    for layer in range(len(halves) // 2):
        part, other = halves[2 * layer], halves[2 * layer + 1]
        for tile in range(4):
            mine, its = part[tile].astype(wide_type), other[tile].astype(wide_type)
            up[layer, :, tile * 256 : (tile + 1) * 256] = jnp.where(first, mine, its)
            down[layer, tile * 256 : (tile + 1) * 256, :] = jnp.where(first, its, mine)


def finish_attend_kernel(meta, *refs):
    halves, (thirds, square) = refs[:-2], refs[-2:]
    first = meta[4] == 0
    for layer in range(len(halves) // 2):
        part, other = halves[2 * layer], halves[2 * layer + 1]
        mine, its = part[...].astype(wide_type), other[...].astype(wide_type)
        thirds[layer, 0] = jnp.where(first, mine[0], its[0])
        thirds[layer, 1] = jnp.where(first, mine[1], its[1])
        thirds[layer, 2] = jnp.where(first, its[0], mine[0])
        square[layer] = jnp.where(first, its[1], mine[1])


def flip_col(value):
    count = lax.axis_size("col")
    return lax.ppermute(value, "col", [(i, count - 1 - i) for i in range(count)])


def swap_core(value):
    count = lax.axis_size("dp")
    return lax.ppermute(value, "dp", [(i, count - 1 - i) for i in range(count)])


def group_shift(value, step):
    count = lax.axis_size("col")
    half = count // 2
    pairs = [(i, i // half * half + (i % half + step) % half) for i in range(count)]
    return lax.ppermute(value, "col", pairs)


def cross_row(value, first_step, second_step):
    rows = lax.axis_size("row")
    cols = lax.axis_size("col")
    pairs = []
    for core, step in ((0, first_step), (1, second_step)):
        for row in range(rows):
            for col in range(cols):
                source = (core * rows + row) * cols + col
                pairs.append((source, (core * rows + (row ^ step)) * cols + col))
    return lax.ppermute(value, ("dp", "row", "col"), pairs)


def group_total(wide, low):
    arrived = group_shift(low, 1)
    for step in range(2, lax.axis_size("col") // 2):
        wide = wide + group_shift(low, step).astype(wide_type)
    return wide, arrived


def butterfly_sum(value, axes):
    for axis in axes:
        count = lax.axis_size(axis)
        step = 1
        while step < count:
            value = value + lax.ppermute(value, axis, [(i, i ^ step) for i in range(count)])
            step *= 2
    return value


def after(value, *events):
    return lax.optimization_barrier((value,) + events)[0]


def order_blocks(pair):
    count = lax.axis_size("col")
    half = count // 2
    col_index = lax.axis_index("col")
    base = col_index // half * half
    wanted = lax.broadcasted_iota(jnp.int32, (count,) + pair.shape[1:], 0)
    whole = jnp.zeros((count,) + pair.shape[1:], pair.dtype)
    for step in range(half):
        piece = pair if step == 0 else group_shift(pair, step)
        source = base + (col_index - base + half - step) % half
        whole = jnp.where(wanted == source, piece[0][None], whole)
        whole = jnp.where(wanted == count - 1 - source, piece[1][None], whole)
    return whole


def add(left, right):
    return (left.astype(wide_type) + right.astype(wide_type)).astype(low_type)


def gather_near(own):
    return cross_row(own, 1, 2)


def gather_far(near, first_core):
    return cross_row(jnp.where(first_core, near[0], near[1]), 2, 1)


def gather_pieces(own, near, far):
    return (own, near, swap_core(near), far, swap_core(far))


def flip_tiles(shard, first_core):
    half = shard.shape[0] // 2
    return flip_col(jnp.where(first_core, shard[:half], shard[half:]))


def join_tiles(shard, got, other, first_core):
    halves = jnp.where(first_core, jnp.stack([got, other]), jnp.stack([other, got]))
    return jnp.stack([shard, halves.reshape(shard.shape)])


def scatter_first(pieces):
    own, near, near_other, far, far_other = pieces
    return own, near, swap_core(near_other), add(far, swap_core(far_other))


def scatter_third(own, arrived, first_core):
    own = add(own, arrived)
    half = own.shape[1] // 2
    lower, upper = own[:, :half], own[:, half:]
    arrived = swap_core(jnp.where(first_core, upper, lower))
    return add(jnp.where(first_core, lower, upper), arrived)


def body(
    states,
    teacher,
    cotangent,
    lengths,
    norm_gain,
    norm_bias,
    in_weight,
    in_bias,
    proj_weight,
    proj_bias,
    up_weight,
    up_bias,
    down_weight,
    down_bias,
):
    col_count = lax.axis_size("col")
    row_count = lax.axis_size("row")
    core_count = lax.axis_size("dp")
    half_group = col_count // 2
    col_index = lax.axis_index("col")
    row_index = lax.axis_index("row")
    core_index = lax.axis_index("dp")
    group_index = col_index // half_group
    first_core = core_index == 0
    token_rows, width = states.shape
    model_width = width * col_count
    seqs = lengths.shape[0] // 2
    rows = token_rows // 2
    slots = rows // seqs
    hidden_width = up_bias.shape[1]
    tiled = row_count == 4 and width == 256 and hidden_width == 1024 and model_width == 1024
    row_width = model_width // row_count
    heads_width = 2 * width
    feed_width = 2 * hidden_width
    in_thirds = jnp.transpose(in_weight, (0, 2, 1, 3))

    def own_half(value):
        return lax.dynamic_slice_in_dim(value, group_index * rows, rows, 0)

    def other_half(value):
        return lax.dynamic_slice_in_dim(value, (1 - group_index) * rows, rows, 0)

    block_places = []
    for step in range(half_group):
        base = group_index * half_group
        source = base + (col_index - base + half_group - step) % half_group
        block_places = block_places + [source, col_count - 1 - source]

    def join_rows(value, received):
        own = lax.dynamic_slice_in_dim(value, col_index * width, width, 1)
        lower = jnp.where(group_index == 0, own, received)
        upper = jnp.where(group_index == 0, received, own)
        return jnp.concatenate([lower, upper])

    def share_rows(value, kind):
        other = lax.dynamic_slice_in_dim(value, (col_count - 1 - col_index) * width, width, 1)
        return join_rows(value, flip_col(other.astype(kind)).astype(wide_type))

    own_lengths = lax.dynamic_slice_in_dim(lengths, group_index * seqs, seqs, 0)
    meta = jnp.concatenate(
        [
            jnp.stack(
                [
                    row_index,
                    row_index ^ (1 + core_index),
                    row_index ^ (2 - core_index),
                    row_index ^ 3,
                    core_index,
                ]
            ),
            own_lengths,
            jnp.stack(block_places),
        ]
    ).astype(jnp.int32)

    in_full, proj_full, up_full, down_full = ([None] * LAYERS for kind in range(4))
    feature_pack = jnp.concatenate(
        [norm_gain.reshape(-1, width), norm_bias.reshape(-1, width), proj_bias, down_bias]
    )
    hidden_pack = jnp.concatenate([in_bias.reshape(-1, width), up_bias.reshape(-1, width)])
    feature_rows = feature_pack.shape[0]
    small = jnp.concatenate([feature_pack, hidden_pack])
    states_own, states_other = own_half(states), other_half(states)
    gate = []

    def gated(value):
        return after(value, *gate) if gate else value

    def all_shifts(value):
        return [group_shift(value, step) for step in range(1, half_group)]

    def all_blocks(own, own_shifts, flipped, flipped_shifts):
        blocks = [own, flipped]
        for pair in zip(own_shifts, flipped_shifts):
            blocks = blocks + list(pair)
        return blocks

    total_steps = [
        (axis, 2**bit)
        for axis in ("dp", "row")
        for bit in range(lax.axis_size(axis).bit_length() - 1)
    ]
    token_total = jnp.sum(lengths)

    def count_step(value, axis, step):
        size = lax.axis_size(axis)
        return value + lax.ppermute(value, axis, [(i, i ^ step) for i in range(size)])

    if tiled:
        count = 6
        shards, flips, owns, nears, near_others, fars, far_others = (
            [None] * count for kind in range(7)
        )

        def up_tiles(weight):
            return jnp.transpose(weight.reshape(256, 4, 256), (1, 0, 2))

        def flip(place):
            layer = place // 3
            if place % 3 == 0:
                square = gated(proj_weight[layer])[None]
                shards[place] = jnp.concatenate([gated(in_thirds[layer]), square])
            elif place % 3 == 1:
                shards[place] = up_tiles(gated(up_weight[layer]))
            else:
                shards[place] = gated(down_weight[layer]).reshape(4, 256, 256)
            flips[place] = flip_tiles(shards[place], first_core)
            return flips[place]

        def near(place):
            got = gated(flips[place])
            owns[place] = join_tiles(shards[place], got, swap_core(got), first_core)
            nears[place] = cross_row(owns[place], 1, 2)
            return nears[place]

        def near_swap(place):
            near_others[place] = swap_core(gated(nears[place]))
            return near_others[place]

        def far(place):
            value = gated(nears[place])
            fars[place] = cross_row(jnp.where(first_core, value[0], value[1]), 2, 1)
            return fars[place]

        def far_swap(place):
            far_others[place] = swap_core(gated(fars[place]))
            return far_others[place]

        def pieces(place):
            return (
                owns[place],
                nears[place],
                near_others[place],
                fars[place],
                far_others[place],
            )

        gate = [flip(0)]
        states_flipped = flip_col(gated(states_other))
        shifts_own = all_shifts(gated(states_own))
        small_flipped = flip_col(gated(small))
        token_total = count_step(gated(token_total), *total_steps[0])
        gate = [near(0), states_flipped, small_flipped, token_total, *shifts_own]
        small_pair = jnp.stack([small, gated(small_flipped)])
        feature_all = order_blocks(small_pair[:, :feature_rows])
        shifts_flipped = all_shifts(gated(states_flipped))
        token_total = count_step(gated(token_total), *total_steps[1])
        gate = [far(0), flip(1), near_swap(0), token_total, feature_all, *shifts_flipped]
        states_blocks = all_blocks(states_own, shifts_own, states_flipped, shifts_flipped)
        token_total = count_step(gated(token_total), *total_steps[2])
        first_slot = [near(1), flip(2), token_total]
        far_swap(0)
        in_full[0], proj_full[0] = (pieces(0), 0), (pieces(0), 3)
    else:

        def both_blocks(shard):
            own = lax.all_gather(shard, "row", axis=0, tiled=False)
            return jnp.stack([own, flip_col(own)])

        for layer in range(LAYERS):
            whole = jnp.transpose(both_blocks(in_thirds[layer]), (2, 1, 3, 0, 4))
            in_full[layer] = ((whole.reshape(3, model_width, heads_width),), 0)
            whole = jnp.transpose(both_blocks(proj_weight[layer]), (0, 2, 1, 3))
            proj_full[layer] = ((whole.reshape(2, width, model_width),), 0)
            whole = both_blocks(up_weight[layer]).reshape(2, model_width, -1, 256)
            whole = jnp.transpose(whole, (0, 2, 1, 3))
            up_full[layer] = ((whole.reshape(-1, model_width, 256),), 0)
            whole = jnp.transpose(both_blocks(down_weight[layer]), (0, 2, 1, 3))
            down_full[layer] = ((whole.reshape(-1, 256, model_width),), 0)
        states_flipped = flip_col(states_other)
        small_flipped = flip_col(small)
        states_blocks = all_blocks(
            states_own, all_shifts(states_own), states_flipped, all_shifts(states_flipped)
        )
        for step in total_steps:
            token_total = count_step(token_total, *step)
        small_pair = jnp.stack([small, small_flipped])
        feature_all = order_blocks(small_pair[:, :feature_rows])

    feature_all = jnp.transpose(feature_all, (1, 0, 2)).reshape(feature_rows, model_width)
    gains = feature_all[: 2 * LAYERS].reshape(LAYERS, 2, 1, model_width)
    shifts = feature_all[2 * LAYERS : 4 * LAYERS].reshape(LAYERS, 2, 1, model_width)
    proj_shift = feature_all[4 * LAYERS : 5 * LAYERS].reshape(LAYERS, 1, model_width)
    down_shift = feature_all[5 * LAYERS :].reshape(LAYERS, 1, model_width)
    hidden_pair = small_pair[:, feature_rows:]
    in_shift = hidden_pair[:, : 2 * LAYERS].reshape(2, LAYERS, 2, width)
    in_shift = jnp.transpose(in_shift, (1, 2, 0, 3)).reshape(LAYERS, 2, 1, heads_width)
    up_shift = hidden_pair[:, 2 * LAYERS :].reshape(2, LAYERS, hidden_width)
    up_shift = jnp.transpose(up_shift, (1, 0, 2)).reshape(LAYERS, 1, feed_width)


    def shape(*dims, kind=wide_type):
        return jax.ShapeDtypeStruct(dims, kind)

    def call(kernel, cost, operands, specs, outs, scratch=()):
        return pl.pallas_call(
            kernel,
            out_shape=outs,
            in_specs=specs,
            out_specs=[VMEM] * len(outs),
            scratch_shapes=list(scratch),
            compiler_params=pltpu.CompilerParams(vmem_limit_bytes=vmem_bytes),
            cost_estimate=pl.CostEstimate(
                flops=int(cost * 9.2e9), bytes_accessed=1024 * 1024, transcendentals=0
            ),
        )(*operands)

    wide_rows = shape(rows, model_width)
    low_rows = shape(rows, model_width, kind=low_type)
    low_heads = shape(rows, heads_width, kind=low_type)
    heads = heads_width // HEAD_DIM
    feed_tiles = feed_width // 256
    attend_scratch = [
        pltpu.VMEM((3, model_width, heads_width), low_type),
        pltpu.VMEM((2, width, model_width), low_type),
    ]
    feed_scratch = [
        pltpu.VMEM((feed_tiles, model_width, 256), low_type),
        pltpu.VMEM((feed_tiles, 256, model_width), low_type),
    ]
    sems = [pltpu.SemaphoreType.DMA((8,)), pltpu.SemaphoreType.DMA((8,))]

    def attend(layer, base, sums):
        first = len(sums) == 0
        params = [gains[layer, 0], shifts[layer, 0], in_shift[layer, 0], in_shift[layer, 1]]
        in_refs, in_offset = in_full[layer]
        proj_refs, proj_offset = proj_full[layer]
        counts = (len(base), len(sums), 4, len(in_refs), len(proj_refs), 9, 4)
        operands = [meta, *base, *sums, *params, *in_refs, *proj_refs]
        specs = [SMEM] + [VMEM] * (4 + len(base) + len(sums)) + [ANY] * (len(in_refs) + len(proj_refs))
        kernel = functools.partial(attend_kernel, first, slots, counts, (in_offset, proj_offset))
        outs = [
            wide_rows,
            low_rows,
            low_heads,
            low_heads,
            low_heads,
            shape(rows, heads),
            low_heads,
            wide_rows,
            low_rows,
        ]
        return call(kernel, 10.5, operands, specs, outs, attend_scratch + sems)

    def feed(layer, base, sums):
        params = [gains[layer, 1], shifts[layer, 1], up_shift[layer]]
        up_refs, up_offset = up_full[layer]
        down_refs, down_offset = down_full[layer]
        counts = (4, 3, len(up_refs), len(down_refs), 6, 4)
        operands = [meta, base, *sums, *params, *up_refs, *down_refs]
        specs = [SMEM] + [VMEM] * 7 + [ANY] * (len(up_refs) + len(down_refs))
        kernel = functools.partial(feed_kernel, counts, (up_offset, down_offset))
        low_feed = shape(rows, feed_width, kind=low_type)
        outs = [wide_rows, low_rows, low_feed, low_feed, wide_rows, low_rows]
        return call(kernel, 12.0, operands, specs, outs, feed_scratch + sems)

    def feed_back(layer, grad, slope):
        up_refs, up_offset = up_full[layer]
        down_refs, down_offset = down_full[layer]
        counts = (2, len(up_refs), len(down_refs), 7, 4)
        operands = [meta, grad, slope, *up_refs, *down_refs]
        specs = [SMEM] + [VMEM] * 2 + [ANY] * (len(up_refs) + len(down_refs))
        kernel = functools.partial(feed_back_kernel, slots, counts, (up_offset, down_offset))
        outs = [
            wide_rows,
            low_rows,
            shape(rows, feed_width, kind=low_type),
            shape(1, model_width),
            shape(1, feed_width),
            wide_rows,
            low_rows,
        ]
        return call(kernel, 10.0, operands, specs, outs, feed_scratch + sems)

    def attend_back(layer, sums, middle, masked, saved):
        in_refs, in_offset = in_full[layer]
        proj_refs, proj_offset = proj_full[layer]
        counts = (4, 1, 4, len(in_refs), len(proj_refs), 9, 5)
        operands = [meta, *sums, middle, masked, gains[layer, 1], *saved, *in_refs, *proj_refs]
        specs = [SMEM] + [VMEM] * 9 + [ANY] * (len(in_refs) + len(proj_refs))
        kernel = functools.partial(attend_back_kernel, slots, counts, (in_offset, proj_offset))
        outs = [
            wide_rows,
            low_rows,
            shape(1, model_width),
            shape(1, model_width),
            shape(1, model_width),
            shape(3, rows, heads_width, kind=low_type),
            shape(2, heads_width),
            wide_rows,
            low_rows,
        ]
        scratch = attend_scratch + [pltpu.VMEM((rows, heads_width), low_type)] + sems
        return call(kernel, 12.0, operands, specs, outs, scratch)

    def weight_tiles(kernel, tiles, cost, *operands):
        outs = [shape(2, tiles, 256, 256, kind=low_type)] * 3
        outs = outs + [shape(tiles, 256, 256, kind=low_type)] * 2
        specs = [SMEM] + [VMEM] * len(operands)
        return call(kernel, cost, (meta,) + operands, specs, outs)

    positions = jnp.arange(slots, dtype=jnp.int32)
    all_mask = (positions[None, :] < lengths[:, None]).reshape(token_rows, 1).astype(wide_type)
    teacher_wide = teacher.astype(wide_type)

    def near_add(near, arrived, moved):
        tiles = moved.shape[0]
        both = pl.BlockSpec((2, 4, 256, 256), lambda index: (0, index, 0, 0))
        single = pl.BlockSpec((4, 256, 256), lambda index: (index, 0, 0))
        return pl.pallas_call(
            near_add_kernel,
            grid=(tiles // 4,),
            out_shape=shape(2, tiles, 256, 256, kind=low_type),
            in_specs=[SMEM, both, both, single],
            out_specs=both,
            cost_estimate=pl.CostEstimate(
                flops=int(tiles * 2.4e9), bytes_accessed=1024 * 1024, transcendentals=0
            ),
        )(meta, near, arrived, moved)

    def finish(kernel, cost, outs, parts):
        halves = []
        for part in parts:
            halves = halves + [part, swap_core(part)]
        return call(kernel, cost, (meta, *halves), [SMEM] + [VMEM] * len(halves), outs)

    saved = []
    base, sums = states_blocks, ()
    for layer in range(LAYERS):
        if layer > 0:
            sums = (*sums, down_shift[layer - 1])
        current, normed_one, queries, keys, values, lse, mixed, wide, low = attend(
            layer, base, sums
        )
        event = wide
        if layer == 0:
            if tiled:
                gate = [wide, *first_slot]
                second_slot = [far(1), near(2), flip(3), near_swap(1)]
            wide, arrived = group_total(wide, low)
            token_total = token_total.astype(wide_type)
            factor = 2.0 * token_rows * core_count * row_count / token_total
            seed_share = cotangent - factor * all_mask * teacher_wide
            seed_own, seed_other = own_half(seed_share), other_half(seed_share)
            if tiled:
                gate = [*second_slot, arrived]
                second_slot = [far(2), near(3), flip(4), far_swap(1), near_swap(2)]
                gate = [fars[2]]
                far_swap(2)
                up_full[0], down_full[0] = (pieces(1), 0), (pieces(2), 0)
        else:
            if tiled:
                low = after(low, seed_flipped)
                gate = [event, *second_slot, seed_flipped]
                second_slot = [far(5), far_swap(4), near_swap(5)]
                gate = [fars[5]]
                far_swap(5)
                up_full[1], down_full[1] = (pieces(4), 0), (pieces(5), 0)
            wide, arrived = group_total(wide, low)
            gate = [arrived]
            shifts_own, shifts_flipped = all_shifts(gated(seed_own)), all_shifts(gated(seed_flipped))
            seed_blocks = all_blocks(seed_own, shifts_own, seed_flipped, shifts_flipped)
        middle, normed_two, hidden, slope, wide, low = feed(
            layer, current, (wide, arrived, proj_shift[layer])
        )
        if layer == 1:
            low = after(low, *seed_blocks)
        event = wide
        wide, arrived = group_total(wide, low)
        if layer == 0:
            gate = [event, *second_slot] if tiled else []
            if tiled:
                second_slot = [far(3), near(4), flip(5), near_swap(3)]
                gate = [fars[3]]
                far_swap(3)
                in_full[1], proj_full[1] = (pieces(3), 0), (pieces(3), 3)
                gate = [arrived, *second_slot]
                second_slot = [near(5), far(4), near_swap(4)]
            seed_flipped = flip_col(gated(seed_other))
        base, sums = [middle], (wide, arrived)
        saved.append(
            (current, normed_one, queries, keys, values, lse, mixed, middle, normed_two, hidden, slope)
        )
    final, grad = call(
        functools.partial(last_kernel, slots),
        4.3,
        (meta, factor.reshape(1), *base, *sums, down_shift[LAYERS - 1], *seed_blocks),
        [SMEM, SMEM] + [VMEM] * (4 + len(seed_blocks)),
        [wide_rows, wide_rows],
    )
    output_other = lax.dynamic_slice_in_dim(
        final, (col_count - 1 - col_index) * width, width, 1
    )
    output_halves = [flip_col(output_other[: rows // 2])]

    feature_grads = {}
    hidden_grads = {}
    in_grads, proj_grads, up_grads, down_grads = ([None] * LAYERS for kind in range(4))

    way = []
    for layer in reversed(range(LAYERS)):
        current, normed_one, queries, keys, values, lse, mixed, middle, normed_two, hidden, slope = (
            saved[layer]
        )
        masked, masked_low, pre, down_bias_part, up_bias_part, wide, low = feed_back(
            layer, grad, slope
        )
        if tiled:
            if layer == LAYERS - 1:
                gate = [low, output_halves[0]]
            else:
                gate = [low, far_moved]
        wide, arrived = group_total(wide, gated(low))
        if tiled:
            tiles = weight_tiles(
                feed_weight_kernel, 8, 9.0, normed_two, gated(pre), hidden, masked_low
            )
            way.append(scatter_first(tiles))
            gate = [arrived, *tiles]
            if layer < LAYERS - 1:
                gate = gate + list(way[-1])
                own, near_part, near_arrived, far_part = way[-2]
                near_sent = near_add(near_part, near_arrived, far_moved)
                part = scatter_third(way[-3][0], near_moved, first_core)
                gate = gate + [near_sent, part]
                near_moved = cross_row(near_sent, 1, 2)
                flip_moved = flip_col(after(part[1], *gate))
            arrived = gated(arrived)
            far_moved = cross_row(gated(way[-1][3]), 2, 1)
        (
            grad,
            grad_low,
            gain_two,
            shift_two,
            proj_bias_part,
            triple,
            in_bias_part,
            wide,
            low,
        ) = attend_back(layer, (wide, arrived), middle, masked, (queries, keys, values, lse))
        if layer == LAYERS - 1:
            output_halves.append(flip_col(gated(output_other[rows // 2 :])))
        if tiled:
            gate = [low, *output_halves[1:]] if layer == LAYERS - 1 else [low, far_moved]
        wide, arrived = group_total(wide, gated(low))
        if tiled:
            own, near_part, near_arrived, far_part = way[-1]
            near_sent = near_add(near_part, near_arrived, far_moved)
            if layer < LAYERS - 1:
                pass
            else:
                received = gated(jnp.concatenate(output_halves))
            tiles = weight_tiles(
                attend_weight_kernel, 4, 5.5, normed_one, gated(triple), mixed, grad_low
            )
            way.append(scatter_first(tiles))
            gate = [arrived, *tiles, *way[-1], near_sent]
            if layer == LAYERS - 1:
                output_share = join_rows(final, received)
                residue = (output_share - teacher_wide) * all_mask
                squared = jnp.sum(residue * residue)
                gate = gate + [squared]
            if layer < LAYERS - 1:
                feed_parts = [add(part[0], flip_moved)]
                part = scatter_third(way[-3][0], near_moved, first_core)
                gate = gate + [part, *feed_parts]
                flip_moved = flip_col(part[1])
            near_moved = cross_row(near_sent, 1, 2)
            arrived = gated(arrived)
            far_moved = cross_row(gated(way[-1][3]), 2, 1)
        else:
            if layer == LAYERS - 1:
                output_share = join_rows(final, jnp.concatenate(output_halves))
                residue = (output_share - teacher_wide) * all_mask
                squared = jnp.sum(residue * residue)

            def product(spec, left, right):
                return jnp.einsum(spec, left, right, preferred_element_type=wide_type)

            def own_block(blocks):
                part = lax.psum_scatter(
                    blocks.astype(low_type), "row", scatter_dimension=1, tiled=False
                )
                mine = add(part[0], flip_col(part[1]))
                return mine.astype(wide_type) + swap_core(mine).astype(wide_type)

            def by_row(value):
                return value.reshape(rows, row_count, row_width)

            def by_block(value):
                return value.reshape(value.shape[:-1] + (2, -1))

            in_grads[layer] = own_block(
                product("trd,ptbe->brpde", by_row(normed_one), by_block(triple))
            )
            proj_grads[layer] = own_block(
                product("tbe,trd->bred", by_block(mixed), by_row(grad_low))
            )
            up_grads[layer] = own_block(product("trd,tbe->brde", by_row(normed_two), by_block(pre)))
            down_grads[layer] = own_block(
                product("tbe,trd->bred", by_block(hidden), by_row(masked_low))
            )
        grad, gain_one, shift_one = call(
            pull_kernel,
            4.3,
            (current, gains[layer, 0], grad, wide, arrived),
            [VMEM] * 5,
            [wide_rows, shape(1, model_width), shape(1, model_width)],
        )
        feature_grads[layer] = (
            gain_one,
            gain_two,
            shift_one,
            shift_two,
            proj_bias_part,
            down_bias_part,
        )
        hidden_grads[layer] = jnp.concatenate(
            [
                jnp.transpose(in_bias_part.reshape(2, 2, width), (1, 0, 2)),
                up_bias_part.reshape(2, -1, width),
            ],
            axis=1,
        )

    if tiled:
        gate = [grad, far_moved]
        own, near_part, near_arrived, far_part = way[-1]
        near_sent = near_add(near_part, near_arrived, far_moved)
        attend_parts = [add(part[0], flip_moved)]
        part = scatter_third(way[-2][0], near_moved, first_core)
        last_moved = cross_row(after(near_sent, part, *attend_parts), 1, 2)
        other = lax.dynamic_slice_in_dim(grad, (col_count - 1 - col_index) * width, width, 1)
        count = part[1].shape[0] * 256
        moved = jnp.concatenate([part[1].reshape(count, 256), other.astype(low_type)])
        moved = flip_col(moved)
        feed_parts.append(add(part[0], moved[:count].reshape(part[0].shape)))
        input_share = join_rows(grad, moved[count:].astype(wide_type))
        part = scatter_third(way[-1][0], last_moved, first_core)
        gate = [part]
        attend_parts.append(add(part[0], flip_col(part[1])))
        up_grad, down_grad = finish(
            finish_feed_kernel,
            3.0,
            [shape(LAYERS, 256, 1024), shape(LAYERS, 1024, 256)],
            feed_parts[::-1],
        )
        in_grad, proj_grad = finish(
            finish_attend_kernel,
            2.0,
            [shape(LAYERS, 3, 256, 256), shape(LAYERS, 256, 256)],
            attend_parts[::-1],
        )
    else:
        input_share = share_rows(grad, low_type)
        up_grad, down_grad = jnp.stack(up_grads), jnp.stack(down_grads)
        in_grad, proj_grad = jnp.stack(in_grads), jnp.stack(proj_grads)
    feature_parts = jnp.concatenate(
        [part for layer in range(LAYERS) for part in feature_grads[layer]]
    )
    feature_parts = gated(feature_parts).reshape(-1, col_count, width)
    own_parts = lax.dynamic_index_in_dim(feature_parts, col_index, 1, False)
    other_parts = lax.dynamic_index_in_dim(feature_parts, col_count - 1 - col_index, 1, False)
    hidden_parts = jnp.concatenate([hidden_grads[layer] for layer in range(LAYERS)], axis=1)
    extra = jnp.zeros((1, width), wide_type).at[0, 0].set(squared)
    packed = jnp.concatenate(
        [jnp.stack([own_parts, other_parts]), hidden_parts, jnp.stack([extra, extra])], axis=1
    )
    packed = butterfly_sum(packed, ("dp", "row"))
    vectors = packed[0] + flip_col(packed[1])
    squared_total = butterfly_sum(packed[0, -1, 0], ("col",))
    loss_value = squared_total / (token_total * model_width)
    per_layer = len(feature_grads[0])
    features = vectors[: LAYERS * per_layer].reshape(LAYERS, per_layer, width)
    hiddens = vectors[LAYERS * per_layer : -1].reshape(LAYERS, -1, width)
    return (
        loss_value,
        output_share,
        input_share,
        features[:, 0:2],
        features[:, 2:4],
        jnp.transpose(in_grad, (0, 2, 1, 3)),
        hiddens[:, 0:2],
        proj_grad,
        features[:, 4],
        up_grad,
        hiddens[:, 2:].reshape(LAYERS, hidden_width),
        down_grad,
        features[:, 5],
    )


def solution(mesh):
    in_specs = (
        P(("dp", "row"), "col"),
        P(("dp", "row"), "col"),
        P(("dp", "row"), "col"),
        P(("dp", "row")),
        P(None, None, "col"),
        P(None, None, "col"),
        P(None, "row", None, "col"),
        P(None, None, "col"),
        P(None, "col", "row"),
        P(None, "col"),
        P(None, "row", "col"),
        P(None, "col"),
        P(None, "col", "row"),
        P(None, "col"),
    )
    out_specs = (
        P(),
        P(("dp", "row"), "col"),
        P(("dp", "row"), "col"),
        P(None, None, "col"),
        P(None, None, "col"),
        P(None, "row", None, "col"),
        P(None, None, "col"),
        P(None, "col", "row"),
        P(None, "col"),
        P(None, "row", "col"),
        P(None, "col"),
        P(None, "col", "row"),
        P(None, "col"),
    )
    return jax.shard_map(body, mesh=mesh, in_specs=in_specs, out_specs=out_specs, check_vma=False)
```
